32 devices in a mesh: dp: 8 (over z, x), mp: 4 (over y, core).
Axes of the slice: x: 2, y: 2, z: 4, core: 2. Of those that a mesh axis runs over, the one named last changes fastest.
Arguments:
- tokens: bfloat16 [8192, 1024], P(('dp', 'mp')), may hold values from -6 to 6
- cotangent: bfloat16 [8192, 1024], P(('dp', 'mp')), may hold values from -6 to 6
- domain: int32 [8], P('dp'), may hold values from 0 to 3
- domain_weight: float32 [4], replicated, may hold values from 0.25 to 4
- query_weight: bfloat16 [1024, 1024], P('dp'), may hold values from -0.1875 to 0.1875
- key_weight: bfloat16 [1024, 1024], P('dp'), may hold values from -0.1875 to 0.1875
- value_weight: bfloat16 [1024, 1024], P('dp'), may hold values from -0.1875 to 0.1875
- beta_weight: bfloat16 [1024, 8], P('dp'), may hold values from -0.1875 to 0.1875
- conv_query: bfloat16 [4, 1024], P(None, 'dp'), may hold values from -3 to 3
- conv_key: bfloat16 [4, 1024], P(None, 'dp'), may hold values from -3 to 3
- conv_value: bfloat16 [4, 1024], P(None, 'dp'), may hold values from -3 to 3
- out_gain: bfloat16 [128], P('dp'), may hold values from 0.25 to 1.75
- out_weight: bfloat16 [1024, 1024], P('dp'), may hold values from -0.1875 to 0.1875
- norm_first: bfloat16 [1024], P('dp'), may hold values from 0.25 to 1.75
- norm_second: bfloat16 [1024], P('dp'), may hold values from 0.25 to 1.75
- gate_weight: bfloat16 [1024, 2816], P('dp', 'mp'), may hold values from -0.1875 to 0.1875
- up_weight: bfloat16 [1024, 2816], P('dp', 'mp'), may hold values from -0.1875 to 0.1875
- down_weight: bfloat16 [2816, 1024], P('mp', 'dp'), may hold values from -0.109375 to 0.109375
Outputs:
- output: bfloat16 [8192, 1024], P(('dp', 'mp'))
- input_grad: float32 [8192, 1024], P(('dp', 'mp'))
- query_weight_grad: float32 [1024, 1024], P('dp')
- key_weight_grad: float32 [1024, 1024], P('dp')
- value_weight_grad: float32 [1024, 1024], P('dp')
- beta_weight_grad: float32 [1024, 8], P('dp')
- conv_query_grad: float32 [4, 1024], P(None, 'dp')
- conv_key_grad: float32 [4, 1024], P(None, 'dp')
- conv_value_grad: float32 [4, 1024], P(None, 'dp')
- out_gain_grad: float32 [128], P('dp')
- out_weight_grad: float32 [1024, 1024], P('dp')
- norm_first_grad: float32 [1024], P('dp')
- norm_second_grad: float32 [1024], P('dp')
- gate_weight_grad: float32 [1024, 2816], P('dp', 'mp')
- up_weight_grad: float32 [1024, 2816], P('dp', 'mp')
- down_weight_grad: float32 [2816, 1024], P('mp', 'dp')
The draws below stay inside these ranges and needn't reach their ends.
All inputs are finite; a program needn't handle non-finite values.
Results may differ from the reference program's by a relative error of at most 0.019.
Values may be sent and summed in bfloat16 or wider, within the bound.
A program may use at most 192 MiB of HBM per device.

```python
import math
import jax
import jax.numpy as jnp
import numpy as np
from jax import lax

D = 1024
H = 8
DK = 128
FF = 2816
KW = 4
C = 64
NDOM = 4
LENGTH = 1024
NSEQ = 8
TOKENS = 8192


def set_ends(drawn, own_key, smallest, largest):
    spot = [jax.random.randint(jax.random.fold_in(own_key, axis), (), 0, length) for axis, length in enumerate(drawn.shape)]
    longest = drawn.shape.index(max(drawn.shape))
    next_to = spot[:longest] + [(spot[longest] + 1) % drawn.shape[longest]] + spot[longest + 1:]
    return drawn.at[tuple(spot)].set(smallest).at[tuple(next_to)].set(largest)


def shard_levels(own_key, dims, cuts, least, high):
    loudness = 1.0
    for position, parts in cuts:
        heights = jax.random.uniform(jax.random.fold_in(jax.random.fold_in(own_key, 6), position), (parts,), jnp.float32, least / len(cuts), high / len(cuts))
        loudness = loudness * jnp.repeat(jnp.exp(heights), dims[position] // parts).reshape((-1,) + (1,) * (len(dims) - 1 - position))
    return loudness


def rank_bounds(number_of, skew):
    loads = [(1 << 20) // math.isqrt(standing ** skew) + 1 for standing in range(1, number_of + 1)]
    width = 1 + sum(loads) // (1 << 30)
    return np.cumsum(np.array([max(1, weight // width) for weight in loads]))


def ranked_ids(own_key, shape, count, skew):
    table = rank_bounds(count, skew)
    lot = jax.random.randint(jax.random.fold_in(own_key, 1), shape, 0, int(table[count - 1]))
    rank = jnp.searchsorted(jnp.asarray(table, jnp.int32), lot, side="right")
    return jax.random.permutation(jax.random.fold_in(own_key, 2), count)[rank].astype(jnp.int32)


def scatter_about(stream_key, dims, spread, most, cuts=(), kind=jnp.bfloat16):
    factor_of = shard_levels(stream_key, dims, cuts, -0.22, 0.18) if cuts else 1.0
    drawn = jax.random.normal(stream_key, dims, jnp.float32) * spread * factor_of
    return jnp.minimum(jnp.maximum(drawn, -most), most).astype(kind)


def setup_inputs(seed: int = 0) -> dict:
    key_of = jax.random.split(jax.random.key(seed), 19)
    return {
        "tokens": scatter_about(key_of[0], (TOKENS, D), 1.0, 6.0, ((0, 32),)),
        "cotangent": scatter_about(key_of[1], (TOKENS, D), 1.0, 6.0, ((0, 32),)),
        "domain": set_ends(ranked_ids(key_of[2], (NSEQ,), NDOM, 2), jax.random.fold_in(key_of[2], 3), 0, NDOM - 1).astype(jnp.int32),
        "domain_weight": jnp.clip(jnp.exp(jax.random.uniform(key_of[3], (NDOM,), jnp.float32, math.log(0.25), math.log(4.0))), 0.25, 4.0),
        "query_weight": scatter_about(key_of[4], (D, D), D ** -0.5, 0.1875, ((0, 8),)),
        "key_weight": scatter_about(key_of[5], (D, D), D ** -0.5, 0.1875, ((0, 8),)),
        "value_weight": scatter_about(key_of[6], (D, D), D ** -0.5, 0.1875, ((0, 8),)),
        "beta_weight": scatter_about(key_of[7], (D, H), D ** -0.5, 0.1875, ((0, 8),)),
        "conv_query": scatter_about(key_of[8], (KW, D), 0.5, 3.0, ((1, 8),)),
        "conv_key": scatter_about(key_of[9], (KW, D), 0.5, 3.0, ((1, 8),)),
        "conv_value": scatter_about(key_of[10], (KW, D), 0.5, 3.0, ((1, 8),)),
        "out_gain": jnp.clip(1.0 + 0.15 * jax.random.normal(key_of[11], (DK,), jnp.float32), 0.25, 1.75).astype(jnp.bfloat16),
        "out_weight": scatter_about(key_of[12], (D, D), D ** -0.5, 0.1875, ((0, 8),)),
        "norm_first": jnp.clip(1.0 + 0.15 * jax.random.normal(key_of[13], (D,), jnp.float32), 0.25, 1.75).astype(jnp.bfloat16),
        "norm_second": jnp.clip(1.0 + 0.15 * jax.random.normal(key_of[14], (D,), jnp.float32), 0.25, 1.75).astype(jnp.bfloat16),
        "gate_weight": scatter_about(key_of[15], (D, FF), D ** -0.5, 0.1875, ((0, 8), (1, 4))),
        "up_weight": scatter_about(key_of[16], (D, FF), D ** -0.5, 0.1875, ((0, 8), (1, 4))),
        "down_weight": scatter_about(key_of[17], (FF, D), FF ** -0.5, 0.109375, ((0, 4), (1, 8))),
    }


highest_precision = lax.Precision.HIGHEST

@jax.custom_vjp
def low(v):
    return lax.optimization_barrier(v.astype(jnp.bfloat16)).astype(jnp.float32)

@jax.custom_vjp
def low_back(v):
    return v

def low_keep(v):
    return (low(v), None)

def low_pass(kept, grad):
    return (grad,)

def back_keep(v):
    return (v, None)

def back_low(kept, grad):
    return (low(grad),)
low.defvjp(low_keep, low_pass)
low_back.defvjp(back_keep, back_low)

def rms_norm(values, scales):
    return values * lax.rsqrt(lax.optimization_barrier(jnp.mean(values * values, axis=-1, keepdims=True)) + 1e-06) * scales

def unit_rows(values):
    return values * lax.rsqrt(lax.optimization_barrier(jnp.sum(values * values, axis=-1, keepdims=True)) + 1e-06)

def conv_rows(padded, kernels):
    tap_count = kernels.shape[0]
    length = padded.shape[0] - tap_count + 1
    summed = kernels[0] * padded[0:length]
    for offset in range(1, tap_count):
        summed = summed + kernels[offset] * padded[offset:offset + length]
    return summed

def activate(padded, beta_pre, conv_query, conv_key, conv_value):
    model_width = conv_query.shape[1]
    head_count = beta_pre.shape[1]
    head_feature_width = model_width // head_count
    mixed = jax.nn.silu(conv_rows(padded, jnp.concatenate([conv_query, conv_key, conv_value], axis=1)))
    length = mixed.shape[0]
    query_row_block = unit_rows(mixed[:, :model_width].reshape(length, head_count, head_feature_width)) * head_feature_width ** (-0.5)
    key_row_block = unit_rows(mixed[:, model_width:2 * model_width].reshape(length, head_count, head_feature_width))
    value_rows = mixed[:, 2 * model_width:].reshape(length, head_count, head_feature_width)
    beta_rows = jax.nn.sigmoid(beta_pre)[..., None]
    return (query_row_block, key_row_block, value_rows, beta_rows)

def lower_system(key_row_block, beta_rows):
    block_size = key_row_block.shape[1]
    row_index = lax.broadcasted_iota(jnp.int32, (block_size, block_size), 0)
    col_index = lax.broadcasted_iota(jnp.int32, (block_size, block_size), 1)
    gram_matrix = jnp.einsum('hik,hjk->hij', key_row_block * beta_rows, key_row_block, precision=highest_precision)
    return jnp.where(row_index > col_index, gram_matrix, 0.0) + jnp.where(row_index == col_index, 1.0, 0.0)

def solve_lower(matrix, right_side):
    return jax.scipy.linalg.solve_triangular(matrix, right_side, lower=True, unit_diagonal=True)

def block_step(current_state, block_data):
    query_row_block, key_row_block, value_rows, beta_rows = block_data
    block_size = key_row_block.shape[1]
    head_feature_width = key_row_block.shape[2]
    matrix = lower_system(key_row_block, beta_rows)
    triangular_result = jax.vmap(solve_lower)(matrix, jnp.concatenate([key_row_block * beta_rows, value_rows * beta_rows], axis=-1))
    prediction_error = triangular_result[..., head_feature_width:] - jnp.einsum('ezw,ewo->ezo', triangular_result[..., :head_feature_width], current_state, precision=highest_precision)
    row_index = lax.broadcasted_iota(jnp.int32, (block_size, block_size), 0)
    col_index = lax.broadcasted_iota(jnp.int32, (block_size, block_size), 1)
    attention_scores = jnp.where(row_index >= col_index, jnp.einsum('hik,hjk->hij', query_row_block, key_row_block, precision=highest_precision), 0.0)
    output = jnp.einsum('ezw,ewo->ezo', query_row_block, current_state, precision=highest_precision) + jnp.einsum('trn,tnk->trk', attention_scores, prediction_error, precision=highest_precision)
    current_state = current_state + jnp.einsum('olb,oly->oby', key_row_block, prediction_error, precision=highest_precision)
    return (current_state, output)

def to_blocks(tensor, block_size):
    block_count = tensor.shape[0] // block_size
    return tensor.reshape(block_count, block_size, tensor.shape[1], tensor.shape[2]).transpose(0, 2, 1, 3)

def from_blocks(tensor):
    return tensor.transpose(0, 2, 1, 3).reshape(tensor.shape[0] * tensor.shape[2], tensor.shape[1], tensor.shape[3])

def run_mixer(query_row_block, key_row_block, value_rows, beta_rows, state_in, block_size):
    blocks = (to_blocks(query_row_block, block_size), to_blocks(key_row_block, block_size), to_blocks(value_rows, block_size), to_blocks(beta_rows, block_size))
    state_out, outputs = lax.scan(jax.checkpoint(block_step), state_in, blocks)
    return (from_blocks(outputs), state_out)

def out_norm(outputs, scales):
    normed_out = outputs * lax.rsqrt(lax.optimization_barrier(jnp.mean(outputs * outputs, axis=-1, keepdims=True)) + 1e-05) * scales
    return normed_out.reshape(outputs.shape[0], outputs.shape[1] * outputs.shape[2])

def swiglu(gate_up):
    half_width = gate_up.shape[1] // 2
    return jax.nn.silu(gate_up[:, :half_width]) * gate_up[:, half_width:]

def forward(tokens, query_weight, key_weight, value_weight, beta_weight, conv_query, conv_key, conv_value, out_gain, out_weight, norm_first, norm_second, gate_weight, up_weight, down_weight):
    normed = low(rms_norm(tokens, norm_first))
    projected = low_back(jnp.concatenate([jnp.dot(normed, query_weight, precision=highest_precision), jnp.dot(normed, key_weight, precision=highest_precision), jnp.dot(normed, value_weight, precision=highest_precision)], axis=1))
    beta_pre = low_back(jnp.dot(normed, beta_weight, precision=highest_precision))
    padded = jnp.concatenate([jnp.zeros((KW - 1, projected.shape[1]), jnp.float32), projected], axis=0)
    query_row_block, key_row_block, value_rows, beta_rows = activate(padded, beta_pre, conv_query, conv_key, conv_value)
    outputs, final_state = run_mixer(query_row_block, key_row_block, value_rows, beta_rows, jnp.zeros((H, DK, DK), jnp.float32), C)
    mixed = low(out_norm(outputs, out_gain))
    middle = tokens + low_back(jnp.dot(mixed, out_weight, precision=highest_precision))
    second = low(rms_norm(middle, norm_second))
    gate_up = low_back(jnp.concatenate([jnp.dot(second, gate_weight, precision=highest_precision), jnp.dot(second, up_weight, precision=highest_precision)], axis=1))
    hidden = low(swiglu(gate_up))
    return middle + low_back(jnp.dot(hidden, down_weight, precision=highest_precision))

def reference(tokens, cotangent, domain, domain_weight, query_weight, key_weight, value_weight, beta_weight, conv_query, conv_key, conv_value, out_gain, out_weight, norm_first, norm_second, gate_weight, up_weight, down_weight):
    weights = tuple((matrix.astype(jnp.float32) for matrix in (query_weight, key_weight, value_weight, beta_weight, conv_query, conv_key, conv_value, out_gain, out_weight, norm_first, norm_second, gate_weight, up_weight, down_weight)))
    token_seqs = tokens.astype(jnp.float32).reshape(NSEQ, LENGTH, D)
    cot_seqs = cotangent.astype(jnp.float32).reshape(NSEQ, LENGTH, D)
    seq_scales = domain_weight[domain]

    def per_sequence(grad_sums, sequence):
        seq_tokens, seq_cot, seq_scale = sequence
        result, pullback = jax.vjp(forward, seq_tokens, *weights)
        seq_grads = pullback(seq_cot * seq_scale)
        grad_sums = tuple((total_grad + new_grad for total_grad, new_grad in zip(grad_sums, seq_grads[1:])))
        return (grad_sums, (result.astype(jnp.bfloat16), seq_grads[0]))
    initial = tuple((jnp.zeros(matrix.shape, jnp.float32) for matrix in weights))
    grad_sums, (outputs, input_grads) = lax.scan(per_sequence, initial, (token_seqs, cot_seqs, seq_scales))
    return (outputs.reshape(TOKENS, D), input_grads.reshape(TOKENS, D), grad_sums[0], grad_sums[1], grad_sums[2], grad_sums[3], grad_sums[4], grad_sums[5], grad_sums[6], grad_sums[7], grad_sums[8], grad_sums[9], grad_sums[10], grad_sums[11], grad_sums[12], grad_sums[13])
```

```python
from functools import partial

import jax
import jax.numpy as jnp
from jax import lax
from jax.experimental import pallas as pl
from jax.experimental.pallas import tpu as pltpu
from jax.sharding import PartitionSpec as P

BLOCK = 128
MESH = pl.DeviceIdType.MESH
F32 = jnp.float32
BF16 = jnp.bfloat16
MIB = 1 << 20
VM = pl.BlockSpec(memory_space=pltpu.VMEM)
ANY = pl.BlockSpec(memory_space=pl.ANY)


def dot(a, b, ta=False, tb=False):
    dims = (((0 if ta else 1,), (1 if tb else 0,)), ((), ()))
    return lax.dot_general(a, b, dims, preferred_element_type=F32)


def halves(a):
    high = a.astype(BF16)
    return high, (a - high.astype(F32)).astype(BF16)


def mm(a, b, ta=False, tb=False):
    ah, al = halves(a)
    bh, bl = halves(b)
    da, db = 0 if ta else 1, 1 if tb else 0
    left = jnp.concatenate([ah, al], axis=da)
    right = jnp.concatenate([bh, bh], axis=db)
    return dot(left, right, ta, tb) + dot(ah, bl, ta, tb)


def iota2(size):
    return (
        lax.broadcasted_iota(jnp.int32, (size, size), 0),
        lax.broadcasted_iota(jnp.int32, (size, size), 1),
    )


def unit_lower_inverse(strict):
    size = strict.shape[0]
    row, col = iota2(size)
    inverse = jnp.where(row == col, 1.0, 0.0) - jnp.where((row >> 1) == (col >> 1), strict, 0.0)
    shift = 1
    while (1 << shift) < size:
        inside = (row >> (shift + 1)) == (col >> (shift + 1))
        apart = (row >> shift) != (col >> shift)
        corner = jnp.where(inside & apart, strict, 0.0)
        inverse = inverse - mm(mm(inverse, corner), inverse)
        shift += 1
    return inverse


def sigmoid(a):
    return 1.0 / (1.0 + jnp.exp(-a))


class Gather:
    def __init__(self, axis, count, src, out, sems, slot):
        self.axis, self.src, self.out = axis, src, out
        self.outer = count // 2
        self.me = lax.axis_index(axis)
        self.a, self.b = self.me // 2, self.me % 2
        self.sa, self.ra, self.sb, self.rb, self.local = (s.at[slot] for s in sems)
        self.beside = self.a * 2 + 1 - self.b

    @staticmethod
    def scratch(count, slots):
        return [pltpu.SemaphoreType.DMA((slots, count // 2))] * 4 + [
            pltpu.SemaphoreType.DMA((slots, 1))
        ]

    def copy(self, src, block, send, recv, target):
        return pltpu.make_async_remote_copy(
            src_ref=src,
            dst_ref=self.out.at[block],
            send_sem=send,
            recv_sem=recv,
            device_id={self.axis: target},
            device_id_type=MESH,
        )

    def own(self):
        return pltpu.make_async_copy(self.src, self.out.at[self.me], self.local.at[0])

    def to_outer(self, k):
        return self.copy(
            self.src,
            self.me,
            self.sa.at[k],
            self.ra.at[k],
            (self.a + k) % self.outer * 2 + self.b,
        )

    def source(self, k):
        return (self.a + self.outer - k) % self.outer * 2 + self.b

    def to_beside(self, k):
        block = self.source(k)
        src = self.src if k == 0 else self.out.at[block]
        return self.copy(src, block, self.sb.at[k], self.rb.at[k], self.beside)

    def start(self):
        for k in range(1, self.outer):
            self.to_outer(k).start()
        self.to_beside(0).start()
        self.own().start()

    def forward(self, k):
        self.to_outer(k).wait_recv()
        self.to_beside(k).start()

    def finish(self):
        self.own().wait()
        for k in range(self.outer):
            if k:
                self.to_outer(k).wait_send()
            self.to_beside(k).wait()


class ReduceScatter:
    def __init__(self, axis, count, blocks, near, joined, far, sems, slot):
        self.axis, self.blocks, self.near, self.joined, self.far = axis, blocks, near, joined, far
        self.outer = count // 2
        self.me = lax.axis_index(axis)
        self.a, self.b = self.me // 2, self.me % 2
        self.sa, self.ra, self.sb, self.rb = (s.at[slot] for s in sems)
        self.beside = self.a * 2 + 1 - self.b

    @staticmethod
    def scratch(count, slots):
        return [pltpu.SemaphoreType.DMA((slots, count // 2))] * 4

    @staticmethod
    def buffers(count, rows, columns, kind=BF16):
        outer = count // 2
        return [
            pltpu.VMEM((outer, rows, columns), kind),
            pltpu.VMEM((outer, rows, columns), kind),
            pltpu.VMEM((outer, rows, columns), kind),
        ]

    def target(self, k):
        return (self.a + k) % self.outer

    def to_beside(self, k):
        return pltpu.make_async_remote_copy(
            src_ref=self.blocks.at[self.target(k) * 2 + 1 - self.b],
            dst_ref=self.near.at[k],
            send_sem=self.sb.at[k],
            recv_sem=self.rb.at[k],
            device_id={self.axis: self.beside},
            device_id_type=MESH,
        )

    def to_outer(self, k):
        return pltpu.make_async_remote_copy(
            src_ref=self.joined.at[k],
            dst_ref=self.far.at[k],
            send_sem=self.sa.at[k],
            recv_sem=self.ra.at[k],
            device_id={self.axis: self.target(k) * 2 + self.b},
            device_id_type=MESH,
        )

    def order(self):
        return [k for k in range(1, self.outer)] + [0]

    def start(self):
        for k in self.order():
            self.to_beside(k).start()

    def join(self, k):
        self.to_beside(k).wait_recv()
        total = self.blocks[self.target(k) * 2 + self.b].astype(F32) + self.near[k].astype(F32)
        if k == 0:
            return total
        self.joined[k] = total.astype(self.joined.dtype)
        self.to_outer(k).start()

    def finish(self, total):
        for k in range(1, self.outer):
            self.to_outer(k).wait_recv()
            total = total + self.far[k].astype(F32)
        for k in range(self.outer):
            self.to_beside(k).wait_send()
            if k:
                self.to_outer(k).wait_send()
        return total


def greet(counts, whole=()):
    barrier = pltpu.get_barrier_semaphore()
    number = 0
    for axis, count in counts:
        me = lax.axis_index(axis)
        if axis in whole:
            targets = [(me + k) % count for k in range(1, count)]
        else:
            targets = [(me // 2 + k) % (count // 2) * 2 + me % 2 for k in range(1, count // 2)]
            targets.append(me // 2 * 2 + 1 - me % 2)
        for target in targets:
            pl.semaphore_signal(barrier, inc=1, device_id={axis: target}, device_id_type=MESH)
        number += len(targets)
    pl.semaphore_wait(barrier, number)


def gather_kernel(dp, mp, *refs):
    tokens, cotangent, qkv, small, gate, up, down, out = refs[:8]
    tokens_all, cotangent_all, qkv_all, small_all, gate_all, up_all, down_all, out_rows = refs[8:16]
    sems_mp = refs[16:21]
    sems_dp = refs[21:26]
    out_send, out_recv, out_local = refs[26:29]
    greet((("dp", dp), ("mp", mp)), whole=("dp",))
    over_mp = [
        Gather("mp", mp, tokens, tokens_all, sems_mp, 0),
        Gather("mp", mp, cotangent, cotangent_all, sems_mp, 1),
    ]
    over_dp = [
        Gather("dp", dp, src, dst, sems_dp, slot)
        for slot, (src, dst) in enumerate(
            ((small, small_all), (qkv, qkv_all), (gate, gate_all), (up, up_all), (down, down_all))
        )
    ]
    over_mp[0].start()
    over_dp[0].start()
    over_dp[1].start()
    over_mp[1].start()
    for g in over_dp[2:]:
        g.start()
    me = lax.axis_index("dp")
    column = lax.axis_index("mp")
    share = dp // mp

    def row_copy(k, source):
        return pltpu.make_async_remote_copy(
            src_ref=out,
            dst_ref=out_rows.at[source],
            send_sem=out_send.at[k],
            recv_sem=out_recv.at[source],
            device_id={"dp": (me + k) % dp},
            device_id_type=MESH,
        )

    sends_out = me // share == column

    @pl.when(sends_out)
    def _():
        for k in range(1, dp):
            row_copy(k, me % share).start()
        pltpu.make_async_copy(out, out_rows.at[me % share], out_local.at[0]).start()

    for group in (over_mp, over_dp):
        for g in group:
            for k in range(1, g.outer):
                g.forward(k)
    for g in over_mp + over_dp:
        g.finish()

    @pl.when(sends_out)
    def _():
        for k in range(1, dp):
            row_copy(k, me % share).wait_send()
        pltpu.make_async_copy(out, out_rows.at[me % share], out_local.at[0]).wait()

    for source in range(share):

        @pl.when(column * share + source != me)
        def _(source=source):
            row_copy(1, source).wait_recv()


def conv_window(p, start, columns, taps):
    window = p[pl.ds(start, BLOCK + 8), columns]
    return [window[8 - taps + 1 + j : 8 - taps + 1 + j + BLOCK] for j in range(taps)]


def activated(p, conv, start, part, head, width, taps):
    columns = slice(part * width + head * BLOCK, part * width + (head + 1) * BLOCK)
    shifted = conv_window(p, start, columns, taps)
    pre = conv[0:1, columns] * shifted[0]
    for j in range(1, taps):
        pre = pre + conv[j : j + 1, columns] * shifted[j]
    gate = sigmoid(pre)
    return pre * gate, gate, shifted


def mixer_forward_kernel(taps, heads, *refs):
    (tokens, qkv, beta_rows, conv, first, gain, out_rows) = refs[:7]
    (part, h, p, beta_pre, inverse, w, scores, step, delta, state, o, m) = refs[7:19]
    (u, offset, q_all) = refs[19:22]
    length, model = tokens.shape
    width = heads * BLOCK
    blocks = length // BLOCK
    rows = 256
    p[0:8] = jnp.zeros((8, p.shape[1]), F32)

    @pl.loop(0, length // rows)
    def _(i):
        at = pl.ds(pl.multiple_of(i * rows, rows), rows)
        x = tokens[at].astype(F32)
        normed = x * lax.rsqrt(jnp.mean(x * x, axis=-1, keepdims=True) + 1e-06) * first[...]
        low = normed.astype(BF16)
        h[at] = low
        p[pl.ds(pl.multiple_of(i * rows + 8, 8), rows)] = dot(low, qkv[...])
        beta_pre[at] = dot(low, beta_rows[...], tb=True)

    row, col = iota2(BLOCK)
    scale = BLOCK**-0.5

    def prepare(c, head):
        start = pl.multiple_of(c * BLOCK, BLOCK)
        place = head * blocks + c
        lanes = slice(head * BLOCK, (head + 1) * BLOCK)
        s, _, _ = activated(p, conv, start, 0, head, width, taps)
        q = s * (lax.rsqrt(jnp.sum(s * s, axis=-1, keepdims=True) + 1e-06) * scale)
        s, _, _ = activated(p, conv, start, 1, head, width, taps)
        k = s * lax.rsqrt(jnp.sum(s * s, axis=-1, keepdims=True) + 1e-06)
        v, _, _ = activated(p, conv, start, 2, head, width, taps)
        beta = sigmoid(beta_pre[pl.ds(start, BLOCK), head : head + 1])
        kb = k * beta
        strict = jnp.where(row > col, mm(kb, k, tb=True), 0.0)
        x = unit_lower_inverse(strict)
        wu = mm(x, jnp.concatenate([kb, v * beta], axis=1))
        sc = jnp.where(row >= col, mm(q, k, tb=True), 0.0)
        gb = mm(k, wu, ta=True)
        inverse[place] = x
        w[place] = wu[:, :BLOCK]
        u[place] = wu[:, BLOCK:]
        scores[place] = sc
        step[place] = gb[:, :BLOCK]
        offset[place] = gb[:, BLOCK:]
        q_all[pl.ds(start, BLOCK), lanes] = q

    @pl.loop(0, blocks)
    def _(c):
        for head in range(heads):
            prepare(c, head)

    def advance(c, states):
        after = []
        for head in range(heads):
            place = head * blocks + c
            state[place] = states[head]
            after.append(states[head] - mm(step[place], states[head]) + offset[place])
        return tuple(after)

    lax.fori_loop(0, blocks, advance, tuple(jnp.zeros((BLOCK, BLOCK), F32) for _ in range(heads)))

    @pl.loop(0, blocks)
    def _(c):
        start = pl.multiple_of(c * BLOCK, BLOCK)
        for head in range(heads):
            place = head * blocks + c
            lanes = slice(head * BLOCK, (head + 1) * BLOCK)
            q = q_all[pl.ds(start, BLOCK), lanes]
            both = mm(jnp.concatenate([w[place], q], axis=0), state[place])
            d = u[place] - both[:BLOCK]
            delta[place] = d
            out = both[BLOCK:] + mm(scores[place], d)
            o[pl.ds(start, BLOCK), lanes] = out
            r = lax.rsqrt(jnp.mean(out * out, axis=-1, keepdims=True) + 1e-05)
            m[pl.ds(start, BLOCK), lanes] = (out * r * gain[...]).astype(BF16)

    @pl.loop(0, length // rows)
    def _(i):
        at = pl.ds(pl.multiple_of(i * rows, rows), rows)
        part[at] = dot(m[at], out_rows[...]).astype(BF16)


def middle_kernel(mp, part, tokens, second, y1, h2_all, *scratch):
    near, joined, far, low = scratch[:4]
    sems, gather_sems = scratch[4:8], scratch[8:13]
    greet((("mp", mp),))
    reduce = ReduceScatter("mp", mp, part, near, joined, far, sems, 0)
    reduce.start()
    for k in range(1, reduce.outer):
        reduce.join(k)
    y = tokens[...].astype(F32) + reduce.finish(reduce.join(0))
    y1[...] = y
    low[...] = (
        y * lax.rsqrt(jnp.mean(y * y, axis=-1, keepdims=True) + 1e-06) * second[...]
    ).astype(BF16)
    gather = Gather("mp", mp, low, h2_all, gather_sems, 0)
    gather.start()
    for k in range(1, gather.outer):
        gather.forward(k)
    gather.finish()


def feed_kernel(h2, cot, scale, gate, up, down, y_part, dh_part, d_gate, d_up, d_down, z, dg, du, gb):
    length, model = h2.shape
    rows = 256

    @pl.loop(0, length // rows)
    def _(i):
        at = pl.ds(pl.multiple_of(i * rows, rows), rows)
        x = h2[at]
        g = dot(x, gate[...])
        u = dot(x, up[...])
        sg = sigmoid(g)
        silu = g * sg
        hidden = (silu * u).astype(BF16)
        z[at] = hidden
        y_part[at] = dot(hidden, down[...], tb=True).astype(BF16)
        low = (cot[at].astype(F32) * scale[...]).astype(BF16)
        gb[at] = low
        dz = dot(low, down[...])
        dgl = (dz * u * (sg + silu * (1.0 - sg))).astype(BF16)
        dul = (dz * silu).astype(BF16)
        dg[at] = dgl
        du[at] = dul
        dh_part[at] = (dot(dgl, gate[...], tb=True) + dot(dul, up[...], tb=True)).astype(BF16)

    tile = 256

    @pl.loop(0, model // tile)
    def _(i):
        at = pl.ds(pl.multiple_of(i * tile, tile), tile)
        x = h2[:, at]
        d_gate[at] = dot(x, dg[...], ta=True).astype(BF16)
        d_up[at] = dot(x, du[...], ta=True).astype(BF16)
        d_down[at] = dot(gb[:, at], z[...], ta=True).astype(BF16)


def turn_kernel(mp, dh_part, y_part, cot, y1, second, scale, dy1, ab_all, output, d_second, *scratch):
    near, joined, far, low = scratch[:4]
    near_y, joined_y, far_y = scratch[4:7]
    sems, gather_sems = scratch[7:11], scratch[11:16]
    greet((("mp", mp),))
    reduce = ReduceScatter("mp", mp, dh_part, near, joined, far, sems, 0)
    reduce_y = ReduceScatter("mp", mp, y_part, near_y, joined_y, far_y, sems, 1)
    reduce.start()
    reduce_y.start()
    for k in range(1, reduce.outer):
        reduce.join(k)
    dh = reduce.finish(reduce.join(0))
    y = y1[...]
    r = lax.rsqrt(jnp.mean(y * y, axis=-1, keepdims=True) + 1e-06)
    d_second[...] = jnp.sum(dh * y * r, axis=0, keepdims=True)
    scaled = second[...] * dh
    grad = (
        cot[...].astype(F32) * scale[...]
        + r * scaled
        - y * (r * r * r * jnp.mean(y * scaled, axis=-1, keepdims=True))
    )
    dy1[...] = grad
    low[...] = grad.astype(BF16)
    gather = Gather("mp", mp, low, ab_all, gather_sems, 0)
    gather.start()
    for k in range(1, reduce.outer):
        reduce_y.join(k)
    branch = reduce_y.join(0)
    for k in range(1, gather.outer):
        gather.forward(k)
    output[...] = (y + reduce_y.finish(branch)).astype(BF16)
    gather.finish()


def mixer_backward_kernel(taps, heads, *refs):
    (ab, out_rows, m, o, gain, p, conv, beta_pre, beta_rows) = refs[:9]
    (inverse, w, scores, step, delta, state, h, qkv) = refs[9:17]
    (dh_part, d_out, d_qkv, d_beta, d_conv, d_gain) = refs[17:23]
    (do, entry, ds_all, dc, dp_low, db_low) = refs[23:29]
    length, model = ab.shape
    width = heads * BLOCK
    blocks = length // BLOCK
    rows = 256
    row, col = iota2(BLOCK)
    scale = BLOCK**-0.5
    d_gain[...] = jnp.zeros_like(d_gain)
    d_conv[...] = jnp.zeros_like(d_conv)
    dc[pl.ds(length, 8)] = jnp.zeros((8, dc.shape[1]), F32)

    @pl.loop(0, length // rows)
    def _(i):
        at = pl.ds(pl.multiple_of(i * rows, rows), rows)
        dm = dot(ab[at], out_rows[...], tb=True)
        for head in range(heads):
            lanes = slice(head * BLOCK, (head + 1) * BLOCK)
            x = o[at, lanes]
            g = dm[:, lanes]
            r = lax.rsqrt(jnp.mean(x * x, axis=-1, keepdims=True) + 1e-05)
            d_gain[...] += jnp.sum(g * x * r, axis=0, keepdims=True)
            scaled = g * gain[...]
            do[at, lanes] = r * scaled - x * (
                r * r * r * jnp.mean(x * scaled, axis=-1, keepdims=True)
            )

    tile = 256

    @pl.loop(0, model // tile)
    def _(i):
        at = pl.ds(pl.multiple_of(i * tile, tile), tile)
        d_out[:, at] = dot(m[...], ab[:, at], ta=True).astype(BF16)

    def queries(start, head):
        s, gate, shifted = activated(p, conv, start, 0, head, width, taps)
        r = lax.rsqrt(jnp.sum(s * s, axis=-1, keepdims=True) + 1e-06)
        return s, gate, shifted, r

    @pl.loop(0, blocks)
    def _(c):
        start = pl.multiple_of(c * BLOCK, BLOCK)
        for head in range(heads):
            place = head * blocks + c
            lanes = slice(head * BLOCK, (head + 1) * BLOCK)
            s, _, _, r = queries(start, head)
            effective = s * (r * scale) - mm(scores[place], w[place])
            entry[place] = mm(effective, do[pl.ds(start, BLOCK), lanes], ta=True)

    def retreat(i, grads):
        c = blocks - 1 - i
        before = []
        for head in range(heads):
            place = head * blocks + c
            ds_all[place] = grads[head]
            before.append(grads[head] - mm(step[place], grads[head], ta=True) + entry[place])
        return tuple(before)

    lax.fori_loop(0, blocks, retreat, tuple(jnp.zeros((BLOCK, BLOCK), F32) for _ in range(heads)))

    def through(pre_parts, grad, start, part, head):
        s, gate, shifted = pre_parts
        columns = slice(part * width + head * BLOCK, part * width + (head + 1) * BLOCK)
        d_pre = grad * (gate + s * (1.0 - gate))
        dc[pl.ds(start, BLOCK), columns] = d_pre
        for j in range(taps):
            d_conv[j : j + 1, columns] += jnp.sum(d_pre * shifted[j], axis=0, keepdims=True)

    @pl.loop(0, blocks)
    def _(c):
        start = pl.multiple_of(c * BLOCK, BLOCK)
        beta_lanes = jnp.zeros((BLOCK, BLOCK), F32)
        for head in range(heads):
            place = head * blocks + c
            lanes = slice(head * BLOCK, (head + 1) * BLOCK)
            sq, gq, hq, rq = queries(start, head)
            q = sq * (rq * scale)
            sk, gk, hk = activated(p, conv, start, 1, head, width, taps)
            rk = lax.rsqrt(jnp.sum(sk * sk, axis=-1, keepdims=True) + 1e-06)
            k = sk * rk
            v, gv, hv = activated(p, conv, start, 2, head, width, taps)
            beta = sigmoid(beta_pre[pl.ds(start, BLOCK), head : head + 1])
            kb = k * beta
            d_o = do[pl.ds(start, BLOCK), lanes]
            d = delta[place]
            s_in = state[place]
            ds_out = ds_all[place]
            d_delta = mm(scores[place], d_o, ta=True) + mm(k, ds_out)
            e = mm(inverse[place], d_delta, ta=True)
            d_scores = jnp.where(row >= col, mm(d_o, d, tb=True), 0.0)
            d_strict = jnp.where(row > col, -mm(e, d, tb=True), 0.0)
            dq = mm(d_o, s_in, tb=True) + mm(d_scores, k)
            f = mm(d_strict, k) - mm(e, s_in, tb=True)
            dk = (
                mm(d_scores, q, ta=True)
                + mm(d, ds_out, tb=True)
                + mm(d_strict, kb, ta=True)
                + beta * f
            )
            d_beta_row = jnp.sum(f * k + e * v, axis=-1, keepdims=True) * beta * (1.0 - beta)
            beta_lanes = beta_lanes + jnp.where(col == head, d_beta_row, 0.0)
            gq_in = dq * scale
            through(
                (sq, gq, hq),
                rq * gq_in - sq * (rq * rq * rq * jnp.sum(sq * gq_in, axis=-1, keepdims=True)),
                start, 0, head,
            )
            through(
                (sk, gk, hk),
                rk * dk - sk * (rk * rk * rk * jnp.sum(sk * dk, axis=-1, keepdims=True)),
                start, 1, head,
            )
            through((v, gv, hv), beta * e, start, 2, head)
        db_low[pl.ds(start, BLOCK)] = beta_lanes.astype(BF16)

    @pl.loop(0, blocks)
    def _(c):
        start = pl.multiple_of(c * BLOCK, BLOCK)
        window = dc[pl.ds(start, BLOCK + 8)]
        total = conv[taps - 1 : taps] * window[0:BLOCK]
        for j in range(taps - 1):
            ahead = taps - 1 - j
            total = total + conv[j : j + 1] * window[ahead : ahead + BLOCK]
        dp_low[pl.ds(start, BLOCK)] = total.astype(BF16)

    @pl.loop(0, length // rows)
    def _(i):
        at = pl.ds(pl.multiple_of(i * rows, rows), rows)
        dh_part[at] = (
            dot(dp_low[at], qkv[...], tb=True) + dot(db_low[at], beta_rows[...])
        ).astype(BF16)

    @pl.loop(0, model // tile)
    def _(i):
        at = pl.ds(pl.multiple_of(i * tile, tile), tile)
        x = h[:, at]
        d_qkv[at] = dot(x, dp_low[...], ta=True).astype(BF16)
        d_beta[:, at] = dot(db_low[...], x, ta=True)[0 : d_beta.shape[0]]


def final_kernel(dp, mp, first_row, *refs):
    (dh_part, tokens, first, dy1, qkv_part, out_part, small_part, gate_part, up_part, down_part) = refs[:10]
    (input_grad, d_query, d_key, d_value, d_outw, d_small, d_gate, d_up, d_down) = refs[10:19]
    scratch = refs[19:]
    cursor = 0

    def take(n):
        nonlocal cursor
        cursor += n
        return scratch[cursor - n : cursor]

    near, joined, far = take(3)
    dp_buffers = [take(3) for _ in range(6)]
    out_columns, = take(1)
    small_own, = take(1)
    shared, shared_all, small_low, small_all = take(4)
    sems_mp, sems_dp, sems_share = take(4), take(4), take(5)
    swap_send, swap_recv = take(2)
    greet((("dp", dp), ("mp", mp)), whole=("mp",))
    share = mp
    column = lax.axis_index("mp")
    group = out_part.shape[1]
    rows = tokens.shape[0]

    over_dp = [
        ReduceScatter("dp", dp, blocks, *buffers, sems_dp, slot)
        for slot, (blocks, buffers) in enumerate(
            zip((qkv_part, gate_part, up_part, down_part, out_columns, small_own), dp_buffers)
        )
    ]
    reduce = ReduceScatter("mp", mp, dh_part, near, joined, far, sems_mp, 0)
    reduce.start()
    over_dp[0].start()

    def swap(k):
        target = (column + k) % mp
        per = dp // mp
        return pltpu.make_async_remote_copy(
            src_ref=out_part.at[target],
            dst_ref=out_columns.at[pl.ds(column * per, per)],
            send_sem=swap_send.at[k],
            recv_sem=swap_recv.at[k],
            device_id={"mp": target},
            device_id_type=MESH,
        )

    def swap_in(k):
        source = (column + mp - k) % mp
        per = dp // mp
        return pltpu.make_async_remote_copy(
            src_ref=out_part.at[source],
            dst_ref=out_columns.at[pl.ds(source * per, per)],
            send_sem=swap_send.at[k],
            recv_sem=swap_recv.at[k],
            device_id={"mp": (column + k) % mp},
            device_id_type=MESH,
        )

    for k in range(1, mp):
        swap(k).start()
    per = dp // mp
    out_columns[pl.ds(column * per, per)] = out_part[column]
    for k in range(1, mp):
        swap_in(k).wait_recv()
    over_dp[4].start()
    for g in over_dp[1:4]:
        g.start()

    for k in range(1, reduce.outer):
        reduce.join(k)
    dh = reduce.finish(reduce.join(0))
    x = tokens[...].astype(F32)
    s = lax.rsqrt(jnp.mean(x * x, axis=-1, keepdims=True) + 1e-06)
    d_first = jnp.sum(dh * x * s, axis=0, keepdims=True)
    scaled = first[...] * dh
    input_grad[...] = (
        dy1[...] + s * scaled - x * (s * s * s * jnp.mean(x * scaled, axis=-1, keepdims=True))
    )
    small_own[...] = small_part[...]
    lanes = small_own.shape[2]
    for i in range(dp):
        small_own[i, first_row : first_row + 1] = d_first[:, i * lanes : (i + 1) * lanes]
    over_dp[5].start()

    order = [0, 4, 5, 1, 2, 3]
    for index in order:
        for k in range(1, over_dp[index].outer):
            over_dp[index].join(k)
    width = qkv_part.shape[2]
    third = width // 3
    total = over_dp[0].finish(over_dp[0].join(0))
    shared[:, 0:width] = total.astype(BF16)
    shared[:, width:] = over_dp[4].finish(over_dp[4].join(0)).astype(BF16)
    small_low[...] = over_dp[5].finish(over_dp[5].join(0))
    wide = Gather("mp", mp, shared, shared_all, sems_share, 0)
    narrow = Gather("mp", mp, small_low, small_all, sems_share, 1)
    wide.start()
    narrow.start()
    for index, result in ((1, d_gate), (2, d_up), (3, d_down)):
        result[...] = over_dp[index].finish(over_dp[index].join(0))
    for g in (wide, narrow):
        for k in range(1, g.outer):
            g.forward(k)
        g.finish()
    for k in range(1, mp):
        swap(k).wait_send()
    for i in range(mp):
        at = slice(i * third, (i + 1) * third)
        for index, result in enumerate((d_query, d_key, d_value, d_outw)):
            result[:, at] = shared_all[i, :, index * third : (index + 1) * third].astype(F32)
    small_total = small_all[0]
    for i in range(1, mp):
        small_total = small_total + small_all[i]
    d_small[...] = small_total


def call(kernel, outs, ins_specs, args, scratch=(), collective=None, name=None, out_specs=None, limit=60):
    return pl.pallas_call(
        kernel,
        out_shape=[jax.ShapeDtypeStruct(shape, kind) for shape, kind in outs],
        in_specs=ins_specs,
        out_specs=[VM] * len(outs) if out_specs is None else out_specs,
        scratch_shapes=list(scratch),
        compiler_params=pltpu.CompilerParams(
            collective_id=collective,
            has_side_effects=collective is not None,
            vmem_limit_bytes=limit * MIB,
        ),
        name=name,
    )(*args)


def shards(
    dp,
    mp,
    tokens,
    cotangent,
    domain,
    domain_weight,
    query_weight,
    key_weight,
    value_weight,
    beta_weight,
    conv_query,
    conv_key,
    conv_value,
    out_gain,
    out_weight,
    norm_first,
    norm_second,
    gate_weight,
    up_weight,
    down_weight,
):
    column = lax.axis_index("mp")
    own, model = tokens.shape
    length = own * mp
    shard = query_weight.shape[0]
    taps = conv_query.shape[0]
    all_heads = beta_weight.shape[1]
    heads = all_heads // mp
    width = model // mp
    feed = gate_weight.shape[1]
    lanes = norm_first.shape[0]
    gains = out_gain.shape[0]
    conv_row, gain_row = all_heads, all_heads + 3 * taps + 2
    first_row, second_row = gain_row - 2, gain_row - 1
    small_rows = -(-(gain_row + 1) // 16) * 16

    def mine(a):
        return lax.dynamic_slice_in_dim(a, column * width, width, 1)

    qkv_own = jnp.concatenate([mine(query_weight), mine(key_weight), mine(value_weight)], axis=1)
    small_own = jnp.concatenate(
        [
            beta_weight.T,
            conv_query,
            conv_key,
            conv_value,
            norm_first[None],
            norm_second[None],
            jnp.pad(out_gain, (0, lanes - gains))[None],
            jnp.zeros((small_rows - gain_row - 1, lanes), BF16),
        ],
        axis=0,
    )
    gathered = call(
        partial(gather_kernel, dp, mp),
        [
            ((mp, own, model), BF16),
            ((mp, own, model), BF16),
            ((dp, shard, 3 * width), BF16),
            ((dp, small_rows, lanes), BF16),
            ((dp, shard, feed), BF16),
            ((dp, shard, feed), BF16),
            ((dp, shard, feed), BF16),
            ((dp // mp, shard, model), BF16),
        ],
        [ANY] * 8,
        (tokens, cotangent, qkv_own, small_own, gate_weight, up_weight, down_weight.T, out_weight),
        Gather.scratch(mp, 2)
        + Gather.scratch(dp, 5)
        + [
            pltpu.SemaphoreType.DMA((dp,)),
            pltpu.SemaphoreType.DMA((dp // mp,)),
            pltpu.SemaphoreType.DMA((1,)),
        ],
        collective=0,
        name="gather",
        out_specs=[ANY] * 8,
        limit=16,
    )
    tokens_all, cot_all, qkv, small_all, gate, up, down, out_rows = gathered
    tokens_all = tokens_all.reshape(length, model)
    cot_all = cot_all.reshape(length, model)
    qkv = qkv.reshape(model, 3 * width)
    gate, up, down = (a.reshape(model, feed) for a in (gate, up, down))
    out_rows = out_rows.reshape(width, model)
    small = small_all.transpose(1, 0, 2).reshape(small_rows, model).astype(F32)
    beta_rows = jnp.pad(
        lax.dynamic_slice_in_dim(small, column * heads, heads, 0), ((0, BLOCK - heads), (0, 0))
    ).astype(BF16)
    conv = mine(small[conv_row : conv_row + 3 * taps])
    conv = jnp.concatenate([conv[i * taps : (i + 1) * taps] for i in range(3)], axis=1)
    first = small[first_row : first_row + 1]
    second = small[second_row : second_row + 1]
    gain = small_all[:, gain_row, :gains].reshape(1, -1).astype(F32)
    domain_index = lax.broadcasted_iota(jnp.int32, domain_weight.shape, 0)
    loss_scale = jnp.sum(jnp.where(domain_index == domain[0], domain_weight, 0.0)).reshape(1, 1)

    count = heads * (length // BLOCK)
    square = ((count, BLOCK, BLOCK), F32)
    squares = pltpu.VMEM(*square)
    part, h, p, beta_pre, inverse, w, scores, step, delta, state, o, m = call(
        partial(mixer_forward_kernel, taps, heads),
        [
            ((length, model), BF16),
            ((length, model), BF16),
            ((length + 8, 3 * width), F32),
            ((length, BLOCK), F32),
            square,
            square,
            square,
            square,
            square,
            square,
            ((length, width), F32),
            ((length, width), BF16),
        ],
        [VM] * 7,
        (tokens_all, qkv, beta_rows, conv, first, gain, out_rows),
        [squares, squares, pltpu.VMEM((length, width), F32)],
        name="mixer_forward",
    )

    def blocks_of(a):
        return a.reshape(mp, own, model)

    y1, h2_all = call(
        partial(middle_kernel, mp),
        [((own, model), F32), ((mp, own, model), BF16)],
        [VM] * 3,
        (blocks_of(part), tokens, second),
        ReduceScatter.buffers(mp, own, model)
        + [pltpu.VMEM((own, model), BF16)]
        + ReduceScatter.scratch(mp, 1)
        + Gather.scratch(mp, 1),
        collective=1,
        name="middle",
    )
    low_feed = pltpu.VMEM((length, feed), BF16)
    y_part, dh_part, d_gate, d_up, d_down = call(
        feed_kernel,
        [((length, model), BF16)] * 2 + [((model, feed), BF16)] * 3,
        [VM] * 6,
        (h2_all.reshape(length, model), cot_all, loss_scale, gate, up, down),
        [low_feed, low_feed, low_feed, pltpu.VMEM((length, model), BF16)],
        name="feed",
    )
    dy1, ab_all, output, d_second = call(
        partial(turn_kernel, mp),
        [
            ((own, model), F32),
            ((mp, own, model), BF16),
            ((own, model), BF16),
            ((1, model), F32),
        ],
        [VM] * 6,
        (blocks_of(dh_part), blocks_of(y_part), cotangent, y1, second, loss_scale),
        ReduceScatter.buffers(mp, own, model)
        + [pltpu.VMEM((own, model), BF16)]
        + ReduceScatter.buffers(mp, own, model)
        + ReduceScatter.scratch(mp, 2)
        + Gather.scratch(mp, 1),
        collective=2,
        name="turn",
    )
    dh_part, d_out, d_qkv, d_beta, d_conv, d_gain = call(
        partial(mixer_backward_kernel, taps, heads),
        [
            ((length, model), BF16),
            ((width, model), BF16),
            ((model, 3 * width), BF16),
            ((heads, model), F32),
            ((taps, 3 * width), F32),
            ((1, BLOCK), F32),
        ],
        [VM] * 17,
        (
            ab_all.reshape(length, model), out_rows, m, o, gain, p, conv, beta_pre, beta_rows,
            inverse, w, scores, step, delta, state, h, qkv,
        ),
        [
            pltpu.VMEM((length, width), F32),
            squares,
            squares,
            pltpu.VMEM((length + 8, 3 * width), F32),
            pltpu.VMEM((length, 3 * width), BF16),
            pltpu.VMEM((length, BLOCK), BF16),
        ],
        name="mixer_backward",
    )
    small_part = jnp.zeros((small_rows, model), F32)
    small_part = lax.dynamic_update_slice(small_part, d_beta, (column * heads, 0))
    d_conv = d_conv.reshape(taps, 3, width).transpose(1, 0, 2).reshape(3 * taps, width)
    small_part = lax.dynamic_update_slice(small_part, d_conv, (conv_row, column * width))
    small_part = lax.dynamic_update_slice(small_part, d_second, (second_row, 0))
    small_part = small_part.reshape(small_rows, dp, lanes).transpose(1, 0, 2)
    gain_part = jnp.pad(d_gain.reshape(dp, 1, gains), ((0, 0), (0, 0), (0, lanes - gains)))
    small_part = lax.dynamic_update_slice(small_part, gain_part, (0, gain_row, 0))

    def dp_blocks(a):
        return a.reshape(dp, shard, a.shape[1])

    out_part = d_out.reshape(width, mp, width).transpose(1, 0, 2).reshape(mp, dp // mp, shard, width)
    sizes = (3 * width, feed, feed, feed, width)
    results = call(
        partial(final_kernel, dp, mp, first_row),
        [
            ((own, model), F32),
            ((shard, model), F32),
            ((shard, model), F32),
            ((shard, model), F32),
            ((shard, model), F32),
            ((small_rows, lanes), F32),
            ((shard, feed), F32),
            ((shard, feed), F32),
            ((shard, feed), F32),
        ],
        [VM] * 10,
        (
            blocks_of(dh_part), tokens, first, dy1, dp_blocks(d_qkv), out_part, small_part,
            dp_blocks(d_gate), dp_blocks(d_up), dp_blocks(d_down),
        ),
        ReduceScatter.buffers(mp, own, model)
        + [b for size in sizes for b in ReduceScatter.buffers(dp, shard, size)]
        + ReduceScatter.buffers(dp, small_rows, lanes, F32)
        + [
            pltpu.VMEM((dp, shard, width), BF16),
            pltpu.VMEM((dp, small_rows, lanes), F32),
            pltpu.VMEM((shard, 4 * width), BF16),
            pltpu.VMEM((mp, shard, 4 * width), BF16),
            pltpu.VMEM((small_rows, lanes), F32),
            pltpu.VMEM((mp, small_rows, lanes), F32),
        ]
        + ReduceScatter.scratch(mp, 1)
        + ReduceScatter.scratch(dp, 6)
        + Gather.scratch(mp, 2)
        + [pltpu.SemaphoreType.DMA((mp,)), pltpu.SemaphoreType.DMA((mp,))],
        collective=3,
        name="final",
    )
    input_grad, d_query, d_key, d_value, d_outw, d_small, d_gate, d_up, d_down = results
    return (
        output,
        input_grad,
        d_query,
        d_key,
        d_value,
        d_small[0:all_heads].T,
        d_small[conv_row : conv_row + taps],
        d_small[conv_row + taps : conv_row + 2 * taps],
        d_small[conv_row + 2 * taps : conv_row + 3 * taps],
        d_small[gain_row, :gains],
        d_outw,
        d_small[first_row],
        d_small[second_row],
        d_gate,
        d_up,
        d_down.T,
    )


def solution(mesh):
    dp, mp = mesh.shape["dp"], mesh.shape["mp"]
    weight = P("dp", None)
    split = P(None, "dp")
    rows = P(("dp", "mp"), None)
    return jax.shard_map(
        partial(shards, dp, mp),
        mesh=mesh,
        in_specs=(
            rows, rows, P("dp"), P(), weight, weight, weight, weight, split, split, split,
            P("dp"), weight, P("dp"), P("dp"), P("dp", "mp"), P("dp", "mp"), P("mp", "dp"),
        ),
        out_specs=(
            rows, rows, weight, weight, weight, weight, split, split, split,
            P("dp"), weight, P("dp"), P("dp"), P("dp", "mp"), P("dp", "mp"), P("mp", "dp"),
        ),
        check_vma=False,
    )
```

```python
from functools import partial

import jax
import jax.numpy as jnp
from jax import lax
from jax.experimental import pallas as pl
from jax.experimental.pallas import tpu as pltpu
from jax.sharding import PartitionSpec as P

BLOCK = 128
MESH = pl.DeviceIdType.MESH
F32 = jnp.float32
BF16 = jnp.bfloat16
MIB = 1 << 20
VM = pl.BlockSpec(memory_space=pltpu.VMEM)
ANY = pl.BlockSpec(memory_space=pl.ANY)
SM = pl.BlockSpec(memory_space=pltpu.SMEM)


def dot(a, b, ta=False, tb=False):
    dims = (((0 if ta else 1,), (1 if tb else 0,)), ((), ()))
    return lax.dot_general(a, b, dims, preferred_element_type=F32)


def halves(a):
    high = a.astype(BF16)
    return high, (a - high.astype(F32)).astype(BF16)


def mm(a, b, ta=False, tb=False):
    ah, al = halves(a)
    bh, bl = halves(b)
    da, db = 0 if ta else 1, 1 if tb else 0
    left = jnp.concatenate([ah, al], axis=da)
    right = jnp.concatenate([bh, bh], axis=db)
    columns = b.shape[1 - db]
    if columns > BLOCK:
        return dot(left, right, ta, tb) + dot(ah, bl, ta, tb)
    rest = jnp.concatenate([bl, jnp.zeros_like(bl)], axis=db)
    both = dot(left, jnp.concatenate([right, rest], axis=1 - db), ta, tb)
    return both[:, :columns] + both[:, columns:]


def each(function, *lists):
    return [function(*items) for items in zip(*lists)]


def iota2(size):
    return (
        lax.broadcasted_iota(jnp.int32, (size, size), 0),
        lax.broadcasted_iota(jnp.int32, (size, size), 1),
    )


def unit_lower_inverses(stricts):
    size = stricts[0].shape[0]
    row, col = iota2(size)
    pairs = (row >> 1) == (col >> 1)
    unit = jnp.where(row == col, 1.0, 0.0)
    inverses = each(lambda a: unit - jnp.where(pairs, a, 0.0), stricts)
    shift = 1
    while (1 << shift) < size:
        inside = (row >> (shift + 1)) == (col >> (shift + 1))
        apart = (row >> shift) != (col >> shift)
        corner = inside & apart
        moved = each(lambda x, a: mm(x, jnp.where(corner, a, 0.0)), inverses, stricts)
        moved = each(mm, moved, inverses)
        inverses = each(lambda x, t: x - t, inverses, moved)
        shift += 1
    return inverses


def sigmoid(a):
    return 1.0 / (1.0 + jnp.exp(-a))


class Gather:
    def __init__(self, axis, count, src, place, sems, slot):
        self.axis, self.src, self.place = axis, src, place
        self.outer = count // 2
        self.me = lax.axis_index(axis)
        self.a, self.b = self.me // 2, self.me % 2
        self.sa, self.ra, self.sb, self.rb, self.local = (s.at[slot] for s in sems)
        self.beside = self.a * 2 + 1 - self.b

    @staticmethod
    def scratch(count, slots):
        return [pltpu.SemaphoreType.DMA((slots, count // 2))] * 4 + [
            pltpu.SemaphoreType.DMA((slots, 1))
        ]

    def copy(self, src, block, send, recv, target):
        return pltpu.make_async_remote_copy(
            src_ref=src,
            dst_ref=self.place(block),
            send_sem=send,
            recv_sem=recv,
            device_id={self.axis: target},
            device_id_type=MESH,
        )

    def own(self):
        return pltpu.make_async_copy(self.src, self.place(self.me), self.local.at[0])

    def source(self, k):
        return (self.a + self.outer - k) % self.outer * 2 + self.b

    def source_beside(self, k):
        return (self.a + self.outer - k) % self.outer * 2 + 1 - self.b

    def to_outer(self, k):
        target = (self.a + k) % self.outer * 2 + self.b
        return self.copy(self.src, self.me, self.sa.at[k], self.ra.at[k], target)

    def to_beside(self, k):
        block = self.source(k)
        src = self.src if k == 0 else self.place(block)
        return self.copy(src, block, self.sb.at[k], self.rb.at[k], self.beside)

    def start_outer(self):
        for k in range(1, self.outer):
            self.to_outer(k).start()

    def start_beside(self):
        self.to_beside(0).start()
        self.own().start()

    def start(self):
        self.start_outer()
        self.start_beside()

    def forward(self, k):
        self.to_outer(k).wait_recv()
        self.to_beside(k).start()

    def forward_all(self):
        for k in range(1, self.outer):
            self.forward(k)

    def arrived(self, k):
        self.to_beside(k).wait_recv()

    def sent(self):
        for k in range(self.outer):
            if k:
                self.to_outer(k).wait_send()
            self.to_beside(k).wait_send()

    def finish(self):
        self.own().wait()
        for k in range(self.outer):
            self.arrived(k)
        self.sent()


class ReduceScatter:
    def __init__(self, axis, count, place, near, far, sems, slot):
        self.axis, self.place, self.near, self.far = axis, place, near, far
        self.outer = count // 2
        self.me = lax.axis_index(axis)
        self.a, self.b = self.me // 2, self.me % 2
        self.sa, self.ra, self.sb, self.rb = (s.at[slot] for s in sems)
        self.beside = self.a * 2 + 1 - self.b

    @staticmethod
    def scratch(count, slots):
        return [pltpu.SemaphoreType.DMA((slots, count // 2))] * 4

    @staticmethod
    def buffers(count, rows, columns, kind=BF16):
        return [pltpu.VMEM((count // 2, rows, columns), kind)] * 2

    def target(self, k):
        return (self.a + k) % self.outer

    def kept(self, k):
        return self.target(k) * 2 + self.b

    def given(self, k):
        return self.target(k) * 2 + 1 - self.b

    def to_beside(self, k):
        return pltpu.make_async_remote_copy(
            src_ref=self.place(self.given(k)),
            dst_ref=self.near.at[k],
            send_sem=self.sb.at[k],
            recv_sem=self.rb.at[k],
            device_id={self.axis: self.beside},
            device_id_type=MESH,
        )

    def to_outer(self, k):
        return pltpu.make_async_remote_copy(
            src_ref=self.place(self.kept(k)),
            dst_ref=self.far.at[k],
            send_sem=self.sa.at[k],
            recv_sem=self.ra.at[k],
            device_id={self.axis: self.target(k) * 2 + self.b},
            device_id_type=MESH,
        )

    def start(self):
        for k in [*range(1, self.outer), 0]:
            self.to_beside(k).start()

    def join(self, k):
        self.to_beside(k).wait_recv()
        block = self.place(self.kept(k))
        total = block[...].astype(F32) + self.near[k].astype(F32)
        if k == 0:
            return total
        block[...] = total.astype(block.dtype)
        self.to_outer(k).start()

    def join_all(self):
        for k in range(1, self.outer):
            self.join(k)

    def finish(self):
        total = self.join(0)
        for k in range(1, self.outer):
            self.to_outer(k).wait_recv()
            total = total + self.far[k].astype(F32)
        return total

    def sent(self):
        for k in range(self.outer):
            self.to_beside(k).wait_send()
            if k:
                self.to_outer(k).wait_send()


def leading(ref):
    return lambda i: ref.at[i]


def columns_of(ref, size):
    return lambda i: ref.at[:, pl.ds(pl.multiple_of(i * size, size), size)]


def greet(counts):
    barrier = pltpu.get_barrier_semaphore()
    for axis, count in counts:
        me = lax.axis_index(axis)
        for k in range(1, count):
            pl.semaphore_signal(
                barrier, inc=1, device_id={axis: (me + k) % count}, device_id_type=MESH
            )
    pl.semaphore_wait(barrier, sum(count - 1 for _, count in counts))


class Taker:
    def __init__(self, refs):
        self.refs, self.cursor = refs, 0

    def __call__(self, count):
        self.cursor += count
        return self.refs[self.cursor - count : self.cursor]

    def one(self):
        return self(1)[0]


def activated(p, conv, start, part, head, width, taps):
    columns = slice(part * width + head * BLOCK, part * width + (head + 1) * BLOCK)
    window = p[pl.ds(start, BLOCK + 8), columns]
    shifted = [window[8 - taps + 1 + j : 8 - taps + 1 + j + BLOCK] for j in range(taps)]
    pre = conv[0:1, columns] * shifted[0]
    for j in range(1, taps):
        pre = pre + conv[j : j + 1, columns] * shifted[j]
    gate = sigmoid(pre)
    return pre * gate, gate, shifted


def inverse_norm(s):
    return lax.rsqrt(jnp.sum(s * s, axis=-1, keepdims=True) + 1e-06)


def place_lanes(index, count, lanes, gains):
    row = lax.broadcasted_iota(jnp.int32, (lanes, count * gains), 0)
    col = lax.broadcasted_iota(jnp.int32, (lanes, count * gains), 1)
    return jnp.where((col == row + index * gains) & (row < gains), 1.0, 0.0)


def block_kernel(dp, mp, taps, heads, gains, flip, rows_of, *refs):
    take = Taker(refs)
    domain, domain_weight = take(2)
    tokens, cot = take(2)
    projections, smalls = take(4), take(7)
    gate_own, up_own, down_own = take(3)
    output, input_grad, shared_all, d_small, d_gate, d_up, d_down = take(7)
    cot_all, gate_all, up_all, down_all = take(4)
    stored = take(10)
    rows_all, ab_all, y_part, dh_part, low = take(5)
    qkv, out_rows, out_columns = take(3)
    y1, beta_rows, conv, first, second, gain, beta_pre = take(7)
    gate_part, up_part, down_part, out_part, qkv_part = take(5)
    near_y, far_y, near_h, far_h = take(4)
    buffers = [take(2) for _ in range(6)]
    small_own, small_all, small, small_part, shared, small_low, small_sums = take(7)
    sems_mp, sems_dp, reduce_sems, dp_sems, share_sems = take(5), take(5), take(4), take(4), take(5)
    rows_send, rows_recv, swap_send, swap_recv, saved_sem, load_sem, feed_sem = take(7)
    conv_row, first_row, second_row, gain_row = rows_of
    own, model = tokens.shape
    length = own * mp
    shard = model // dp
    width = heads * BLOCK
    blocks = length // BLOCK
    lanes = small_own.shape[1]
    feed = gate_own.shape[0] if flip else gate_own.shape[1]
    per = dp // mp
    column = lax.axis_index("mp")
    mine = pl.ds(pl.multiple_of(column * width, BLOCK), width)
    tile, wide_tile = 256, 512
    per_tile = tile // shard
    row, col = iota2(BLOCK)
    scale = BLOCK**-0.5
    group = 4 if blocks % 4 == 0 else 1
    loss_scale = jnp.zeros((1, 1), F32)
    for i in range(domain_weight.shape[0]):
        loss_scale = loss_scale + jnp.where(domain[0] == i, domain_weight[i], 0.0)

    small_own[...] = jnp.zeros_like(small_own)
    line = 0
    for ref in smalls:
        small_own[line : line + ref.shape[0], 0 : ref.shape[1]] = ref[...].astype(F32)
        line += ref.shape[0]

    greet((("dp", dp), ("mp", mp)))
    small_gather = Gather("dp", dp, small_own, leading(small_all), sems_dp, 0)
    places = [lambda d, i=i: qkv.at[d, :, i * width : (i + 1) * width] for i in range(3)]
    *qkv_gathers, out_gather = [
        Gather("dp", dp, src.at[:, mine], place, sems_dp, 1 + i)
        for i, (src, place) in enumerate(zip(projections, [*places, leading(out_columns)]))
    ]
    token_gather = Gather("mp", mp, tokens, leading(rows_all), sems_mp, 0)
    cot_gather = Gather("mp", mp, cot, leading(cot_all), sems_mp, 1)
    feed_gathers = [
        Gather(
            "dp",
            dp,
            src,
            columns_of(dst, lanes) if flip else leading(dst),
            sems_dp,
            5 + i,
        )
        for i, (src, dst) in enumerate(
            ((gate_own, gate_all), (up_own, up_all), (down_own, down_all))
        )
    ]
    small_gather.start()
    for g in qkv_gathers:
        g.start()
    token_gather.start()
    small_gather.forward_all()
    qkv_gathers[0].forward_all()
    token_gather.forward_all()
    for g in qkv_gathers[1:]:
        g.forward_all()
    out_gather.start_outer()
    for g in feed_gathers:
        g.start_outer()
    cot_gather.start()
    small_gather.finish()

    for d in range(dp):
        small[:, d * lanes : (d + 1) * lanes] = small_all[d]
    beta_rows[...] = jnp.zeros_like(beta_rows)
    picked = []
    for head in range(heads):
        wanted = jnp.zeros((1, model), F32)
        for g in range(heads * mp):
            wanted = jnp.where(column * heads + head == g, small[g : g + 1], wanted)
        picked.append(wanted)
    beta_rows[0:16] = jnp.concatenate(
        picked + [jnp.zeros((16 - heads, model), F32)], axis=0
    ).astype(BF16)
    for i in range(3):
        for j in range(taps):
            at = conv_row + i * taps + j
            conv[j : j + 1, i * width : (i + 1) * width] = small[at : at + 1, mine]
    first[...] = small[first_row : first_row + 1]
    second[...] = small[second_row : second_row + 1]
    total = jnp.zeros((8, dp * gains), F32)
    for d in range(dp):
        line = jnp.broadcast_to(small_all[d, gain_row : gain_row + 1], (8, lanes))
        total = total + dot(line.astype(BF16), place_lanes(d, dp, lanes, gains).astype(BF16))
    gain[...] = total[0:1]

    token_gather.finish()
    h2_gather = Gather("mp", mp, low, leading(rows_all), sems_mp, 2)
    ab_gather = Gather("mp", mp, low, leading(ab_all), sems_mp, 3)
    reduce_part = ReduceScatter("mp", mp, leading(y_part), near_y, far_y, reduce_sems, 0)
    reduce_h2 = ReduceScatter("mp", mp, leading(dh_part), near_h, far_h, reduce_sems, 1)
    reduce_y = ReduceScatter("mp", mp, leading(y_part), near_y, far_y, reduce_sems, 2)
    reduce_h = ReduceScatter("mp", mp, leading(dh_part), near_h, far_h, reduce_sems, 3)
    over_dp = [
        ReduceScatter(
            "dp",
            dp,
            columns_of(part, shard) if flip and slot < 3 else leading(part),
            *pair,
            dp_sems,
            slot,
        )
        for slot, (part, pair) in enumerate(
            zip((gate_part, up_part, down_part, out_columns, qkv_part, small_part), buffers)
        )
    ]
    reduce_gate, reduce_up, reduce_down, reduce_out, reduce_qkv, reduce_small = over_dp

    def mixer_forward(
        h, p, inverse, w, scores, step, delta, state, o, m, u, offset, q_all
    ):
        saved = (h, p, inverse, w, scores, step, delta, state, o, m)
        for i in range(mp):
            x = rows_all[i].astype(F32)
            normed = x * lax.rsqrt(jnp.mean(x * x, axis=-1, keepdims=True) + 1e-06) * first[...]
            h[i * own : (i + 1) * own] = normed.astype(BF16)
        for g in qkv_gathers:
            g.finish()
        out_gather.start_beside()
        for g in feed_gathers:
            g.start_beside()

        p[0:8] = jnp.zeros((8, p.shape[1]), F32)
        p[length + 8 :] = jnp.zeros((8, p.shape[1]), F32)
        weight = qkv.reshape(model, 3 * width)

        @pl.loop(0, mp)
        def _(i):
            at = pl.ds(pl.multiple_of(i * own, own), own)
            low = h[at]
            p[pl.ds(pl.multiple_of(i * own + 8, 8), own)] = dot(low, weight[...])
            beta_pre[at] = dot(low, beta_rows[...], tb=True)

        def save(index):
            return pltpu.make_async_copy(saved[index], stored[index], saved_sem.at[index])

        for index in (0, 1):
            save(index).start()


        def prepare(i):
            chains = [(i * group + j, head) for j in range(group) for head in range(heads)]
            starts = [pl.multiple_of(c * BLOCK, BLOCK) for c, _ in chains]
            places = [head * blocks + c for c, head in chains]
            ks, kbs, vbs, qs = [], [], [], []
            for (c, head), start in zip(chains, starts):
                s, _, _ = activated(p, conv, start, 0, head, width, taps)
                qs.append(s * (inverse_norm(s) * scale))
                s, _, _ = activated(p, conv, start, 1, head, width, taps)
                k = s * inverse_norm(s)
                v, _, _ = activated(p, conv, start, 2, head, width, taps)
                beta = sigmoid(beta_pre[pl.ds(start, BLOCK), head : head + 1])
                ks.append(k)
                kbs.append(k * beta)
                vbs.append(v * beta)
            for place, q in zip(places, qs):
                q_all[place] = q
            stricts = each(lambda a, b: jnp.where(row > col, mm(a, b, tb=True), 0.0), kbs, ks)
            for place, a in zip(places, each(lambda q, k: mm(q, k, tb=True), qs, ks)):
                scores[place] = jnp.where(row >= col, a, 0.0)
            xs = unit_lower_inverses(stricts)
            for place, x in zip(places, xs):
                inverse[place] = x
            wus = each(lambda x, a, b: mm(x, jnp.concatenate([a, b], axis=1)), xs, kbs, vbs)
            for place, wu in zip(places, wus):
                w[place] = wu[:, :BLOCK]
                u[place] = wu[:, BLOCK:]
            for place, gb in zip(places, each(lambda k, wu: mm(k, wu, ta=True), ks, wus)):
                step[place] = gb[:, :BLOCK]
                offset[place] = gb[:, BLOCK:]

        def swap(k, block, source):
            columns = pl.ds(pl.multiple_of(source * width, BLOCK), width)
            return pltpu.make_async_remote_copy(
                src_ref=out_columns.at[pl.ds(block * per, per)],
                dst_ref=out_rows.at[:, :, columns],
                send_sem=rows_send.at[k],
                recv_sem=rows_recv.at[k],
                device_id={"mp": (column + k) % mp},
                device_id_type=MESH,
            )

        half = blocks // group // 2
        pl.loop(0, half)(prepare)
        out_gather.forward_all()
        feed_gathers[0].forward(1)
        pl.loop(half, blocks // group)(prepare)
        for index in (2, 3, 4, 5):
            save(index).start()
        for k in range(2, feed_gathers[0].outer):
            feed_gathers[0].forward(k)
        cot_gather.forward_all()
        out_gather.finish()
        for k in range(1, mp):
            swap(k, (column + k) % mp, column).start()
        out_rows[:, :, mine] = out_columns[pl.ds(column * per, per)]

        def advance(c, states):
            places = [head * blocks + c for head in range(heads)]
            for place, s in zip(places, states):
                state[place] = s
            moved = each(lambda place, s: mm(step[place], s), places, states)
            return tuple(each(lambda place, s, t: s - t + offset[place], places, states, moved))

        lax.fori_loop(0, blocks, advance, tuple(jnp.zeros((BLOCK, BLOCK), F32) for _ in range(heads)))
        save(7).start()

        for k in range(1, mp):
            swap(k, column, (column + mp - k) % mp).wait_recv()
        out_weight = out_rows.reshape(width, model)

        def outputs(index):
            per = own // BLOCK
            chains = [(index * per + j, head) for j in range(per) for head in range(heads)]
            places = [head * blocks + c for c, head in chains]
            boths = each(
                lambda at: mm(jnp.concatenate([w[at], q_all[at]], axis=0), state[at]), places
            )
            ds = each(lambda at, both: u[at] - both[:BLOCK], places, boths)
            for place, d in zip(places, ds):
                delta[place] = d
            outs = each(lambda at, d: mm(scores[at], d), places, ds)
            outs = each(lambda both, out: both[BLOCK:] + out, boths, outs)
            for (c, head), out in zip(chains, outs):
                rows = pl.ds(pl.multiple_of(c * BLOCK, BLOCK), BLOCK)
                at = slice(head * BLOCK, (head + 1) * BLOCK)
                o[rows, at] = out
                r = lax.rsqrt(jnp.mean(out * out, axis=-1, keepdims=True) + 1e-05)
                m[rows, at] = (out * r * gain[...]).astype(BF16)
            at = pl.ds(pl.multiple_of(index * own, own), own)
            y_part[index] = dot(m[at], out_weight[...]).astype(BF16)

        for k in [*range(1, reduce_part.outer), 0]:
            outputs(reduce_part.given(k))
            reduce_part.to_beside(k).start()
            outputs(reduce_part.kept(k))
            if k:
                reduce_part.join(k)
        for index in (6, 8, 9):
            save(index).start()
        feed_gathers[1].forward_all()
        y = tokens[...].astype(F32) + reduce_part.finish()
        y1[...] = y
        low[...] = (
            y * lax.rsqrt(jnp.mean(y * y, axis=-1, keepdims=True) + 1e-06) * second[...]
        ).astype(BF16)
        h2_gather.start()
        reduce_part.sent()
        for k in range(1, mp):
            swap(k, (column + k) % mp, column).wait_send()
        for index in range(10):
            save(index).wait()

    square = pltpu.VMEM((heads * blocks, BLOCK, BLOCK), F32)
    mixer_buffers = [
        pltpu.VMEM((length, model), BF16),
        pltpu.VMEM((length + 16, 3 * width), F32),
        *[square] * 6,
        pltpu.VMEM((length, width), F32),
        pltpu.VMEM((length, width), BF16),
    ]
    pl.run_scoped(mixer_forward, *mixer_buffers, square, square, square)

    def feed_forward(gate, up, down, gb, z, dg, du):
        def load(index):
            src, dst = ((gate_all, gate), (up_all, up), (down_all, down), (cot_all, gb))[index]
            return pltpu.make_async_copy(src, dst, feed_sem.at[index])

        gate_w, up_w, down_w = (
            a if flip else a.reshape(model, feed) for a in (gate, up, down)
        )

        def hidden_rows(index):
            at = pl.ds(pl.multiple_of(index * own, own), own)
            x = rows_all[index]
            g = dot(x, gate_w[...], tb=flip)
            u = dot(x, up_w[...], tb=flip)
            sg = sigmoid(g)
            silu = g * sg
            z[at] = (silu * u).astype(BF16)
            dg[at] = (u * (sg + silu * (1.0 - sg))).astype(BF16)
            du[at] = silu.astype(BF16)

        def result_rows(index):
            at = pl.ds(pl.multiple_of(index * own, own), own)
            dz = dot(gb[index], down_w[...], tb=flip)
            dgl = (dz * dg[at].astype(F32)).astype(BF16)
            dul = (dz * du[at].astype(F32)).astype(BF16)
            dg[at] = dgl
            du[at] = dul
            dh_part[index] = (
                dot(dgl, gate_w[...], tb=not flip) + dot(dul, up_w[...], tb=not flip)
            ).astype(BF16)
            y_part[index] = dot(z[at], down_w[...], tb=not flip).astype(BF16)

        def weight_gradient(part, left, right, reduce):
            @pl.loop(0, model // wide_tile)
            def _(i):
                at = pl.ds(pl.multiple_of(i * wide_tile, wide_tile), wide_tile)
                x = left[:, :, at].reshape(length, wide_tile)
                if flip:
                    part[:, at] = dot(right[...], x, ta=True).astype(BF16)
                else:
                    total = dot(x, right[...], ta=True).astype(BF16)
                    count = wide_tile // shard
                    part[pl.ds(i * count, count)] = total.reshape(count, shard, feed)

            reduce.start()

        outer = h2_gather.outer
        cot_gather.finish()
        load(3).start()
        for index in range(2):
            feed_gathers[index].finish()
            load(index).start()
        for index in (3, 0, 1):
            load(index).wait()
        gb[...] = (gb[...].astype(F32) * loss_scale).astype(BF16)
        h2_gather.own().wait()
        hidden_rows(h2_gather.me)
        h2_gather.arrived(0)
        hidden_rows(h2_gather.beside)
        for k in range(1, outer):
            h2_gather.forward(k)
            hidden_rows(h2_gather.source(k))
            h2_gather.arrived(k)
            hidden_rows(h2_gather.source_beside(k))
        feed_gathers[2].forward_all()
        weight_gradient(down_part, gb, z, reduce_down)
        feed_gathers[2].finish()
        load(2).start()
        load(2).wait()
        for k in [*range(1, outer), 0]:
            result_rows(reduce_h2.given(k))
            reduce_h2.to_beside(k).start()
            reduce_y.to_beside(k).start()
            result_rows(reduce_h2.kept(k))
            if k:
                reduce_h2.join(k)
        weight_gradient(gate_part, rows_all, dg, reduce_gate)
        weight_gradient(up_part, rows_all, du, reduce_up)

    weights = pltpu.VMEM((feed, model) if flip else (dp, shard, feed), BF16)
    hidden = pltpu.VMEM((length, feed), BF16)
    pl.run_scoped(
        feed_forward,
        weights,
        weights,
        weights,
        pltpu.VMEM((mp, own, model), BF16),
        hidden,
        hidden,
        hidden,
    )
    h2_gather.sent()

    def mixer(
        h, p, inverse, w, scores, step, delta, state, o, m, ds_all, dp_low, db_low,
    ):
        do, entry, dc = o, w, p
        targets = (h, p, inverse, w, scores, step, delta, state, o, m)

        def load(index):
            return pltpu.make_async_copy(stored[index], targets[index], load_sem.at[index])

        for index in (1, 4, 3, 8, 9, 5, 2, 6, 7, 0):
            load(index).start()

        dh = reduce_h2.finish()
        y = y1[...]
        r = lax.rsqrt(jnp.mean(y * y, axis=-1, keepdims=True) + 1e-06)
        small[...] = jnp.zeros_like(small)
        small[second_row : second_row + 1] = jnp.sum(dh * y * r, axis=0, keepdims=True)
        scaled = second[...] * dh
        grad = (
            cot[...].astype(F32) * loss_scale
            + r * scaled
            - y * (r * r * r * jnp.mean(y * scaled, axis=-1, keepdims=True))
        )
        input_grad[...] = grad
        low[...] = grad.astype(BF16)
        ab_gather.start()
        reduce_h2.sent()

        for index in (1, 4, 3):
            load(index).wait()
        dc[length + 8 :] = jnp.zeros((8, dc.shape[1]), F32)

        def chains_of(i, size):
            chains = [(i * size + j, head) for j in range(size) for head in range(heads)]
            starts = [pl.multiple_of(c * BLOCK, BLOCK) for c, _ in chains]
            places = [head * blocks + c for c, head in chains]
            return chains, starts, places

        def lane(head):
            return slice(head * BLOCK, (head + 1) * BLOCK)

        @pl.loop(0, blocks // group)
        def _(i):
            chains, starts, places = chains_of(i, group)
            moved = each(lambda at: mm(scores[at], w[at]), places)
            for (c, head), start, place, t in zip(chains, starts, places, moved):
                s, _, _ = activated(p, conv, start, 0, head, width, taps)
                ds_all[place] = s * (inverse_norm(s) * scale) - t

        ab_gather.forward_all()
        reduce_y.join_all()
        ab_gather.finish()
        for index in (8, 9, 5):
            load(index).wait()
        out_weight = out_rows.reshape(width, model)
        d_gain = jnp.zeros((1, BLOCK), F32)
        for i in range(mp):
            dm = dot(ab_all[i], out_weight[...], tb=True)
            at = slice(i * own, (i + 1) * own)
            for head in range(heads):
                x = o[at, lane(head)]
                g = dm[:, lane(head)]
                r = lax.rsqrt(jnp.mean(x * x, axis=-1, keepdims=True) + 1e-05)
                d_gain = d_gain + jnp.sum(g * x * r, axis=0, keepdims=True)
                scaled = g * gain[...]
                do[at, lane(head)] = r * scaled - x * (
                    r * r * r * jnp.mean(x * scaled, axis=-1, keepdims=True)
                )
        for d in range(dp):
            moved = mm(
                jnp.broadcast_to(d_gain, (8, BLOCK)), place_lanes(d, dp, lanes, gains), tb=True
            )
            small_part[d, gain_row : gain_row + 1] = moved[0:1]
        @pl.loop(0, mp)
        def _(i):
            x = ab_all[:, :, pl.ds(pl.multiple_of(i * width, BLOCK), width)].reshape(length, width)
            out_part[i] = dot(m[...], x, ta=True).astype(BF16).reshape(per, shard, width)

        def swap(k, block):
            return pltpu.make_async_remote_copy(
                src_ref=out_part.at[block],
                dst_ref=out_columns.at[pl.ds(column * per, per)],
                send_sem=swap_send.at[k],
                recv_sem=swap_recv.at[k],
                device_id={"mp": (column + k) % mp},
                device_id_type=MESH,
            )

        def swap_in(k):
            source = (column + mp - k) % mp
            return pltpu.make_async_remote_copy(
                src_ref=out_part.at[source],
                dst_ref=out_columns.at[pl.ds(source * per, per)],
                send_sem=swap_send.at[k],
                recv_sem=swap_recv.at[k],
                device_id={"mp": (column + k) % mp},
                device_id_type=MESH,
            )

        for k in range(1, mp):
            swap(k, (column + k) % mp).start()
        out_columns[pl.ds(column * per, per)] = out_part[column]

        @pl.loop(0, blocks // group)
        def _(i):
            chains, starts, places = chains_of(i, group)
            grads = [do[pl.ds(start, BLOCK), lane(head)] for (_, head), start in zip(chains, starts)]
            for place, t in zip(places, each(lambda at, g: mm(ds_all[at], g, ta=True), places, grads)):
                entry[place] = t

        def retreat(i, grads):
            places = [head * blocks + blocks - 1 - i for head in range(heads)]
            for place, g in zip(places, grads):
                ds_all[place] = g
            moved = each(lambda at, g: mm(step[at], g, ta=True), places, grads)
            return tuple(each(lambda at, g, t: g - t + entry[at], places, grads, moved))

        lax.fori_loop(
            0, blocks, retreat, tuple(jnp.zeros((BLOCK, BLOCK), F32) for _ in range(heads))
        )
        for index in (2, 6, 7, 0):
            load(index).wait()
        reduce_gate.join_all()
        d_conv = small
        conv_lanes = pl.ds(pl.multiple_of(column * width, BLOCK), width)

        def through(parts, grad, start, part, head):
            s, gate, shifted = parts
            columns = slice(part * width + head * BLOCK, part * width + (head + 1) * BLOCK)
            d_pre = grad * (gate + s * (1.0 - gate))
            dc[pl.ds(pl.multiple_of(start + 8, 8), BLOCK), columns] = d_pre
            at = pl.ds(pl.multiple_of(column * width + head * BLOCK, BLOCK), BLOCK)
            for j in range(taps):
                line = conv_row + part * taps + j
                d_conv[line : line + 1, at] += jnp.sum(d_pre * shifted[j], axis=0, keepdims=True)

        def gradients(i):
            chains, starts, places = chains_of(steps - 1 - i, size)
            qparts, kparts, vparts = (
                [
                    activated(p, conv, start, part, head, width, taps)
                    for (_, head), start in zip(chains, starts)
                ]
                for part in range(3)
            )
            rqs = [inverse_norm(s) for s, _, _ in qparts]
            rks = [inverse_norm(s) for s, _, _ in kparts]
            qs = [part[0] * (r * scale) for part, r in zip(qparts, rqs)]
            ks = [part[0] * r for part, r in zip(kparts, rks)]
            betas = [
                sigmoid(beta_pre[pl.ds(start, BLOCK), head : head + 1])
                for (_, head), start in zip(chains, starts)
            ]
            kbs = each(lambda k, beta: k * beta, ks, betas)
            d_os = [do[pl.ds(start, BLOCK), lane(head)] for (_, head), start in zip(chains, starts)]
            deltas = [delta[at] for at in places]
            s_ins = [state[at] for at in places]
            ds_outs = [ds_all[at] for at in places]
            t1 = each(lambda at, g: mm(scores[at], g, ta=True), places, d_os)
            t2 = each(mm, ks, ds_outs)
            d_scores = each(
                lambda g, d: jnp.where(row >= col, mm(g, d, tb=True), 0.0), d_os, deltas
            )
            dq1 = each(lambda g, s: mm(g, s, tb=True), d_os, s_ins)
            es = each(lambda at, a, b: mm(inverse[at], a + b, ta=True), places, t1, t2)
            dq2 = each(mm, d_scores, ks)
            dk1 = each(lambda a, q: mm(a, q, ta=True), d_scores, qs)
            d_stricts = each(
                lambda e, d: jnp.where(row > col, -mm(e, d, tb=True), 0.0), es, deltas
            )
            dk2 = each(lambda d, s: mm(d, s, tb=True), deltas, ds_outs)
            f2 = each(lambda e, s: mm(e, s, tb=True), es, s_ins)
            f1 = each(mm, d_stricts, ks)
            dk3 = each(lambda a, kb: mm(a, kb, ta=True), d_stricts, kbs)
            fs = each(lambda a, b: a - b, f1, f2)
            dks = each(
                lambda a, b, c, beta, f: a + b + c + beta * f, dk1, dk2, dk3, betas, fs
            )
            rows = {}
            for n, ((c, head), start) in enumerate(zip(chains, starts)):
                beta, e, f = betas[n], es[n], fs[n]
                d_beta = jnp.sum(f * ks[n] + e * vparts[n][0], axis=-1, keepdims=True)
                d_beta = jnp.where(col == head, d_beta * beta * (1.0 - beta), 0.0)
                rows.setdefault(n // heads, []).append(d_beta)
                sq, rq, gq_in = qparts[n][0], rqs[n], (dq1[n] + dq2[n]) * scale
                through(
                    qparts[n],
                    rq * gq_in - sq * (rq * rq * rq * jnp.sum(sq * gq_in, axis=-1, keepdims=True)),
                    start, 0, head,
                )
                sk, rk, dk = kparts[n][0], rks[n], dks[n]
                through(
                    kparts[n],
                    rk * dk - sk * (rk * rk * rk * jnp.sum(sk * dk, axis=-1, keepdims=True)),
                    start, 1, head,
                )
                through(vparts[n], beta * e, start, 2, head)
            for n, parts in rows.items():
                db_low[pl.ds(starts[n * heads], BLOCK)] = sum(parts).astype(BF16)

        size = 2 if blocks % 4 == 0 else 1
        steps = blocks // size
        pl.loop(0, steps // 2)(gradients)
        reduce_up.join_all()
        for k in range(1, mp):
            swap_in(k).wait_recv()
        reduce_out.start()
        pl.loop(steps // 2, steps)(gradients)

        @pl.loop(0, blocks)
        def _(c):
            start = pl.multiple_of(c * BLOCK, BLOCK)
            window = dc[pl.ds(pl.multiple_of(start + 8, 8), BLOCK + 8)]
            total = conv[taps - 1 : taps] * window[0:BLOCK]
            for j in range(taps - 1):
                ahead = taps - 1 - j
                total = total + conv[j : j + 1] * window[ahead : ahead + BLOCK]
            dp_low[pl.ds(start, BLOCK)] = total.astype(BF16)

        @pl.loop(0, model // tile)
        def _(i):
            x = h[:, pl.ds(pl.multiple_of(i * tile, tile), tile)]
            total = dot(x, dp_low[...], ta=True).astype(BF16)
            qkv_part[pl.ds(i * per_tile, per_tile)] = total.reshape(per_tile, shard, 3 * width)

        reduce_qkv.start()
        reduce_down.join_all()
        weight = qkv.reshape(model, 3 * width)

        def rows(index):
            at = pl.ds(pl.multiple_of(index * own, own), own)
            dh_part[index] = (
                dot(dp_low[at], weight[...], tb=True) + dot(db_low[at], beta_rows[...])
            ).astype(BF16)

        for k in [*range(1, reduce_h.outer), 0]:
            rows(reduce_h.given(k))
            reduce_h.to_beside(k).start()
            rows(reduce_h.kept(k))
            if k:
                reduce_h.join(k)
        d_beta = dot(db_low[...], h[...], ta=True)
        for g in range(heads * mp):
            line = d_beta[g % heads : g % heads + 1]
            small[g : g + 1] = jnp.where(column == g // heads, line, 0.0)
        for k in range(1, mp):
            swap(k, (column + k) % mp).wait_send()

    pl.run_scoped(
        mixer,
        *mixer_buffers,
        square,
        pltpu.VMEM((length, 3 * width), BF16),
        pltpu.VMEM((length, BLOCK), BF16),
    )
    reduce_out.join_all()
    for reduce, result in ((reduce_gate, d_gate), (reduce_up, d_up), (reduce_down, d_down)):
        result[...] = reduce.finish()
    output[...] = (y1[...] + reduce_y.finish()).astype(BF16)
    reduce_qkv.join_all()
    dh = reduce_h.finish()
    x = tokens[...].astype(F32)
    s = lax.rsqrt(jnp.mean(x * x, axis=-1, keepdims=True) + 1e-06)
    small[first_row : first_row + 1] = jnp.sum(dh * x * s, axis=0, keepdims=True)
    for d in range(dp):
        small_part[d, 0:gain_row] = small[0:gain_row, d * lanes : (d + 1) * lanes]
        small_part[d, gain_row + 1 :] = jnp.zeros((small_part.shape[1] - gain_row - 1, lanes), F32)
    reduce_small.start()
    scaled = first[...] * dh
    input_grad[...] += s * scaled - x * (
        s * s * s * jnp.mean(x * scaled, axis=-1, keepdims=True)
    )
    reduce_small.join_all()
    shared[:, 3 * width :] = reduce_out.finish().astype(BF16)
    small_low[...] = reduce_small.finish()
    narrow = Gather("mp", mp, small_low, leading(small_sums), share_sems, 1)
    narrow.start()
    shared[:, : 3 * width] = reduce_qkv.finish().astype(BF16)
    wide = Gather("mp", mp, shared, leading(shared_all), share_sems, 0)
    wide.start()
    narrow.forward_all()
    wide.forward_all()
    narrow.finish()
    small_total = small_sums[0]
    for i in range(1, mp):
        small_total = small_total + small_sums[i]
    d_small[...] = small_total
    wide.finish()
    ab_gather_done = (reduce_y, reduce_h, *over_dp)
    for reduce in ab_gather_done:
        reduce.sent()


def finish_kernel(mp, heads, taps, gains, rows_of, *refs):
    take = Taker(refs)
    output_in, input_grad_in, shared, small, gate_in, up_in, down_in = take(7)
    output, input_grad = take(2)
    models, smalls, feeds = take(4), take(7), take(3)
    width = heads * BLOCK
    output[...] = output_in[...]
    input_grad[...] = input_grad_in[...]
    for i in range(mp):
        at = slice(i * width, (i + 1) * width)
        for index, result in enumerate(models):
            result[:, at] = shared[i, :, index * width : (index + 1) * width].astype(F32)
    line = 0
    for ref in smalls:
        ref[...] = small[line : line + ref.shape[0], 0 : ref.shape[1]]
        line += ref.shape[0]
    for src, dst in zip((gate_in, up_in, down_in), feeds):
        dst[...] = src[...]


def call(kernel, ins, outs, scratch, collective, name, limit):
    return pl.pallas_call(
        kernel,
        out_shape=[jax.ShapeDtypeStruct(shape, kind) for _, shape, kind in outs],
        in_specs=[spec for spec, _ in ins],
        out_specs=[spec for spec, _, _ in outs],
        scratch_shapes=list(scratch),
        compiler_params=pltpu.CompilerParams(
            collective_id=collective,
            has_side_effects=collective is not None,
            vmem_limit_bytes=limit * MIB,
        ),
        name=name,
    )(*[array for _, array in ins])


def shards(
    dp,
    mp,
    tokens,
    cotangent,
    domain,
    domain_weight,
    query_weight,
    key_weight,
    value_weight,
    beta_weight,
    conv_query,
    conv_key,
    conv_value,
    out_gain,
    out_weight,
    norm_first,
    norm_second,
    gate_weight,
    up_weight,
    down_weight,
):
    own, model = tokens.shape
    length = own * mp
    shard = query_weight.shape[0]
    taps = conv_query.shape[0]
    all_heads = beta_weight.shape[1]
    heads = all_heads // mp
    width = model // mp
    feed = gate_weight.shape[1]
    lanes = norm_first.shape[0]
    gains = out_gain.shape[0]
    conv_row, gain_row = all_heads, all_heads + 3 * taps + 2
    first_row, second_row = gain_row - 2, gain_row - 1
    small_rows = -(-(gain_row + 1) // 8) * 8
    rows_of = (conv_row, first_row, second_row, gain_row)
    flip = lanes % 128 == 0

    square = ((heads * (length // BLOCK), BLOCK, BLOCK), F32)
    stored = [
        ((length, model), BF16),
        ((length + 16, 3 * width), F32),
        *[square] * 6,
        ((length, width), F32),
        ((length, width), BF16),
    ]
    feed_shape = (feed, model) if flip else (dp, shard, feed)
    feed_block = (feed, shard) if flip else (shard, feed)
    feed_grad = (VM, feed_block, F32)
    feed_own = (
        (gate_weight.T, up_weight.T, down_weight) if flip else (gate_weight, up_weight, down_weight.T)
    )
    token_rows = ((mp, own, model), BF16)
    sizes = (feed_block,) * 3 + ((shard, width), (shard, 3 * width))
    results = call(
        partial(block_kernel, dp, mp, taps, heads, gains, flip, rows_of),
        [
            (SM, domain), (SM, domain_weight),
            (VM, tokens), (VM, cotangent), (ANY, query_weight), (ANY, key_weight), (ANY, value_weight),
            (ANY, out_weight),
            (VM, beta_weight.T), (VM, conv_query), (VM, conv_key), (VM, conv_value),
            (VM, norm_first[None]), (VM, norm_second[None]), (VM, out_gain[None]),
            *[(ANY, a) for a in feed_own],
        ],
        [
            (VM, (own, model), BF16),
            (VM, (own, model), F32),
            (VM, (mp, shard, 4 * width), BF16),
            (VM, (small_rows, lanes), F32),
            *[feed_grad] * 3,
            (ANY, *token_rows), *[(ANY, feed_shape, BF16)] * 3,
            *[(ANY, *kind) for kind in stored],
        ],
        [pltpu.VMEM(*token_rows)] * 4
        + [
            pltpu.VMEM((own, model), BF16),
            pltpu.VMEM((dp, shard, 3 * width), BF16),
            pltpu.VMEM((dp // mp, shard, model), BF16),
            pltpu.VMEM((dp, shard, width), BF16),
            pltpu.VMEM((own, model), F32),
            pltpu.VMEM((BLOCK, model), BF16),
            pltpu.VMEM((taps, 3 * width), F32),
            pltpu.VMEM((1, model), F32),
            pltpu.VMEM((1, model), F32),
            pltpu.VMEM((1, BLOCK), F32),
            pltpu.VMEM((length, BLOCK), F32),
        ]
        + [pltpu.VMEM(feed_shape, BF16)] * 3
        + [
            pltpu.VMEM((mp, dp // mp, shard, width), BF16),
            pltpu.VMEM((dp, shard, 3 * width), BF16),
        ]
        + ReduceScatter.buffers(mp, own, model) * 2
        + [b for size in sizes for b in ReduceScatter.buffers(dp, *size)]
        + ReduceScatter.buffers(dp, small_rows, lanes, F32)
        + [
            pltpu.VMEM((small_rows, lanes), F32),
            pltpu.VMEM((dp, small_rows, lanes), F32),
            pltpu.VMEM((small_rows, model), F32),
            pltpu.VMEM((dp, small_rows, lanes), F32),
            pltpu.VMEM((shard, 4 * width), BF16),
            pltpu.VMEM((small_rows, lanes), F32),
            pltpu.VMEM((mp, small_rows, lanes), F32),
        ]
        + Gather.scratch(mp, 4)
        + Gather.scratch(dp, 8)
        + ReduceScatter.scratch(mp, 4)
        + ReduceScatter.scratch(dp, 6)
        + Gather.scratch(mp, 2)
        + [pltpu.SemaphoreType.DMA((mp,))] * 4
        + [
            pltpu.SemaphoreType.DMA((10,)),
            pltpu.SemaphoreType.DMA((10,)),
            pltpu.SemaphoreType.DMA((4,)),
        ],
        0,
        "block",
        63,
    )
    back = results[:7]

    small_shapes = [(all_heads, lanes)] + [(taps, lanes)] * 3 + [(1, lanes)] * 2 + [(1, gains)]
    results = call(
        partial(finish_kernel, mp, heads, taps, gains, rows_of),
        [(VM, a) for a in back],
        [
            (VM, (own, model), BF16),
            (VM, (own, model), F32),
            *[(VM, (shard, model), F32)] * 4,
            *[(VM, shape, F32) for shape in small_shapes],
            *[feed_grad] * 3,
        ],
        [],
        None,
        "finish",
        32,
    )
    output, input_grad, d_query, d_key, d_value, d_outw = results[:6]
    d_beta, d_conv_q, d_conv_k, d_conv_v, d_first, d_second, d_gain = results[6:13]
    d_gate, d_up, d_down = results[13:]
    if flip:
        d_gate, d_up = d_gate.T, d_up.T
    else:
        d_down = d_down.T
    return (
        output,
        input_grad,
        d_query,
        d_key,
        d_value,
        d_beta.T,
        d_conv_q,
        d_conv_k,
        d_conv_v,
        d_gain[0],
        d_outw,
        d_first[0],
        d_second[0],
        d_gate,
        d_up,
        d_down,
    )


def solution(mesh):
    dp, mp = mesh.shape["dp"], mesh.shape["mp"]
    weight = P("dp", None)
    split = P(None, "dp")
    rows = P(("dp", "mp"), None)
    return jax.shard_map(
        partial(shards, dp, mp),
        mesh=mesh,
        in_specs=(
            rows, rows, P("dp"), P(), weight, weight, weight, weight, split, split, split,
            P("dp"), weight, P("dp"), P("dp"), P("dp", "mp"), P("dp", "mp"), P("mp", "dp"),
        ),
        out_specs=(
            rows, rows, weight, weight, weight, weight, split, split, split,
            P("dp"), weight, P("dp"), P("dp"), P("dp", "mp"), P("dp", "mp"), P("mp", "dp"),
        ),
        check_vma=False,
    )
```

```python
from functools import partial

import jax
import jax.numpy as jnp
from jax import lax
from jax.experimental import pallas as pl
from jax.experimental.pallas import tpu as pltpu
from jax.sharding import PartitionSpec as P

BLOCK = 128
MESH = pl.DeviceIdType.MESH
F32 = jnp.float32
BF16 = jnp.bfloat16
MIB = 1 << 20
VM = pl.BlockSpec(memory_space=pltpu.VMEM)
ANY = pl.BlockSpec(memory_space=pl.ANY)
SM = pl.BlockSpec(memory_space=pltpu.SMEM)


def dot(a, b, ta=False, tb=False):
    dims = (((0 if ta else 1,), (1 if tb else 0,)), ((), ()))
    return lax.dot_general(a, b, dims, preferred_element_type=F32)


def halves(a):
    high = a.astype(BF16)
    return high, (a - high.astype(F32)).astype(BF16)


def mm(a, b, ta=False, tb=False):
    ah, al = halves(a)
    bh, bl = halves(b)
    da, db = 0 if ta else 1, 1 if tb else 0
    left = jnp.concatenate([ah, al], axis=da)
    right = jnp.concatenate([bh, bh], axis=db)
    columns = b.shape[1 - db]
    if columns > BLOCK:
        return dot(left, right, ta, tb) + dot(ah, bl, ta, tb)
    rest = jnp.concatenate([bl, jnp.zeros_like(bl)], axis=db)
    both = dot(left, jnp.concatenate([right, rest], axis=1 - db), ta, tb)
    return both[:, :columns] + both[:, columns:]


def each(function, *lists):
    return [function(*items) for items in zip(*lists)]


def iota2(size):
    return (
        lax.broadcasted_iota(jnp.int32, (size, size), 0),
        lax.broadcasted_iota(jnp.int32, (size, size), 1),
    )


def unit_lower_inverses(stricts):
    size = stricts[0].shape[0]
    row, col = iota2(size)
    pairs = (row >> 1) == (col >> 1)
    unit = jnp.where(row == col, 1.0, 0.0)
    inverses = each(lambda a: unit - jnp.where(pairs, a, 0.0), stricts)
    shift = 1
    while (1 << shift) < size:
        inside = (row >> (shift + 1)) == (col >> (shift + 1))
        apart = (row >> shift) != (col >> shift)
        corner = inside & apart
        moved = each(lambda x, a: mm(x, jnp.where(corner, a, 0.0)), inverses, stricts)
        moved = each(mm, moved, inverses)
        inverses = each(lambda x, t: x - t, inverses, moved)
        shift += 1
    return inverses


def sigmoid(a):
    return 1.0 / (1.0 + jnp.exp(-a))


class Gather:
    def __init__(self, axis, count, src, place, sems, slot):
        self.axis, self.src, self.place = axis, src, place
        self.outer = count // 2
        self.me = lax.axis_index(axis)
        self.a, self.b = self.me // 2, self.me % 2
        self.sa, self.ra, self.sb, self.rb, self.local = (s.at[slot] for s in sems)
        self.beside = self.a * 2 + 1 - self.b

    @staticmethod
    def scratch(count, slots):
        return [pltpu.SemaphoreType.DMA((slots, count // 2))] * 4 + [
            pltpu.SemaphoreType.DMA((slots, 1))
        ]

    def copy(self, src, block, send, recv, target):
        return pltpu.make_async_remote_copy(
            src_ref=src,
            dst_ref=self.place(block),
            send_sem=send,
            recv_sem=recv,
            device_id={self.axis: target},
            device_id_type=MESH,
        )

    def own(self):
        return pltpu.make_async_copy(self.src, self.place(self.me), self.local.at[0])

    def source(self, k):
        return (self.a + self.outer - k) % self.outer * 2 + self.b

    def source_beside(self, k):
        return (self.a + self.outer - k) % self.outer * 2 + 1 - self.b

    def to_outer(self, k):
        target = (self.a + k) % self.outer * 2 + self.b
        return self.copy(self.src, self.me, self.sa.at[k], self.ra.at[k], target)

    def to_beside(self, k):
        block = self.source(k)
        src = self.src if k == 0 else self.place(block)
        return self.copy(src, block, self.sb.at[k], self.rb.at[k], self.beside)

    def start_outer(self):
        for k in range(1, self.outer):
            self.to_outer(k).start()

    def start_beside(self):
        self.to_beside(0).start()
        self.own().start()

    def start(self):
        self.start_outer()
        self.start_beside()

    def forward(self, k):
        self.to_outer(k).wait_recv()
        self.to_beside(k).start()

    def forward_all(self):
        for k in range(1, self.outer):
            self.forward(k)

    def arrived(self, k):
        self.to_beside(k).wait_recv()

    def sent(self):
        for k in range(self.outer):
            if k:
                self.to_outer(k).wait_send()
            self.to_beside(k).wait_send()

    def finish(self):
        self.own().wait()
        for k in range(self.outer):
            self.arrived(k)
        self.sent()


class ReduceScatter:
    def __init__(self, axis, count, place, near, far, sems, slot):
        self.axis, self.place, self.near, self.far = axis, place, near, far
        self.outer = count // 2
        self.me = lax.axis_index(axis)
        self.a, self.b = self.me // 2, self.me % 2
        self.sa, self.ra, self.sb, self.rb = (s.at[slot] for s in sems)
        self.beside = self.a * 2 + 1 - self.b

    @staticmethod
    def scratch(count, slots):
        return [pltpu.SemaphoreType.DMA((slots, count // 2))] * 4

    @staticmethod
    def buffers(count, rows, columns, kind=BF16):
        return [pltpu.VMEM((count // 2, rows, columns), kind)] * 2

    def target(self, k):
        return (self.a + k) % self.outer

    def kept(self, k):
        return self.target(k) * 2 + self.b

    def given(self, k):
        return self.target(k) * 2 + 1 - self.b

    def to_beside(self, k):
        return pltpu.make_async_remote_copy(
            src_ref=self.place(self.given(k)),
            dst_ref=self.near.at[k],
            send_sem=self.sb.at[k],
            recv_sem=self.rb.at[k],
            device_id={self.axis: self.beside},
            device_id_type=MESH,
        )

    def to_outer(self, k):
        return pltpu.make_async_remote_copy(
            src_ref=self.place(self.kept(k)),
            dst_ref=self.far.at[k],
            send_sem=self.sa.at[k],
            recv_sem=self.ra.at[k],
            device_id={self.axis: self.target(k) * 2 + self.b},
            device_id_type=MESH,
        )

    def start(self):
        for k in [*range(1, self.outer), 0]:
            self.to_beside(k).start()

    def join(self, k):
        self.to_beside(k).wait_recv()
        block = self.place(self.kept(k))
        total = block[...].astype(F32) + self.near[k].astype(F32)
        if k == 0:
            return total
        block[...] = total.astype(block.dtype)
        self.to_outer(k).start()

    def join_all(self):
        for k in range(1, self.outer):
            self.join(k)

    def finish(self):
        total = self.join(0)
        for k in range(1, self.outer):
            self.to_outer(k).wait_recv()
            total = total + self.far[k].astype(F32)
        return total

    def sent(self):
        for k in range(self.outer):
            self.to_beside(k).wait_send()
            if k:
                self.to_outer(k).wait_send()


def leading(ref):
    return lambda i: ref.at[i]


def columns_of(ref, size):
    return lambda i: ref.at[:, pl.ds(pl.multiple_of(i * size, size), size)]


def greet(counts):
    barrier = pltpu.get_barrier_semaphore()
    for axis, count in counts:
        me = lax.axis_index(axis)
        for k in range(1, count):
            pl.semaphore_signal(
                barrier, inc=1, device_id={axis: (me + k) % count}, device_id_type=MESH
            )
    pl.semaphore_wait(barrier, sum(count - 1 for _, count in counts))


class Taker:
    def __init__(self, refs):
        self.refs, self.cursor = refs, 0

    def __call__(self, count):
        self.cursor += count
        return self.refs[self.cursor - count : self.cursor]

    def one(self):
        return self(1)[0]


def activated(p, conv, start, part, head, width, taps):
    columns = slice(part * width + head * BLOCK, part * width + (head + 1) * BLOCK)
    window = p[pl.ds(start, BLOCK + 8), columns]
    shifted = [window[8 - taps + 1 + j : 8 - taps + 1 + j + BLOCK] for j in range(taps)]
    pre = conv[0:1, columns] * shifted[0]
    for j in range(1, taps):
        pre = pre + conv[j : j + 1, columns] * shifted[j]
    gate = sigmoid(pre)
    return pre * gate, gate, shifted


def inverse_norm(s):
    return lax.rsqrt(jnp.sum(s * s, axis=-1, keepdims=True) + 1e-06)


def place_lanes(index, count, lanes, gains):
    row = lax.broadcasted_iota(jnp.int32, (lanes, count * gains), 0)
    col = lax.broadcasted_iota(jnp.int32, (lanes, count * gains), 1)
    return jnp.where((col == row + index * gains) & (row < gains), 1.0, 0.0)


def block_kernel(dp, mp, taps, heads, gains, flip, rows_of, *refs):
    take = Taker(refs)
    domain, domain_weight = take(2)
    tokens, cot = take(2)
    projections, smalls = take(4), take(7)
    gate_own, up_own, down_own = take(3)
    output, input_grad, shared_all, d_small, d_gate, d_up, d_down = take(7)
    cot_all, gate_all, up_all, down_all = take(4)
    stored = take(10)
    rows_all, ab_all, y_part, dh_part, low = take(5)
    qkv, out_rows, out_columns = take(3)
    y1, beta_rows, conv, first, second, gain, beta_pre = take(7)
    gate_part, up_part, down_part, out_part, qkv_part = take(5)
    near_y, far_y, near_h, far_h = take(4)
    buffers = [take(2) for _ in range(6)]
    small_own, small_all, small, small_part, shared, small_low, small_sums = take(7)
    sems_mp, sems_dp, reduce_sems, dp_sems, share_sems = take(5), take(5), take(4), take(4), take(5)
    rows_send, rows_recv, swap_send, swap_recv, saved_sem, load_sem, feed_sem = take(7)
    conv_row, first_row, second_row, gain_row = rows_of
    own, model = tokens.shape
    length = own * mp
    shard = model // dp
    width = heads * BLOCK
    blocks = length // BLOCK
    lanes = small_own.shape[1]
    feed = gate_own.shape[0] if flip else gate_own.shape[1]
    per = dp // mp
    column = lax.axis_index("mp")
    mine = pl.ds(pl.multiple_of(column * width, BLOCK), width)
    tile, wide_tile = 256, 512
    row, col = iota2(BLOCK)
    scale = BLOCK**-0.5
    group = 4 if blocks % 4 == 0 else 1
    loss_scale = jnp.zeros((1, 1), F32)
    for i in range(domain_weight.shape[0]):
        loss_scale = loss_scale + jnp.where(domain[0] == i, domain_weight[i], 0.0)

    small_own[...] = jnp.zeros_like(small_own)
    line = 0
    for ref in smalls:
        small_own[line : line + ref.shape[0], 0 : ref.shape[1]] = ref[...].astype(F32)
        line += ref.shape[0]

    greet((("dp", dp), ("mp", mp)))
    small_gather = Gather("dp", dp, small_own, leading(small_all), sems_dp, 0)
    places = [lambda d, i=i: qkv.at[d, :, i * width : (i + 1) * width] for i in range(3)]
    *qkv_gathers, out_gather = [
        Gather("dp", dp, src.at[:, mine], place, sems_dp, 1 + i)
        for i, (src, place) in enumerate(zip(projections, [*places, leading(out_columns)]))
    ]
    token_gather = Gather("mp", mp, tokens, leading(rows_all), sems_mp, 0)
    cot_gather = Gather("mp", mp, cot, leading(cot_all), sems_mp, 1)
    feed_gathers = [
        Gather(
            "dp",
            dp,
            src,
            columns_of(dst, lanes) if flip else leading(dst),
            sems_dp,
            5 + i,
        )
        for i, (src, dst) in enumerate(
            ((gate_own, gate_all), (up_own, up_all), (down_own, down_all))
        )
    ]
    small_gather.start()
    for g in qkv_gathers:
        g.start()
    token_gather.start()
    small_gather.forward_all()
    qkv_gathers[0].forward_all()
    token_gather.forward_all()
    for g in qkv_gathers[1:]:
        g.forward_all()
    out_gather.start_outer()
    for g in feed_gathers:
        g.start_outer()
    cot_gather.start()
    small_gather.finish()

    for d in range(dp):
        small[:, d * lanes : (d + 1) * lanes] = small_all[d]
    beta_rows[...] = jnp.zeros_like(beta_rows)
    picked = []
    for head in range(heads):
        wanted = jnp.zeros((1, model), F32)
        for g in range(heads * mp):
            wanted = jnp.where(column * heads + head == g, small[g : g + 1], wanted)
        picked.append(wanted)
    beta_rows[0:16] = jnp.concatenate(
        picked + [jnp.zeros((16 - heads, model), F32)], axis=0
    ).astype(BF16)
    for i in range(3):
        for j in range(taps):
            at = conv_row + i * taps + j
            conv[j : j + 1, i * width : (i + 1) * width] = small[at : at + 1, mine]
    first[...] = small[first_row : first_row + 1]
    second[...] = small[second_row : second_row + 1]
    total = jnp.zeros((8, dp * gains), F32)
    for d in range(dp):
        line = jnp.broadcast_to(small_all[d, gain_row : gain_row + 1], (8, lanes))
        total = total + dot(line.astype(BF16), place_lanes(d, dp, lanes, gains).astype(BF16))
    gain[...] = total[0:1]

    token_gather.finish()
    h2_gather = Gather("mp", mp, low, leading(rows_all), sems_mp, 2)
    ab_gather = Gather("mp", mp, low, leading(ab_all), sems_mp, 3)
    reduce_part = ReduceScatter("mp", mp, leading(y_part), near_y, far_y, reduce_sems, 0)
    reduce_h2 = ReduceScatter("mp", mp, leading(dh_part), near_h, far_h, reduce_sems, 1)
    reduce_y = ReduceScatter("mp", mp, leading(y_part), near_y, far_y, reduce_sems, 2)
    reduce_h = ReduceScatter("mp", mp, leading(dh_part), near_h, far_h, reduce_sems, 3)
    over_dp = [
        ReduceScatter(
            "dp",
            dp,
            columns_of(part, shard) if flip and slot < 3 else leading(part),
            *pair,
            dp_sems,
            slot,
        )
        for slot, (part, pair) in enumerate(
            zip((gate_part, up_part, down_part, out_columns, qkv_part, small_part), buffers)
        )
    ]
    reduce_gate, reduce_up, reduce_down, reduce_out, reduce_qkv, reduce_small = over_dp

    def mixer_forward(
        h, p, inverse, w, scores, step, delta, state, o, m, u, offset, q_all
    ):
        saved = (h, p, inverse, w, scores, step, delta, state, o, m)
        for i in range(mp):
            x = rows_all[i].astype(F32)
            normed = x * lax.rsqrt(jnp.mean(x * x, axis=-1, keepdims=True) + 1e-06) * first[...]
            h[i * own : (i + 1) * own] = normed.astype(BF16)
        for g in qkv_gathers:
            g.finish()
        out_gather.start_beside()
        for g in feed_gathers:
            g.start_beside()

        p[0:8] = jnp.zeros((8, p.shape[1]), F32)
        p[length + 8 :] = jnp.zeros((8, p.shape[1]), F32)
        weight = qkv.reshape(model, 3 * width)

        @pl.loop(0, mp)
        def _(i):
            at = pl.ds(pl.multiple_of(i * own, own), own)
            low = h[at]
            p[pl.ds(pl.multiple_of(i * own + 8, 8), own)] = dot(low, weight[...])
            beta_pre[at] = dot(low, beta_rows[...], tb=True)

        def save(index):
            return pltpu.make_async_copy(saved[index], stored[index], saved_sem.at[index])

        for index in (0, 1):
            save(index).start()


        def prepare(i):
            chains = [(i * group + j, head) for j in range(group) for head in range(heads)]
            starts = [pl.multiple_of(c * BLOCK, BLOCK) for c, _ in chains]
            places = [head * blocks + c for c, head in chains]
            ks, kbs, vbs, qs = [], [], [], []
            for (c, head), start in zip(chains, starts):
                s, _, _ = activated(p, conv, start, 0, head, width, taps)
                qs.append(s * (inverse_norm(s) * scale))
                s, _, _ = activated(p, conv, start, 1, head, width, taps)
                k = s * inverse_norm(s)
                v, _, _ = activated(p, conv, start, 2, head, width, taps)
                beta = sigmoid(beta_pre[pl.ds(start, BLOCK), head : head + 1])
                ks.append(k)
                kbs.append(k * beta)
                vbs.append(v * beta)
            for place, q in zip(places, qs):
                q_all[place] = q
            stricts = each(lambda a, b: jnp.where(row > col, mm(a, b, tb=True), 0.0), kbs, ks)
            for place, a in zip(places, each(lambda q, k: mm(q, k, tb=True), qs, ks)):
                scores[place] = jnp.where(row >= col, a, 0.0)
            xs = unit_lower_inverses(stricts)
            for place, x in zip(places, xs):
                inverse[place] = x
            wus = each(lambda x, a, b: mm(x, jnp.concatenate([a, b], axis=1)), xs, kbs, vbs)
            for place, wu in zip(places, wus):
                w[place] = wu[:, :BLOCK]
                u[place] = wu[:, BLOCK:]
            for place, gb in zip(places, each(lambda k, wu: mm(k, wu, ta=True), ks, wus)):
                step[place] = gb[:, :BLOCK]
                offset[place] = gb[:, BLOCK:]

        def swap(k, block, source):
            columns = pl.ds(pl.multiple_of(source * width, BLOCK), width)
            return pltpu.make_async_remote_copy(
                src_ref=out_columns.at[pl.ds(block * per, per)],
                dst_ref=out_rows.at[:, :, columns],
                send_sem=rows_send.at[k],
                recv_sem=rows_recv.at[k],
                device_id={"mp": (column + k) % mp},
                device_id_type=MESH,
            )

        half = blocks // group // 2
        pl.loop(0, half)(prepare)
        out_gather.forward_all()
        feed_gathers[0].forward(1)
        pl.loop(half, blocks // group)(prepare)
        for index in (2, 3, 4, 5):
            save(index).start()
        for k in range(2, feed_gathers[0].outer):
            feed_gathers[0].forward(k)
        cot_gather.forward_all()
        out_gather.finish()
        for k in range(1, mp):
            swap(k, (column + k) % mp, column).start()
        out_rows[:, :, mine] = out_columns[pl.ds(column * per, per)]

        def advance(c, states):
            places = [head * blocks + c for head in range(heads)]
            for place, s in zip(places, states):
                state[place] = s
            moved = each(lambda place, s: mm(step[place], s), places, states)
            return tuple(each(lambda place, s, t: s - t + offset[place], places, states, moved))

        states = tuple(jnp.zeros((BLOCK, BLOCK), F32) for _ in range(heads))
        for c in range(blocks):
            states = advance(c, states)
        save(7).start()

        for k in range(1, mp):
            swap(k, column, (column + mp - k) % mp).wait_recv()
        out_weight = out_rows.reshape(width, model)

        def outputs(index):
            per = own // BLOCK
            chains = [(index * per + j, head) for j in range(per) for head in range(heads)]
            places = [head * blocks + c for c, head in chains]
            boths = each(
                lambda at: mm(jnp.concatenate([w[at], q_all[at]], axis=0), state[at]), places
            )
            ds = each(lambda at, both: u[at] - both[:BLOCK], places, boths)
            for place, d in zip(places, ds):
                delta[place] = d
            outs = each(lambda at, d: mm(scores[at], d), places, ds)
            outs = each(lambda both, out: both[BLOCK:] + out, boths, outs)
            for (c, head), out in zip(chains, outs):
                rows = pl.ds(pl.multiple_of(c * BLOCK, BLOCK), BLOCK)
                at = slice(head * BLOCK, (head + 1) * BLOCK)
                o[rows, at] = out
                r = lax.rsqrt(jnp.mean(out * out, axis=-1, keepdims=True) + 1e-05)
                m[rows, at] = (out * r * gain[...]).astype(BF16)
            at = pl.ds(pl.multiple_of(index * own, own), own)
            y_part[index] = dot(m[at], out_weight[...]).astype(BF16)

        for k in [*range(1, reduce_part.outer), 0]:
            outputs(reduce_part.given(k))
            reduce_part.to_beside(k).start()
            outputs(reduce_part.kept(k))
            if k:
                reduce_part.join(k)
        for index in (6, 8, 9):
            save(index).start()
        feed_gathers[1].forward_all()
        y = tokens[...].astype(F32) + reduce_part.finish()
        y1[...] = y
        low[...] = (
            y * lax.rsqrt(jnp.mean(y * y, axis=-1, keepdims=True) + 1e-06) * second[...]
        ).astype(BF16)
        h2_gather.start()
        feed_gathers[2].forward_all()
        reduce_part.sent()
        for k in range(1, mp):
            swap(k, (column + k) % mp, column).wait_send()
        for index in range(10):
            save(index).wait()

    square = pltpu.VMEM((heads * blocks, BLOCK, BLOCK), F32)
    mixer_buffers = [
        pltpu.VMEM((length, model), BF16),
        pltpu.VMEM((length + 16, 3 * width), F32),
        *[square] * 6,
        pltpu.VMEM((length, width), F32),
        pltpu.VMEM((length, width), BF16),
    ]
    pl.run_scoped(mixer_forward, *mixer_buffers, square, square, square)

    def feed_forward(gate, up, down, gb, z, dg, du):
        def load(index):
            src, dst = ((gate_all, gate), (up_all, up), (down_all, down), (cot_all, gb))[index]
            return pltpu.make_async_copy(src, dst, feed_sem.at[index])

        gate_w, up_w, down_w = (
            a if flip else a.reshape(model, feed) for a in (gate, up, down)
        )

        def hidden_rows(index):
            at = pl.ds(pl.multiple_of(index * own, own), own)
            x = rows_all[index]
            g = dot(x, gate_w[...], tb=flip)
            u = dot(x, up_w[...], tb=flip)
            sg = sigmoid(g)
            silu = g * sg
            z[at] = (silu * u).astype(BF16)
            dg[at] = (u * (sg + silu * (1.0 - sg))).astype(BF16)
            du[at] = silu.astype(BF16)

        def result_rows(index):
            at = pl.ds(pl.multiple_of(index * own, own), own)
            dz = dot(gb[index], down_w[...], tb=flip)
            dgl = (dz * dg[at].astype(F32)).astype(BF16)
            dul = (dz * du[at].astype(F32)).astype(BF16)
            dg[at] = dgl
            du[at] = dul
            dh_part[index] = (
                dot(dgl, gate_w[...], tb=not flip) + dot(dul, up_w[...], tb=not flip)
            ).astype(BF16)
            y_part[index] = dot(z[at], down_w[...], tb=not flip).astype(BF16)

        def weight_gradient(part, left, right, reduce):
            @pl.loop(0, model // wide_tile)
            def _(i):
                at = pl.ds(pl.multiple_of(i * wide_tile, wide_tile), wide_tile)
                x = left[:, :, at].reshape(length, wide_tile)
                if flip:
                    part[:, at] = dot(right[...], x, ta=True).astype(BF16)
                else:
                    total = dot(x, right[...], ta=True).astype(BF16)
                    count = wide_tile // shard
                    part[pl.ds(i * count, count)] = total.reshape(count, shard, feed)

            reduce.start()

        outer = h2_gather.outer
        cot_gather.finish()
        load(3).start()
        for index in range(2):
            feed_gathers[index].finish()
            load(index).start()
        for index in (3, 0, 1):
            load(index).wait()
        gb[...] = (gb[...].astype(F32) * loss_scale).astype(BF16)
        h2_gather.own().wait()
        hidden_rows(h2_gather.me)
        h2_gather.arrived(0)
        hidden_rows(h2_gather.beside)
        for k in range(1, outer):
            h2_gather.forward(k)
            hidden_rows(h2_gather.source(k))
            h2_gather.arrived(k)
            hidden_rows(h2_gather.source_beside(k))
        weight_gradient(down_part, gb, z, reduce_down)
        feed_gathers[2].finish()
        load(2).start()
        load(2).wait()
        for k in [*range(1, outer), 0]:
            result_rows(reduce_h2.given(k))
            reduce_h2.to_beside(k).start()
            reduce_y.to_beside(k).start()
            result_rows(reduce_h2.kept(k))
            if k:
                reduce_h2.join(k)
        weight_gradient(gate_part, rows_all, dg, reduce_gate)
        weight_gradient(up_part, rows_all, du, reduce_up)

    weights = pltpu.VMEM((feed, model) if flip else (dp, shard, feed), BF16)
    hidden = pltpu.VMEM((length, feed), BF16)
    pl.run_scoped(
        feed_forward,
        weights,
        weights,
        weights,
        pltpu.VMEM((mp, own, model), BF16),
        hidden,
        hidden,
        hidden,
    )
    h2_gather.sent()

    def mixer(
        h, p, inverse, w, scores, step, delta, state, o, m, ds_all, dp_low, db_low,
    ):
        do, entry, dc = o, w, p
        targets = (h, p, inverse, w, scores, step, delta, state, o, m)

        def load(index):
            return pltpu.make_async_copy(stored[index], targets[index], load_sem.at[index])

        for index in (1, 4, 3, 8, 9, 5, 2, 6, 7, 0):
            load(index).start()

        dh = reduce_h2.finish()
        y = y1[...]
        r = lax.rsqrt(jnp.mean(y * y, axis=-1, keepdims=True) + 1e-06)
        small[...] = jnp.zeros_like(small)
        small[second_row : second_row + 1] = jnp.sum(dh * y * r, axis=0, keepdims=True)
        scaled = second[...] * dh
        grad = (
            cot[...].astype(F32) * loss_scale
            + r * scaled
            - y * (r * r * r * jnp.mean(y * scaled, axis=-1, keepdims=True))
        )
        input_grad[...] = grad
        low[...] = grad.astype(BF16)
        ab_gather.start()
        reduce_h2.sent()
        reduce_down.join_all()

        for index in (1, 4, 3):
            load(index).wait()
        dc[length + 8 :] = jnp.zeros((8, dc.shape[1]), F32)

        def chains_of(i, size):
            chains = [(i * size + j, head) for j in range(size) for head in range(heads)]
            starts = [pl.multiple_of(c * BLOCK, BLOCK) for c, _ in chains]
            places = [head * blocks + c for c, head in chains]
            return chains, starts, places

        def lane(head):
            return slice(head * BLOCK, (head + 1) * BLOCK)

        @pl.loop(0, blocks // group)
        def _(i):
            chains, starts, places = chains_of(i, group)
            moved = each(lambda at: mm(scores[at], w[at]), places)
            for (c, head), start, place, t in zip(chains, starts, places, moved):
                s, _, _ = activated(p, conv, start, 0, head, width, taps)
                ds_all[place] = s * (inverse_norm(s) * scale) - t

        ab_gather.forward_all()
        reduce_y.join_all()
        ab_gather.finish()
        for index in (8, 9, 5):
            load(index).wait()
        out_weight = out_rows.reshape(width, model)
        d_gain = jnp.zeros((1, BLOCK), F32)
        for i in range(mp):
            dm = dot(ab_all[i], out_weight[...], tb=True)
            at = slice(i * own, (i + 1) * own)
            for head in range(heads):
                x = o[at, lane(head)]
                g = dm[:, lane(head)]
                r = lax.rsqrt(jnp.mean(x * x, axis=-1, keepdims=True) + 1e-05)
                d_gain = d_gain + jnp.sum(g * x * r, axis=0, keepdims=True)
                scaled = g * gain[...]
                do[at, lane(head)] = r * scaled - x * (
                    r * r * r * jnp.mean(x * scaled, axis=-1, keepdims=True)
                )
        for d in range(dp):
            moved = mm(
                jnp.broadcast_to(d_gain, (8, BLOCK)), place_lanes(d, dp, lanes, gains), tb=True
            )
            small_part[d, gain_row : gain_row + 1] = moved[0:1]
        @pl.loop(0, mp)
        def _(i):
            x = ab_all[:, :, pl.ds(pl.multiple_of(i * width, BLOCK), width)].reshape(length, width)
            out_part[i] = dot(m[...], x, ta=True).astype(BF16).reshape(per, shard, width)

        def swap(k, block):
            return pltpu.make_async_remote_copy(
                src_ref=out_part.at[block],
                dst_ref=out_columns.at[pl.ds(column * per, per)],
                send_sem=swap_send.at[k],
                recv_sem=swap_recv.at[k],
                device_id={"mp": (column + k) % mp},
                device_id_type=MESH,
            )

        def swap_in(k):
            source = (column + mp - k) % mp
            return pltpu.make_async_remote_copy(
                src_ref=out_part.at[source],
                dst_ref=out_columns.at[pl.ds(source * per, per)],
                send_sem=swap_send.at[k],
                recv_sem=swap_recv.at[k],
                device_id={"mp": (column + k) % mp},
                device_id_type=MESH,
            )

        for k in range(1, mp):
            swap(k, (column + k) % mp).start()
        out_columns[pl.ds(column * per, per)] = out_part[column]

        @pl.loop(0, blocks // group)
        def _(i):
            chains, starts, places = chains_of(i, group)
            grads = [do[pl.ds(start, BLOCK), lane(head)] for (_, head), start in zip(chains, starts)]
            for place, t in zip(places, each(lambda at, g: mm(ds_all[at], g, ta=True), places, grads)):
                entry[place] = t

        def retreat(i, grads):
            places = [head * blocks + blocks - 1 - i for head in range(heads)]
            for place, g in zip(places, grads):
                ds_all[place] = g
            moved = each(lambda at, g: mm(step[at], g, ta=True), places, grads)
            return tuple(each(lambda at, g, t: g - t + entry[at], places, grads, moved))

        grads = tuple(jnp.zeros((BLOCK, BLOCK), F32) for _ in range(heads))
        for i in range(blocks):
            grads = retreat(i, grads)
        for index in (2, 6, 7, 0):
            load(index).wait()
        reduce_gate.join_all()
        d_conv = small
        conv_lanes = pl.ds(pl.multiple_of(column * width, BLOCK), width)

        def through(parts, grad, start, part, head):
            s, gate, shifted = parts
            columns = slice(part * width + head * BLOCK, part * width + (head + 1) * BLOCK)
            d_pre = grad * (gate + s * (1.0 - gate))
            dc[pl.ds(pl.multiple_of(start + 8, 8), BLOCK), columns] = d_pre
            at = pl.ds(pl.multiple_of(column * width + head * BLOCK, BLOCK), BLOCK)
            for j in range(taps):
                line = conv_row + part * taps + j
                d_conv[line : line + 1, at] += jnp.sum(d_pre * shifted[j], axis=0, keepdims=True)

        def gradients(i):
            chains, starts, places = chains_of(steps - 1 - i, size)
            qparts, kparts, vparts = (
                [
                    activated(p, conv, start, part, head, width, taps)
                    for (_, head), start in zip(chains, starts)
                ]
                for part in range(3)
            )
            rqs = [inverse_norm(s) for s, _, _ in qparts]
            rks = [inverse_norm(s) for s, _, _ in kparts]
            qs = [part[0] * (r * scale) for part, r in zip(qparts, rqs)]
            ks = [part[0] * r for part, r in zip(kparts, rks)]
            betas = [
                sigmoid(beta_pre[pl.ds(start, BLOCK), head : head + 1])
                for (_, head), start in zip(chains, starts)
            ]
            kbs = each(lambda k, beta: k * beta, ks, betas)
            d_os = [do[pl.ds(start, BLOCK), lane(head)] for (_, head), start in zip(chains, starts)]
            deltas = [delta[at] for at in places]
            s_ins = [state[at] for at in places]
            ds_outs = [ds_all[at] for at in places]
            t1 = each(lambda at, g: mm(scores[at], g, ta=True), places, d_os)
            t2 = each(mm, ks, ds_outs)
            d_scores = each(
                lambda g, d: jnp.where(row >= col, mm(g, d, tb=True), 0.0), d_os, deltas
            )
            dq1 = each(lambda g, s: mm(g, s, tb=True), d_os, s_ins)
            es = each(lambda at, a, b: mm(inverse[at], a + b, ta=True), places, t1, t2)
            dq2 = each(mm, d_scores, ks)
            dk1 = each(lambda a, q: mm(a, q, ta=True), d_scores, qs)
            d_stricts = each(
                lambda e, d: jnp.where(row > col, -mm(e, d, tb=True), 0.0), es, deltas
            )
            dk2 = each(lambda d, s: mm(d, s, tb=True), deltas, ds_outs)
            f2 = each(lambda e, s: mm(e, s, tb=True), es, s_ins)
            f1 = each(mm, d_stricts, ks)
            dk3 = each(lambda a, kb: mm(a, kb, ta=True), d_stricts, kbs)
            fs = each(lambda a, b: a - b, f1, f2)
            dks = each(
                lambda a, b, c, beta, f: a + b + c + beta * f, dk1, dk2, dk3, betas, fs
            )
            rows = {}
            for n, ((c, head), start) in enumerate(zip(chains, starts)):
                beta, e, f = betas[n], es[n], fs[n]
                d_beta = jnp.sum(f * ks[n] + e * vparts[n][0], axis=-1, keepdims=True)
                d_beta = jnp.where(col == head, d_beta * beta * (1.0 - beta), 0.0)
                rows.setdefault(n // heads, []).append(d_beta)
                sq, rq, gq_in = qparts[n][0], rqs[n], (dq1[n] + dq2[n]) * scale
                through(
                    qparts[n],
                    rq * gq_in - sq * (rq * rq * rq * jnp.sum(sq * gq_in, axis=-1, keepdims=True)),
                    start, 0, head,
                )
                sk, rk, dk = kparts[n][0], rks[n], dks[n]
                through(
                    kparts[n],
                    rk * dk - sk * (rk * rk * rk * jnp.sum(sk * dk, axis=-1, keepdims=True)),
                    start, 1, head,
                )
                through(vparts[n], beta * e, start, 2, head)
            for n, parts in rows.items():
                db_low[pl.ds(starts[n * heads], BLOCK)] = sum(parts).astype(BF16)

        size = 2 if blocks % 4 == 0 else 1
        steps = blocks // size
        pl.loop(0, steps // 2)(gradients)
        reduce_up.join_all()
        for k in range(1, mp):
            swap_in(k).wait_recv()
        reduce_out.start()
        pl.loop(steps // 2, steps)(gradients)

        @pl.loop(0, blocks)
        def _(c):
            start = pl.multiple_of(c * BLOCK, BLOCK)
            window = dc[pl.ds(pl.multiple_of(start + 8, 8), BLOCK + 8)]
            total = conv[taps - 1 : taps] * window[0:BLOCK]
            for j in range(taps - 1):
                ahead = taps - 1 - j
                total = total + conv[j : j + 1] * window[ahead : ahead + BLOCK]
            dp_low[pl.ds(start, BLOCK)] = total.astype(BF16)

        def projection_gradient(i, size):
            x = h[:, pl.ds(pl.multiple_of(i * size, size), size)]
            total = dot(x, dp_low[...], ta=True).astype(BF16)
            count = size // shard
            qkv_part[pl.ds(i * count, count)] = total.reshape(count, shard, 3 * width)

        if flip:
            for k in [*range(1, reduce_qkv.outer), 0]:
                projection_gradient(reduce_qkv.target(k), 2 * shard)
                reduce_qkv.to_beside(k).start()
        else:
            pl.loop(0, model // tile)(lambda i: projection_gradient(i, tile))
            reduce_qkv.start()
        weight = qkv.reshape(model, 3 * width)

        def rows(index):
            at = pl.ds(pl.multiple_of(index * own, own), own)
            dh_part[index] = (
                dot(dp_low[at], weight[...], tb=True) + dot(db_low[at], beta_rows[...])
            ).astype(BF16)

        for k in [*range(1, reduce_h.outer), 0]:
            rows(reduce_h.given(k))
            reduce_h.to_beside(k).start()
            rows(reduce_h.kept(k))
            if k:
                reduce_h.join(k)
        reduce_out.join_all()
        reduce_qkv.join(1)
        d_beta = dot(db_low[...], h[...], ta=True)
        for g in range(heads * mp):
            line = d_beta[g % heads : g % heads + 1]
            small[g : g + 1] = jnp.where(column == g // heads, line, 0.0)
        for k in range(1, mp):
            swap(k, (column + k) % mp).wait_send()

    pl.run_scoped(
        mixer,
        *mixer_buffers,
        square,
        pltpu.VMEM((length, 3 * width), BF16),
        pltpu.VMEM((length, BLOCK), BF16),
    )
    for reduce, result in ((reduce_gate, d_gate), (reduce_up, d_up), (reduce_down, d_down)):
        result[...] = reduce.finish()
    output[...] = (y1[...] + reduce_y.finish()).astype(BF16)
    for k in range(2, reduce_qkv.outer):
        reduce_qkv.join(k)
    dh = reduce_h.finish()
    x = tokens[...].astype(F32)
    s = lax.rsqrt(jnp.mean(x * x, axis=-1, keepdims=True) + 1e-06)
    small[first_row : first_row + 1] = jnp.sum(dh * x * s, axis=0, keepdims=True)
    for d in range(dp):
        small_part[d, 0:gain_row] = small[0:gain_row, d * lanes : (d + 1) * lanes]
        small_part[d, gain_row + 1 :] = jnp.zeros((small_part.shape[1] - gain_row - 1, lanes), F32)
    reduce_small.start()
    scaled = first[...] * dh
    input_grad[...] += s * scaled - x * (
        s * s * s * jnp.mean(x * scaled, axis=-1, keepdims=True)
    )
    reduce_small.join_all()
    shared[:, 3 * width :] = reduce_out.finish().astype(BF16)
    small_low[...] = reduce_small.finish()
    narrow = Gather("mp", mp, small_low, leading(small_sums), share_sems, 1)
    narrow.start()
    shared[:, : 3 * width] = reduce_qkv.finish().astype(BF16)
    wide = Gather("mp", mp, shared, leading(shared_all), share_sems, 0)
    wide.start()
    narrow.forward_all()
    wide.forward_all()
    narrow.finish()
    small_total = small_sums[0]
    for i in range(1, mp):
        small_total = small_total + small_sums[i]
    d_small[...] = small_total
    wide.finish()
    ab_gather_done = (reduce_y, reduce_h, *over_dp)
    for reduce in ab_gather_done:
        reduce.sent()


def finish_kernel(mp, heads, *refs):
    take = Taker(refs)
    small, shared_in, *passed_in = take(7)
    passed, models, smalls = take(5), take(4), take(7)
    held = take(5)
    shared, wide, sems = take(3)
    width = heads * BLOCK
    loads = [
        pltpu.make_async_copy(src, dst, sems.at[i])
        for i, (src, dst) in enumerate(zip(passed_in, held))
    ]
    copies = [
        pltpu.make_async_copy(src, dst, sems.at[10 + i])
        for i, (src, dst) in enumerate(zip(held, passed))
    ]
    load = pltpu.make_async_copy(shared_in, shared, sems.at[5])
    load.start()
    for copy in loads:
        copy.start()
    line = 0
    for ref in smalls:
        ref[...] = small[line : line + ref.shape[0], 0 : ref.shape[1]]
        line += ref.shape[0]
    load.wait()
    for index, result in enumerate(models):
        for i in range(mp):
            wide[index, :, i * width : (i + 1) * width] = shared[
                i, :, index * width : (index + 1) * width
            ].astype(F32)
        copies.append(pltpu.make_async_copy(wide.at[index], result, sems.at[6 + index]))
        copies[-1].start()
    for first, second in zip(loads, copies):
        first.wait()
        second.start()
    for copy in copies:
        copy.wait()


def call(kernel, ins, outs, scratch, collective, name, limit):
    return pl.pallas_call(
        kernel,
        out_shape=[jax.ShapeDtypeStruct(shape, kind) for _, shape, kind in outs],
        in_specs=[spec for spec, _ in ins],
        out_specs=[spec for spec, _, _ in outs],
        scratch_shapes=list(scratch),
        compiler_params=pltpu.CompilerParams(
            collective_id=collective,
            has_side_effects=collective is not None,
            vmem_limit_bytes=limit * MIB,
        ),
        name=name,
    )(*[array for _, array in ins])


def shards(
    dp,
    mp,
    tokens,
    cotangent,
    domain,
    domain_weight,
    query_weight,
    key_weight,
    value_weight,
    beta_weight,
    conv_query,
    conv_key,
    conv_value,
    out_gain,
    out_weight,
    norm_first,
    norm_second,
    gate_weight,
    up_weight,
    down_weight,
):
    own, model = tokens.shape
    length = own * mp
    shard = query_weight.shape[0]
    taps = conv_query.shape[0]
    all_heads = beta_weight.shape[1]
    heads = all_heads // mp
    width = model // mp
    feed = gate_weight.shape[1]
    lanes = norm_first.shape[0]
    gains = out_gain.shape[0]
    conv_row, gain_row = all_heads, all_heads + 3 * taps + 2
    first_row, second_row = gain_row - 2, gain_row - 1
    small_rows = -(-(gain_row + 1) // 8) * 8
    rows_of = (conv_row, first_row, second_row, gain_row)
    flip = lanes % 128 == 0

    square = ((heads * (length // BLOCK), BLOCK, BLOCK), F32)
    stored = [
        ((length, model), BF16),
        ((length + 16, 3 * width), F32),
        *[square] * 6,
        ((length, width), F32),
        ((length, width), BF16),
    ]
    feed_shape = (feed, model) if flip else (dp, shard, feed)
    feed_block = (feed, shard) if flip else (shard, feed)
    feed_grad = (VM, feed_block, F32)
    feed_own = (
        (gate_weight.T, up_weight.T, down_weight) if flip else (gate_weight, up_weight, down_weight.T)
    )
    token_rows = ((mp, own, model), BF16)
    sizes = (feed_block,) * 3 + ((shard, width), (shard, 3 * width))
    results = call(
        partial(block_kernel, dp, mp, taps, heads, gains, flip, rows_of),
        [
            (SM, domain), (SM, domain_weight),
            (VM, tokens), (VM, cotangent), (ANY, query_weight), (ANY, key_weight), (ANY, value_weight),
            (ANY, out_weight),
            (VM, beta_weight.T), (VM, conv_query), (VM, conv_key), (VM, conv_value),
            (VM, norm_first[None]), (VM, norm_second[None]), (VM, out_gain[None]),
            *[(ANY, a) for a in feed_own],
        ],
        [
            (VM, (own, model), BF16),
            (VM, (own, model), F32),
            (VM, (mp, shard, 4 * width), BF16),
            (VM, (small_rows, lanes), F32),
            *[feed_grad] * 3,
            (ANY, *token_rows), *[(ANY, feed_shape, BF16)] * 3,
            *[(ANY, *kind) for kind in stored],
        ],
        [pltpu.VMEM(*token_rows)] * 4
        + [
            pltpu.VMEM((own, model), BF16),
            pltpu.VMEM((dp, shard, 3 * width), BF16),
            pltpu.VMEM((dp // mp, shard, model), BF16),
            pltpu.VMEM((dp, shard, width), BF16),
            pltpu.VMEM((own, model), F32),
            pltpu.VMEM((BLOCK, model), BF16),
            pltpu.VMEM((taps, 3 * width), F32),
            pltpu.VMEM((1, model), F32),
            pltpu.VMEM((1, model), F32),
            pltpu.VMEM((1, BLOCK), F32),
            pltpu.VMEM((length, BLOCK), F32),
        ]
        + [pltpu.VMEM(feed_shape, BF16)] * 3
        + [
            pltpu.VMEM((mp, dp // mp, shard, width), BF16),
            pltpu.VMEM((dp, shard, 3 * width), BF16),
        ]
        + ReduceScatter.buffers(mp, own, model) * 2
        + [b for size in sizes for b in ReduceScatter.buffers(dp, *size)]
        + ReduceScatter.buffers(dp, small_rows, lanes, F32)
        + [
            pltpu.VMEM((small_rows, lanes), F32),
            pltpu.VMEM((dp, small_rows, lanes), F32),
            pltpu.VMEM((small_rows, model), F32),
            pltpu.VMEM((dp, small_rows, lanes), F32),
            pltpu.VMEM((shard, 4 * width), BF16),
            pltpu.VMEM((small_rows, lanes), F32),
            pltpu.VMEM((mp, small_rows, lanes), F32),
        ]
        + Gather.scratch(mp, 4)
        + Gather.scratch(dp, 8)
        + ReduceScatter.scratch(mp, 4)
        + ReduceScatter.scratch(dp, 6)
        + Gather.scratch(mp, 2)
        + [pltpu.SemaphoreType.DMA((mp,))] * 4
        + [
            pltpu.SemaphoreType.DMA((10,)),
            pltpu.SemaphoreType.DMA((10,)),
            pltpu.SemaphoreType.DMA((4,)),
        ],
        0,
        "block",
        63,
    )
    output, input_grad, shared, small, d_gate, d_up, d_down = results[:7]
    small_shapes = [(all_heads, lanes)] + [(taps, lanes)] * 3 + [(1, lanes)] * 2 + [(1, gains)]
    results = call(
        partial(finish_kernel, mp, heads),
        [(VM, small)] + [(ANY, a) for a in (shared, output, input_grad, d_gate, d_up, d_down)],
        [
            (ANY, (own, model), BF16),
            (ANY, (own, model), F32),
            *[(ANY, feed_block, F32)] * 3,
            *[(ANY, (shard, model), F32)] * 4,
            *[(VM, shape, F32) for shape in small_shapes],
        ],
        [
            pltpu.VMEM((own, model), BF16),
            pltpu.VMEM((own, model), F32),
            *[pltpu.VMEM(feed_block, F32)] * 3,
            pltpu.VMEM((mp, shard, 4 * width), BF16),
            pltpu.VMEM((4, shard, model), F32),
            pltpu.SemaphoreType.DMA((15,)),
        ],
        None,
        "finish",
        60,
    )
    output, input_grad, d_gate, d_up, d_down = results[:5]
    d_query, d_key, d_value, d_outw = results[5:9]
    d_beta, d_conv_q, d_conv_k, d_conv_v, d_first, d_second, d_gain = results[9:]
    if flip:
        d_gate, d_up = d_gate.T, d_up.T
    else:
        d_down = d_down.T
    return (
        output,
        input_grad,
        d_query,
        d_key,
        d_value,
        d_beta.T,
        d_conv_q,
        d_conv_k,
        d_conv_v,
        d_gain[0],
        d_outw,
        d_first[0],
        d_second[0],
        d_gate,
        d_up,
        d_down,
    )


def solution(mesh):
    dp, mp = mesh.shape["dp"], mesh.shape["mp"]
    weight = P("dp", None)
    split = P(None, "dp")
    rows = P(("dp", "mp"), None)
    return jax.shard_map(
        partial(shards, dp, mp),
        mesh=mesh,
        in_specs=(
            rows, rows, P("dp"), P(), weight, weight, weight, weight, split, split, split,
            P("dp"), weight, P("dp"), P("dp"), P("dp", "mp"), P("dp", "mp"), P("mp", "dp"),
        ),
        out_specs=(
            rows, rows, weight, weight, weight, weight, split, split, split,
            P("dp"), weight, P("dp"), P("dp"), P("dp", "mp"), P("dp", "mp"), P("mp", "dp"),
        ),
        check_vma=False,
    )
```

```python
from functools import partial

import jax
import jax.numpy as jnp
from jax import lax
from jax.experimental import pallas as pl
from jax.experimental.pallas import tpu as pltpu
from jax.sharding import PartitionSpec as P

BLOCK = 128
MESH = pl.DeviceIdType.MESH
F32 = jnp.float32
BF16 = jnp.bfloat16
MIB = 1 << 20
VM = pl.BlockSpec(memory_space=pltpu.VMEM)
ANY = pl.BlockSpec(memory_space=pl.ANY)
SM = pl.BlockSpec(memory_space=pltpu.SMEM)


def dot(a, b, ta=False, tb=False):
    dims = (((0 if ta else 1,), (1 if tb else 0,)), ((), ()))
    return lax.dot_general(a, b, dims, preferred_element_type=F32)


def halves(a):
    high = a.astype(BF16)
    return high, (a - high.astype(F32)).astype(BF16)


def mm(a, b, ta=False, tb=False):
    ah, al = halves(a)
    bh, bl = halves(b)
    da, db = 0 if ta else 1, 1 if tb else 0
    left = jnp.concatenate([ah, al], axis=da)
    right = jnp.concatenate([bh, bh], axis=db)
    columns = b.shape[1 - db]
    if columns > BLOCK:
        return dot(left, right, ta, tb) + dot(ah, bl, ta, tb)
    rest = jnp.concatenate([bl, jnp.zeros_like(bl)], axis=db)
    both = dot(left, jnp.concatenate([right, rest], axis=1 - db), ta, tb)
    return both[:, :columns] + both[:, columns:]


def one_pass(a, b, ta=False, tb=False):
    return dot(a.astype(BF16), b.astype(BF16), ta, tb)


def each(function, *lists):
    return [function(*items) for items in zip(*lists)]


def iota2(size):
    return (
        lax.broadcasted_iota(jnp.int32, (size, size), 0),
        lax.broadcasted_iota(jnp.int32, (size, size), 1),
    )


def unit_lower_inverses(stricts):
    size = stricts[0].shape[0]
    row, col = iota2(size)
    pairs = (row >> 1) == (col >> 1)
    unit = jnp.where(row == col, 1.0, 0.0)
    inverses = each(lambda a: unit - jnp.where(pairs, a, 0.0), stricts)
    shift = 1
    while (1 << shift) < size:
        inside = (row >> (shift + 1)) == (col >> (shift + 1))
        apart = (row >> shift) != (col >> shift)
        corner = inside & apart
        moved = each(lambda x, a: mm(x, jnp.where(corner, a, 0.0)), inverses, stricts)
        moved = each(mm, moved, inverses)
        inverses = each(lambda x, t: x - t, inverses, moved)
        shift += 1
    return inverses


def sigmoid(a):
    return 1.0 / (1.0 + jnp.exp(-a))


class Gather:
    def __init__(self, axis, count, src, place, sems, slot):
        self.axis, self.src, self.place = axis, src, place
        self.outer = count // 2
        self.me = lax.axis_index(axis)
        self.a, self.b = self.me // 2, self.me % 2
        self.sa, self.ra, self.sb, self.rb, self.local = (s.at[slot] for s in sems)
        self.beside = self.a * 2 + 1 - self.b

    @staticmethod
    def scratch(count, slots):
        return [pltpu.SemaphoreType.DMA((slots, count // 2))] * 4 + [
            pltpu.SemaphoreType.DMA((slots, 1))
        ]

    def copy(self, src, block, send, recv, target):
        return pltpu.make_async_remote_copy(
            src_ref=src,
            dst_ref=self.place(block),
            send_sem=send,
            recv_sem=recv,
            device_id={self.axis: target},
            device_id_type=MESH,
        )

    def own(self):
        return pltpu.make_async_copy(self.src, self.place(self.me), self.local.at[0])

    def source(self, k):
        return (self.a + self.outer - k) % self.outer * 2 + self.b

    def source_beside(self, k):
        return (self.a + self.outer - k) % self.outer * 2 + 1 - self.b

    def to_outer(self, k):
        target = (self.a + k) % self.outer * 2 + self.b
        return self.copy(self.src, self.me, self.sa.at[k], self.ra.at[k], target)

    def to_beside(self, k):
        block = self.source(k)
        src = self.src if k == 0 else self.place(block)
        return self.copy(src, block, self.sb.at[k], self.rb.at[k], self.beside)

    def start_outer(self):
        for k in range(1, self.outer):
            self.to_outer(k).start()

    def start_beside(self):
        self.to_beside(0).start()
        self.own().start()

    def start(self):
        self.start_outer()
        self.start_beside()

    def forward(self, k):
        self.to_outer(k).wait_recv()
        self.to_beside(k).start()

    def forward_all(self):
        for k in range(1, self.outer):
            self.forward(k)

    def arrived(self, k):
        self.to_beside(k).wait_recv()

    def sent(self):
        for k in range(self.outer):
            if k:
                self.to_outer(k).wait_send()
            self.to_beside(k).wait_send()

    def finish(self):
        self.own().wait()
        for k in range(self.outer):
            self.arrived(k)
        self.sent()


class ReduceScatter:
    def __init__(self, axis, count, place, near, far, sems, slot):
        self.axis, self.place, self.near, self.far = axis, place, near, far
        self.outer = count // 2
        self.me = lax.axis_index(axis)
        self.a, self.b = self.me // 2, self.me % 2
        self.sa, self.ra, self.sb, self.rb = (s.at[slot] for s in sems)
        self.beside = self.a * 2 + 1 - self.b

    @staticmethod
    def scratch(count, slots):
        return [pltpu.SemaphoreType.DMA((slots, count // 2))] * 4

    @staticmethod
    def buffers(count, rows, columns, kind=BF16):
        return [pltpu.VMEM((count // 2, rows, columns), kind)] * 2

    def target(self, k):
        return (self.a + k) % self.outer

    def kept(self, k):
        return self.target(k) * 2 + self.b

    def given(self, k):
        return self.target(k) * 2 + 1 - self.b

    def to_beside(self, k):
        return pltpu.make_async_remote_copy(
            src_ref=self.place(self.given(k)),
            dst_ref=self.near.at[k],
            send_sem=self.sb.at[k],
            recv_sem=self.rb.at[k],
            device_id={self.axis: self.beside},
            device_id_type=MESH,
        )

    def to_outer(self, k):
        return pltpu.make_async_remote_copy(
            src_ref=self.place(self.kept(k)),
            dst_ref=self.far.at[k],
            send_sem=self.sa.at[k],
            recv_sem=self.ra.at[k],
            device_id={self.axis: self.target(k) * 2 + self.b},
            device_id_type=MESH,
        )

    def start(self):
        for k in [*range(1, self.outer), 0]:
            self.to_beside(k).start()

    def join(self, k):
        self.to_beside(k).wait_recv()
        block = self.place(self.kept(k))
        total = block[...].astype(F32) + self.near[k].astype(F32)
        if k == 0:
            return total
        block[...] = total.astype(block.dtype)
        self.to_outer(k).start()

    def join_all(self):
        for k in range(1, self.outer):
            self.join(k)

    def finish(self):
        total = self.join(0)
        for k in range(1, self.outer):
            self.to_outer(k).wait_recv()
            total = total + self.far[k].astype(F32)
        return total

    def sent(self):
        for k in range(self.outer):
            self.to_beside(k).wait_send()
            if k:
                self.to_outer(k).wait_send()


def leading(ref):
    return lambda i: ref.at[i]


def columns_of(ref, size):
    return lambda i: ref.at[:, pl.ds(pl.multiple_of(i * size, size), size)]


def greet(counts):
    barrier = pltpu.get_barrier_semaphore()
    for axis, count in counts:
        me = lax.axis_index(axis)
        for k in range(1, count):
            pl.semaphore_signal(
                barrier, inc=1, device_id={axis: (me + k) % count}, device_id_type=MESH
            )
    pl.semaphore_wait(barrier, sum(count - 1 for _, count in counts))


class Taker:
    def __init__(self, refs):
        self.refs, self.cursor = refs, 0

    def __call__(self, count):
        self.cursor += count
        return self.refs[self.cursor - count : self.cursor]

    def one(self):
        return self(1)[0]


def activated(p, conv, start, part, head, width, taps):
    columns = slice(part * width + head * BLOCK, part * width + (head + 1) * BLOCK)
    window = p[pl.ds(start, BLOCK + 8), columns]
    shifted = [window[8 - taps + 1 + j : 8 - taps + 1 + j + BLOCK] for j in range(taps)]
    pre = conv[0:1, columns] * shifted[0]
    for j in range(1, taps):
        pre = pre + conv[j : j + 1, columns] * shifted[j]
    gate = sigmoid(pre)
    return pre * gate, gate, shifted


def inverse_norm(s):
    return lax.rsqrt(jnp.sum(s * s, axis=-1, keepdims=True) + 1e-06)


def place_lanes(index, count, lanes, gains):
    row = lax.broadcasted_iota(jnp.int32, (lanes, count * gains), 0)
    col = lax.broadcasted_iota(jnp.int32, (lanes, count * gains), 1)
    return jnp.where((col == row + index * gains) & (row < gains), 1.0, 0.0)


def block_kernel(dp, mp, taps, heads, gains, flip, rows_of, *refs):
    take = Taker(refs)
    domain, domain_weight = take(2)
    tokens, cot = take(2)
    projections, smalls = take(4), take(7)
    gate_own, up_own, down_own = take(3)
    output, input_grad, shared_all, d_small, d_gate, d_up, d_down = take(7)
    cot_all, gate_all, up_all, down_all = take(4)
    stored = take(10)
    rows_all, ab_all, y_part, dh_part, low = take(5)
    qkv, out_rows, out_columns = take(3)
    y1, beta_rows, conv, first, second, gain, beta_pre = take(7)
    gate_part, up_part, down_part, out_part = take(4)
    head_parts = take(heads)
    near_y, far_y, near_h, far_h = take(4)
    buffers = [take(2) for _ in range(5 + heads)]
    small_own, small_all, small, small_part, small_low, small_sums = take(6)
    shared = take.one()
    sems_mp, sems_dp, reduce_sems, dp_sems, share_sems = take(5), take(5), take(4), take(4), take(5)
    rows_send, rows_recv, swap_send, swap_recv, saved_sem, load_sem, feed_sem = take(7)
    conv_row, first_row, second_row, gain_row = rows_of
    own, model = tokens.shape
    length = own * mp
    shard = model // dp
    width = heads * BLOCK
    blocks = length // BLOCK
    lanes = small_own.shape[1]
    feed = gate_own.shape[0] if flip else gate_own.shape[1]
    per = dp // mp
    column = lax.axis_index("mp")
    mine = pl.ds(pl.multiple_of(column * width, BLOCK), width)
    tile, wide_tile = 256, 512
    row, col = iota2(BLOCK)
    scale = BLOCK**-0.5
    group = 4 if blocks % 4 == 0 else 1
    loss_scale = jnp.zeros((1, 1), F32)
    for i in range(domain_weight.shape[0]):
        loss_scale = loss_scale + jnp.where(domain[0] == i, domain_weight[i], 0.0)

    small_own[...] = jnp.zeros_like(small_own)
    line = 0
    for ref in smalls:
        small_own[line : line + ref.shape[0], 0 : ref.shape[1]] = ref[...].astype(F32)
        line += ref.shape[0]

    greet((("dp", dp), ("mp", mp)))
    small_gather = Gather("dp", dp, small_own, leading(small_all), sems_dp, 0)
    places = [lambda d, i=i: qkv.at[d, :, i * width : (i + 1) * width] for i in range(3)]
    *qkv_gathers, out_gather = [
        Gather("dp", dp, src.at[:, mine], place, sems_dp, 1 + i)
        for i, (src, place) in enumerate(zip(projections, [*places, leading(out_columns)]))
    ]
    token_gather = Gather("mp", mp, tokens, leading(rows_all), sems_mp, 0)
    cot_gather = Gather("mp", mp, cot, leading(cot_all), sems_mp, 1)
    def feed_gather(src, dst, rows, slot):
        if flip:
            place = lambda d: dst.at[rows, pl.ds(pl.multiple_of(d * lanes, lanes), lanes)]
            return Gather("dp", dp, src.at[rows], place, sems_dp, slot)
        return Gather(
            "dp", dp, src.at[:, rows], lambda d: dst.at[d, :, rows], sems_dp, slot
        )

    whole, cut = slice(0, feed), feed // 256 * 128
    feed_gathers = [
        feed_gather(gate_own, gate_all, whole, 5),
        feed_gather(up_own, up_all, whole, 6),
        feed_gather(down_own, down_all, slice(0, cut), 7),
        feed_gather(down_own, down_all, slice(cut, feed), 8),
    ]
    small_gather.start()
    qkv_gathers[0].start()
    token_gather.start()
    small_gather.forward_all()
    qkv_gathers[0].forward(1)
    qkv_gathers[1].start()
    for k in range(2, qkv_gathers[0].outer):
        qkv_gathers[0].forward(k)
    qkv_gathers[1].forward(1)
    qkv_gathers[2].start()
    for k in range(2, qkv_gathers[1].outer):
        qkv_gathers[1].forward(k)
    token_gather.forward_all()
    qkv_gathers[2].forward(1)
    out_gather.start_outer()
    feed_gathers[0].start_outer()
    for k in range(2, qkv_gathers[2].outer):
        qkv_gathers[2].forward(k)
    cot_gather.start()
    small_gather.finish()

    for d in range(dp):
        small[:, d * lanes : (d + 1) * lanes] = small_all[d]
    beta_rows[...] = jnp.zeros_like(beta_rows)
    picked = []
    for head in range(heads):
        wanted = jnp.zeros((1, model), F32)
        for g in range(heads * mp):
            wanted = jnp.where(column * heads + head == g, small[g : g + 1], wanted)
        picked.append(wanted)
    beta_rows[0:16] = jnp.concatenate(
        picked + [jnp.zeros((16 - heads, model), F32)], axis=0
    ).astype(BF16)
    for i in range(3):
        for j in range(taps):
            at = conv_row + i * taps + j
            conv[j : j + 1, i * width : (i + 1) * width] = small[at : at + 1, mine]
    first[...] = small[first_row : first_row + 1]
    second[...] = small[second_row : second_row + 1]
    total = jnp.zeros((8, dp * gains), F32)
    for d in range(dp):
        line = jnp.broadcast_to(small_all[d, gain_row : gain_row + 1], (8, lanes))
        total = total + dot(line.astype(BF16), place_lanes(d, dp, lanes, gains).astype(BF16))
    gain[...] = total[0:1]

    token_gather.finish()
    h2_gather = Gather("mp", mp, low, leading(rows_all), sems_mp, 2)
    ab_gather = Gather("mp", mp, low, leading(ab_all), sems_mp, 3)
    reduce_part = ReduceScatter("mp", mp, leading(y_part), near_y, far_y, reduce_sems, 0)
    reduce_h2 = ReduceScatter("mp", mp, leading(dh_part), near_h, far_h, reduce_sems, 1)
    reduce_y = ReduceScatter("mp", mp, leading(y_part), near_y, far_y, reduce_sems, 2)
    reduce_h = ReduceScatter("mp", mp, leading(dh_part), near_h, far_h, reduce_sems, 3)
    over_dp = [
        ReduceScatter(
            "dp",
            dp,
            columns_of(part, shard) if flip and slot < 3 else leading(part),
            *pair,
            dp_sems,
            slot,
        )
        for slot, (part, pair) in enumerate(
            zip((gate_part, up_part, down_part, out_columns, *head_parts, small_part), buffers)
        )
    ]
    reduce_gate, reduce_up, reduce_down, reduce_out, *reduce_heads, reduce_small = over_dp

    def mixer_forward(
        h, p, inverse, w, scores, step, delta, state, o, m, u, offset, q_all
    ):
        saved = (h, p, inverse, w, scores, step, delta, state, o, m)
        for i in range(mp):
            x = rows_all[i].astype(F32)
            normed = x * lax.rsqrt(jnp.mean(x * x, axis=-1, keepdims=True) + 1e-06) * first[...]
            h[i * own : (i + 1) * own] = normed.astype(BF16)
        for g in qkv_gathers:
            g.finish()
        out_gather.start_beside()
        for g in feed_gathers:
            g.start_beside()

        p[0:8] = jnp.zeros((8, p.shape[1]), F32)
        p[length + 8 :] = jnp.zeros((8, p.shape[1]), F32)
        weight = qkv.reshape(model, 3 * width)

        @pl.loop(0, mp)
        def _(i):
            at = pl.ds(pl.multiple_of(i * own, own), own)
            low = h[at]
            p[pl.ds(pl.multiple_of(i * own + 8, 8), own)] = dot(low, weight[...])
            beta_pre[at] = dot(low, beta_rows[...], tb=True)

        def save(index):
            return pltpu.make_async_copy(saved[index], stored[index], saved_sem.at[index])

        for index in (0, 1):
            save(index).start()


        def prepare(i):
            chains = [(i * group + j, head) for j in range(group) for head in range(heads)]
            starts = [pl.multiple_of(c * BLOCK, BLOCK) for c, _ in chains]
            places = [head * blocks + c for c, head in chains]
            ks, kbs, vbs, qs = [], [], [], []
            for (c, head), start in zip(chains, starts):
                s, _, _ = activated(p, conv, start, 0, head, width, taps)
                qs.append(s * (inverse_norm(s) * scale))
                s, _, _ = activated(p, conv, start, 1, head, width, taps)
                k = s * inverse_norm(s)
                v, _, _ = activated(p, conv, start, 2, head, width, taps)
                beta = sigmoid(beta_pre[pl.ds(start, BLOCK), head : head + 1])
                ks.append(k)
                kbs.append(k * beta)
                vbs.append(v * beta)
            for place, q in zip(places, qs):
                q_all[place] = q
            stricts = each(lambda a, b: jnp.where(row > col, mm(a, b, tb=True), 0.0), kbs, ks)
            for place, a in zip(places, each(lambda q, k: mm(q, k, tb=True), qs, ks)):
                scores[place] = jnp.where(row >= col, a, 0.0)
            xs = unit_lower_inverses(stricts)
            for place, x in zip(places, xs):
                inverse[place] = x
            wus = each(lambda x, a, b: mm(x, jnp.concatenate([a, b], axis=1)), xs, kbs, vbs)
            for place, wu in zip(places, wus):
                w[place] = wu[:, :BLOCK]
                u[place] = wu[:, BLOCK:]
            for place, gb in zip(places, each(lambda k, wu: mm(k, wu, ta=True), ks, wus)):
                step[place] = gb[:, :BLOCK]
                offset[place] = gb[:, BLOCK:]

        def swap(k, block, source):
            columns = pl.ds(pl.multiple_of(source * width, BLOCK), width)
            return pltpu.make_async_remote_copy(
                src_ref=out_columns.at[pl.ds(block * per, per)],
                dst_ref=out_rows.at[:, :, columns],
                send_sem=rows_send.at[k],
                recv_sem=rows_recv.at[k],
                device_id={"mp": (column + k) % mp},
                device_id_type=MESH,
            )

        half = blocks // group // 2
        pl.loop(0, half)(prepare)
        out_gather.forward_all()
        feed_gathers[1].start_outer()
        pl.loop(half, blocks // group)(prepare)
        for index in (2, 3, 4, 5):
            save(index).start()
        feed_gathers[0].forward_all()
        cot_gather.forward_all()
        out_gather.finish()
        for k in range(1, mp):
            swap(k, (column + k) % mp, column).start()
        out_rows[:, :, mine] = out_columns[pl.ds(column * per, per)]

        def advance(c, states):
            places = [head * blocks + c for head in range(heads)]
            for place, s in zip(places, states):
                state[place] = s
            moved = each(lambda place, s: mm(step[place], s), places, states)
            return tuple(each(lambda place, s, t: s - t + offset[place], places, states, moved))

        states = tuple(jnp.zeros((BLOCK, BLOCK), F32) for _ in range(heads))
        for c in range(blocks):
            states = advance(c, states)
        save(7).start()

        for k in range(1, mp):
            swap(k, column, (column + mp - k) % mp).wait_recv()
        out_weight = out_rows.reshape(width, model)

        def outputs(index):
            per = own // BLOCK
            chains = [(index * per + j, head) for j in range(per) for head in range(heads)]
            places = [head * blocks + c for c, head in chains]
            boths = each(
                lambda at: mm(jnp.concatenate([w[at], q_all[at]], axis=0), state[at]), places
            )
            ds = each(lambda at, both: u[at] - both[:BLOCK], places, boths)
            for place, d in zip(places, ds):
                delta[place] = d
            outs = each(lambda at, d: mm(scores[at], d), places, ds)
            outs = each(lambda both, out: both[BLOCK:] + out, boths, outs)
            for (c, head), out in zip(chains, outs):
                rows = pl.ds(pl.multiple_of(c * BLOCK, BLOCK), BLOCK)
                at = slice(head * BLOCK, (head + 1) * BLOCK)
                o[rows, at] = out
                r = lax.rsqrt(jnp.mean(out * out, axis=-1, keepdims=True) + 1e-05)
                m[rows, at] = (out * r * gain[...]).astype(BF16)
            at = pl.ds(pl.multiple_of(index * own, own), own)
            y_part[index] = dot(m[at], out_weight[...]).astype(BF16)

        for k in [*range(1, reduce_part.outer), 0]:
            outputs(reduce_part.given(k))
            reduce_part.to_beside(k).start()
            outputs(reduce_part.kept(k))
            if k:
                reduce_part.join(k)
        for index in (6, 8, 9):
            save(index).start()
        feed_gathers[2].start_outer()
        feed_gathers[3].start_outer()
        feed_gathers[1].forward_all()
        y = tokens[...].astype(F32) + reduce_part.finish()
        y1[...] = y
        low[...] = (
            y * lax.rsqrt(jnp.mean(y * y, axis=-1, keepdims=True) + 1e-06) * second[...]
        ).astype(BF16)
        h2_gather.start()
        for g in feed_gathers[2:]:
            g.forward_all()
        reduce_part.sent()
        for k in range(1, mp):
            swap(k, (column + k) % mp, column).wait_send()
        for index in range(10):
            save(index).wait()

    square = pltpu.VMEM((heads * blocks, BLOCK, BLOCK), F32)
    mixer_buffers = [
        pltpu.VMEM((length, model), BF16),
        pltpu.VMEM((length + 16, 3 * width), F32),
        *[square] * 6,
        pltpu.VMEM((length, width), F32),
        pltpu.VMEM((length, width), BF16),
    ]
    pl.run_scoped(mixer_forward, *mixer_buffers, square, square, square)

    def feed_forward(gate, up, down, gb, z, dg, du):
        def load(index):
            src, dst = ((gate_all, gate), (up_all, up), (down_all, down), (cot_all, gb))[index]
            return pltpu.make_async_copy(src, dst, feed_sem.at[index])

        gate_w, up_w, down_w = (
            a if flip else a.reshape(model, feed) for a in (gate, up, down)
        )

        def hidden_rows(index):
            at = pl.ds(pl.multiple_of(index * own, own), own)
            x = rows_all[index]
            g = dot(x, gate_w[...], tb=flip)
            u = dot(x, up_w[...], tb=flip)
            sg = sigmoid(g)
            silu = g * sg
            z[at] = (silu * u).astype(BF16)
            dg[at] = (u * (sg + silu * (1.0 - sg))).astype(BF16)
            du[at] = silu.astype(BF16)

        def result_rows(index):
            at = pl.ds(pl.multiple_of(index * own, own), own)
            dz = dot(gb[index], down_w[...], tb=flip)
            dgl = (dz * dg[at].astype(F32)).astype(BF16)
            dul = (dz * du[at].astype(F32)).astype(BF16)
            dg[at] = dgl
            du[at] = dul
            dh_part[index] = (
                dot(dgl, gate_w[...], tb=not flip) + dot(dul, up_w[...], tb=not flip)
            ).astype(BF16)
            y_part[index] = dot(z[at], down_w[...], tb=not flip).astype(BF16)

        def weight_gradient(part, left, right, reduce):
            @pl.loop(0, model // wide_tile)
            def _(i):
                at = pl.ds(pl.multiple_of(i * wide_tile, wide_tile), wide_tile)
                x = left[:, :, at].reshape(length, wide_tile)
                if flip:
                    part[:, at] = dot(right[...], x, ta=True).astype(BF16)
                else:
                    total = dot(x, right[...], ta=True).astype(BF16)
                    count = wide_tile // shard
                    part[pl.ds(i * count, count)] = total.reshape(count, shard, feed)

            reduce.start()

        outer = h2_gather.outer
        cot_gather.finish()
        load(3).start()
        for index in range(2):
            feed_gathers[index].finish()
            load(index).start()
        for index in (3, 0, 1):
            load(index).wait()
        gb[...] = (gb[...].astype(F32) * loss_scale).astype(BF16)
        h2_gather.own().wait()
        hidden_rows(h2_gather.me)
        h2_gather.arrived(0)
        hidden_rows(h2_gather.beside)
        for k in range(1, outer):
            h2_gather.forward(k)
            hidden_rows(h2_gather.source(k))
            h2_gather.arrived(k)
            hidden_rows(h2_gather.source_beside(k))
        for g in feed_gathers[2:]:
            g.finish()
        load(2).start()
        load(2).wait()
        for k in [*range(1, outer), 0]:
            result_rows(reduce_h2.given(k))
            reduce_h2.to_beside(k).start()
            reduce_y.to_beside(k).start()
            result_rows(reduce_h2.kept(k))
            if k:
                reduce_h2.join(k)
        weight_gradient(down_part, gb, z, reduce_down)
        weight_gradient(gate_part, rows_all, dg, reduce_gate)
        weight_gradient(up_part, rows_all, du, reduce_up)

    weights = pltpu.VMEM((feed, model) if flip else (dp, shard, feed), BF16)
    hidden = pltpu.VMEM((length, feed), BF16)
    pl.run_scoped(
        feed_forward,
        weights,
        weights,
        weights,
        pltpu.VMEM((mp, own, model), BF16),
        hidden,
        hidden,
        hidden,
    )
    h2_gather.sent()

    def mixer(
        h, p, inverse, w, scores, step, delta, state, o, m, ds_all, dp_low, db_low,
    ):
        do, entry, dc = o, w, p
        targets = (h, p, inverse, w, scores, step, delta, state, o, m)

        def load(index):
            return pltpu.make_async_copy(stored[index], targets[index], load_sem.at[index])

        for index in (1, 4, 3, 8, 9, 5, 2, 6, 7, 0):
            load(index).start()

        dh = reduce_h2.finish()
        y = y1[...]
        r = lax.rsqrt(jnp.mean(y * y, axis=-1, keepdims=True) + 1e-06)
        small[...] = jnp.zeros_like(small)
        small[second_row : second_row + 1] = jnp.sum(dh * y * r, axis=0, keepdims=True)
        scaled = second[...] * dh
        grad = (
            cot[...].astype(F32) * loss_scale
            + r * scaled
            - y * (r * r * r * jnp.mean(y * scaled, axis=-1, keepdims=True))
        )
        input_grad[...] = grad
        low[...] = grad.astype(BF16)
        ab_gather.start()
        reduce_h2.sent()
        reduce_down.join_all()

        for index in (1, 4, 3):
            load(index).wait()
        dc[length + 8 :] = jnp.zeros((8, dc.shape[1]), F32)

        def chains_of(i, size):
            chains = [(i * size + j, head) for j in range(size) for head in range(heads)]
            starts = [pl.multiple_of(c * BLOCK, BLOCK) for c, _ in chains]
            places = [head * blocks + c for c, head in chains]
            return chains, starts, places

        def lane(head):
            return slice(head * BLOCK, (head + 1) * BLOCK)

        @pl.loop(0, blocks // group)
        def _(i):
            chains, starts, places = chains_of(i, group)
            moved = each(lambda at: mm(scores[at], w[at]), places)
            for (c, head), start, place, t in zip(chains, starts, places, moved):
                s, _, _ = activated(p, conv, start, 0, head, width, taps)
                ds_all[place] = s * (inverse_norm(s) * scale) - t

        for index in (8, 9, 5):
            load(index).wait()
        out_weight = out_rows.reshape(width, model)

        def output_gradients(index, d_gain):
            dm = dot(ab_all[index], out_weight[...], tb=True)
            at = pl.ds(pl.multiple_of(index * own, own), own)
            for head in range(heads):
                x = o[at, lane(head)]
                g = dm[:, lane(head)]
                r = lax.rsqrt(jnp.mean(x * x, axis=-1, keepdims=True) + 1e-05)
                d_gain = d_gain + jnp.sum(g * x * r, axis=0, keepdims=True)
                scaled = g * gain[...]
                do[at, lane(head)] = r * scaled - x * (
                    r * r * r * jnp.mean(x * scaled, axis=-1, keepdims=True)
                )
            return d_gain

        ab_gather.own().wait()
        d_gain = output_gradients(ab_gather.me, jnp.zeros((1, BLOCK), F32))
        ab_gather.arrived(0)
        d_gain = output_gradients(ab_gather.beside, d_gain)
        for k in range(1, ab_gather.outer):
            ab_gather.forward(k)
            if k == 1:
                reduce_y.join_all()
            d_gain = output_gradients(ab_gather.source(k), d_gain)
            ab_gather.arrived(k)
            d_gain = output_gradients(ab_gather.source_beside(k), d_gain)
        ab_gather.sent()
        for d in range(dp):
            moved = mm(
                jnp.broadcast_to(d_gain, (8, BLOCK)), place_lanes(d, dp, lanes, gains), tb=True
            )
            small_part[d, gain_row : gain_row + 1] = moved[0:1]
        @pl.loop(0, mp)
        def _(i):
            x = ab_all[:, :, pl.ds(pl.multiple_of(i * width, BLOCK), width)].reshape(length, width)
            out_part[i] = dot(m[...], x, ta=True).astype(BF16).reshape(per, shard, width)

        def swap(k, block):
            return pltpu.make_async_remote_copy(
                src_ref=out_part.at[block],
                dst_ref=out_columns.at[pl.ds(column * per, per)],
                send_sem=swap_send.at[k],
                recv_sem=swap_recv.at[k],
                device_id={"mp": (column + k) % mp},
                device_id_type=MESH,
            )

        def swap_in(k):
            source = (column + mp - k) % mp
            return pltpu.make_async_remote_copy(
                src_ref=out_part.at[source],
                dst_ref=out_columns.at[pl.ds(source * per, per)],
                send_sem=swap_send.at[k],
                recv_sem=swap_recv.at[k],
                device_id={"mp": (column + k) % mp},
                device_id_type=MESH,
            )

        for k in range(1, mp):
            swap(k, (column + k) % mp).start()
        out_columns[pl.ds(column * per, per)] = out_part[column]

        @pl.loop(0, blocks // group)
        def _(i):
            chains, starts, places = chains_of(i, group)
            grads = [do[pl.ds(start, BLOCK), lane(head)] for (_, head), start in zip(chains, starts)]
            for place, t in zip(places, each(lambda at, g: mm(ds_all[at], g, ta=True), places, grads)):
                entry[place] = t

        def retreat(i, grads):
            places = [head * blocks + blocks - 1 - i for head in range(heads)]
            for place, g in zip(places, grads):
                ds_all[place] = g
            moved = each(lambda at, g: mm(step[at], g, ta=True), places, grads)
            return tuple(each(lambda at, g, t: g - t + entry[at], places, grads, moved))

        grads = tuple(jnp.zeros((BLOCK, BLOCK), F32) for _ in range(heads))
        for i in range(blocks):
            grads = retreat(i, grads)
        for index in (2, 6, 7, 0):
            load(index).wait()
        reduce_gate.join_all()
        d_conv = small
        conv_lanes = pl.ds(pl.multiple_of(column * width, BLOCK), width)

        def through(parts, grad, start, part, head):
            s, gate, shifted = parts
            columns = slice(part * width + head * BLOCK, part * width + (head + 1) * BLOCK)
            d_pre = grad * (gate + s * (1.0 - gate))
            dc[pl.ds(pl.multiple_of(start + 8, 8), BLOCK), columns] = d_pre
            at = pl.ds(pl.multiple_of(column * width + head * BLOCK, BLOCK), BLOCK)
            for j in range(taps):
                line = conv_row + part * taps + j
                d_conv[line : line + 1, at] += jnp.sum(d_pre * shifted[j], axis=0, keepdims=True)

        def gradients(i, only):
            chains = [((steps - 1 - i) * size + j, only) for j in range(size)]
            starts = [pl.multiple_of(c * BLOCK, BLOCK) for c, _ in chains]
            places = [head * blocks + c for c, head in chains]
            qparts, kparts, vparts = (
                [
                    activated(p, conv, start, part, head, width, taps)
                    for (_, head), start in zip(chains, starts)
                ]
                for part in range(3)
            )
            rqs = [inverse_norm(s) for s, _, _ in qparts]
            rks = [inverse_norm(s) for s, _, _ in kparts]
            qs = [part[0] * (r * scale) for part, r in zip(qparts, rqs)]
            ks = [part[0] * r for part, r in zip(kparts, rks)]
            betas = [
                sigmoid(beta_pre[pl.ds(start, BLOCK), head : head + 1])
                for (_, head), start in zip(chains, starts)
            ]
            kbs = each(lambda k, beta: k * beta, ks, betas)
            d_os = [do[pl.ds(start, BLOCK), lane(head)] for (_, head), start in zip(chains, starts)]
            deltas = [delta[at] for at in places]
            s_ins = [state[at] for at in places]
            ds_outs = [ds_all[at] for at in places]
            t1 = each(lambda at, g: one_pass(scores[at], g, ta=True), places, d_os)
            t2 = each(one_pass, ks, ds_outs)
            d_scores = each(
                lambda g, d: jnp.where(row >= col, one_pass(g, d, tb=True), 0.0), d_os, deltas
            )
            dq1 = each(lambda g, s: one_pass(g, s, tb=True), d_os, s_ins)
            es = each(lambda at, a, b: one_pass(inverse[at], a + b, ta=True), places, t1, t2)
            dq2 = each(one_pass, d_scores, ks)
            dk1 = each(lambda a, q: one_pass(a, q, ta=True), d_scores, qs)
            d_stricts = each(
                lambda e, d: jnp.where(row > col, -one_pass(e, d, tb=True), 0.0), es, deltas
            )
            dk2 = each(lambda d, s: one_pass(d, s, tb=True), deltas, ds_outs)
            f2 = each(lambda e, s: one_pass(e, s, tb=True), es, s_ins)
            f1 = each(one_pass, d_stricts, ks)
            dk3 = each(lambda a, kb: one_pass(a, kb, ta=True), d_stricts, kbs)
            fs = each(lambda a, b: a - b, f1, f2)
            dks = each(
                lambda a, b, c, beta, f: a + b + c + beta * f, dk1, dk2, dk3, betas, fs
            )
            for n, ((c, head), start) in enumerate(zip(chains, starts)):
                beta, e, f = betas[n], es[n], fs[n]
                d_beta = jnp.sum(f * ks[n] + e * vparts[n][0], axis=-1, keepdims=True)
                d_beta = jnp.where(col == head, d_beta * beta * (1.0 - beta), 0.0)
                if head:
                    d_beta = d_beta + db_low[pl.ds(start, BLOCK)].astype(F32)
                db_low[pl.ds(start, BLOCK)] = d_beta.astype(BF16)
                sq, rq, gq_in = qparts[n][0], rqs[n], (dq1[n] + dq2[n]) * scale
                through(
                    qparts[n],
                    rq * gq_in - sq * (rq * rq * rq * jnp.sum(sq * gq_in, axis=-1, keepdims=True)),
                    start, 0, head,
                )
                sk, rk, dk = kparts[n][0], rks[n], dks[n]
                through(
                    kparts[n],
                    rk * dk - sk * (rk * rk * rk * jnp.sum(sk * dk, axis=-1, keepdims=True)),
                    start, 1, head,
                )
                through(vparts[n], beta * e, start, 2, head)
        size = 4 if blocks % 4 == 0 else 1
        steps = blocks // size

        def before_convolution(head):
            @pl.loop(0, blocks)
            def _(c):
                start = pl.multiple_of(c * BLOCK, BLOCK)
                for part in range(3):
                    at = slice(part * width + head * BLOCK, part * width + (head + 1) * BLOCK)
                    window = dc[pl.ds(pl.multiple_of(start + 8, 8), BLOCK + 8), at]
                    total = conv[taps - 1 : taps, at] * window[0:BLOCK]
                    for j in range(taps - 1):
                        ahead = taps - 1 - j
                        total = total + conv[j : j + 1, at] * window[ahead : ahead + BLOCK]
                    dp_low[pl.ds(start, BLOCK), at] = total.astype(BF16)

        def projection_gradient(i, size, head):
            x = h[:, pl.ds(pl.multiple_of(i * size, size), size)]
            right = jnp.concatenate(
                [
                    dp_low[:, part * width + head * BLOCK : part * width + (head + 1) * BLOCK]
                    for part in range(3)
                ],
                axis=1,
            )
            total = dot(x, right, ta=True).astype(BF16)
            count = size // shard
            head_parts[head][pl.ds(i * count, count)] = total.reshape(count, shard, 3 * BLOCK)

        for head, reduce in enumerate(reduce_heads):
            pl.loop(0, steps)(partial(gradients, only=head))
            before_convolution(head)
            if flip:
                for k in [*range(1, reduce.outer), 0]:
                    projection_gradient(reduce.target(k), 2 * shard, head)
                    reduce.to_beside(k).start()
            else:
                pl.loop(0, model // tile)(partial(projection_gradient, size=tile, head=head))
                reduce.start()
            if head == 0:
                reduce_up.join_all()
                for k in range(1, mp):
                    swap_in(k).wait_recv()
                reduce_out.start()
            else:
                reduce_heads[head - 1].join_all()
        weight = qkv.reshape(model, 3 * width)

        def rows(index):
            at = pl.ds(pl.multiple_of(index * own, own), own)
            dh_part[index] = (
                dot(dp_low[at], weight[...], tb=True) + dot(db_low[at], beta_rows[...])
            ).astype(BF16)

        for k in [*range(1, reduce_h.outer), 0]:
            rows(reduce_h.given(k))
            reduce_h.to_beside(k).start()
            rows(reduce_h.kept(k))
            if k:
                reduce_h.join(k)
        reduce_out.join_all()
        reduce_heads[-1].join(1)
        d_beta = dot(db_low[...], h[...], ta=True)
        for g in range(heads * mp):
            line = d_beta[g % heads : g % heads + 1]
            small[g : g + 1] = jnp.where(column == g // heads, line, 0.0)
        for k in range(1, mp):
            swap(k, (column + k) % mp).wait_send()

    pl.run_scoped(
        mixer,
        *mixer_buffers,
        square,
        pltpu.VMEM((length, 3 * width), BF16),
        pltpu.VMEM((length, BLOCK), BF16),
    )
    for reduce, result in ((reduce_gate, d_gate), (reduce_up, d_up), (reduce_down, d_down)):
        result[...] = reduce.finish()
    output[...] = (y1[...] + reduce_y.finish()).astype(BF16)
    for k in range(2, reduce_heads[-1].outer):
        reduce_heads[-1].join(k)
    dh = reduce_h.finish()
    x = tokens[...].astype(F32)
    s = lax.rsqrt(jnp.mean(x * x, axis=-1, keepdims=True) + 1e-06)
    small[first_row : first_row + 1] = jnp.sum(dh * x * s, axis=0, keepdims=True)
    for d in range(dp):
        small_part[d, 0:gain_row] = small[0:gain_row, d * lanes : (d + 1) * lanes]
        small_part[d, gain_row + 1 :] = jnp.zeros((small_part.shape[1] - gain_row - 1, lanes), F32)
    reduce_small.start()
    scaled = first[...] * dh
    input_grad[...] += s * scaled - x * (
        s * s * s * jnp.mean(x * scaled, axis=-1, keepdims=True)
    )
    reduce_small.join_all()
    def share(slot, reduce):
        size = reduce.near.shape[2]
        low_at = shared.at[:, slot * 3 * BLOCK : slot * 3 * BLOCK + size]
        low_at[...] = reduce.finish().astype(BF16)
        gather = Gather(
            "mp",
            mp,
            low_at,
            lambda i: shared_all.at[i, :, slot * 3 * BLOCK : slot * 3 * BLOCK + size],
            share_sems,
            slot,
        )
        gather.start()
        return gather

    gathers = [share(heads, reduce_out)]
    for head in range(heads - 1):
        gathers.append(share(head, reduce_heads[head]))
    small_low[...] = reduce_small.finish()
    narrow = Gather("mp", mp, small_low, leading(small_sums), share_sems, heads + 1)
    narrow.start()
    gathers.append(share(heads - 1, reduce_heads[-1]))
    for g in gathers[:-1]:
        g.forward_all()
    narrow.forward_all()
    gathers[-1].forward_all()
    narrow.finish()
    small_total = small_sums[0]
    for i in range(1, mp):
        small_total = small_total + small_sums[i]
    d_small[...] = small_total
    for g in gathers:
        g.finish()
    ab_gather_done = (reduce_y, reduce_h, *over_dp)
    for reduce in ab_gather_done:
        reduce.sent()


def finish_kernel(mp, heads, *refs):
    take = Taker(refs)
    small, shared_in, *passed_in = take(7)
    passed, models, smalls = take(5), take(4), take(7)
    held = take(5)
    shared, wide, sems = take(3)
    width = heads * BLOCK
    loads = [
        pltpu.make_async_copy(src, dst, sems.at[i])
        for i, (src, dst) in enumerate(zip(passed_in, held))
    ]
    copies = [
        pltpu.make_async_copy(src, dst, sems.at[10 + i])
        for i, (src, dst) in enumerate(zip(held, passed))
    ]
    load = pltpu.make_async_copy(shared_in, shared, sems.at[5])
    load.start()
    for copy in loads:
        copy.start()
    line = 0
    for ref in smalls:
        ref[...] = small[line : line + ref.shape[0], 0 : ref.shape[1]]
        line += ref.shape[0]
    load.wait()
    for index, result in enumerate(models):
        for i in range(mp):
            for head in range(heads):
                at = head * 3 * BLOCK + index * BLOCK if index < 3 else 3 * width + head * BLOCK
                to = i * width + head * BLOCK
                wide[index, :, to : to + BLOCK] = shared[i, :, at : at + BLOCK].astype(F32)
        copies.append(pltpu.make_async_copy(wide.at[index], result, sems.at[6 + index]))
        copies[-1].start()
    for first, second in zip(loads, copies):
        first.wait()
        second.start()
    for copy in copies:
        copy.wait()


def call(kernel, ins, outs, scratch, collective, name, limit):
    return pl.pallas_call(
        kernel,
        out_shape=[jax.ShapeDtypeStruct(shape, kind) for _, shape, kind in outs],
        in_specs=[spec for spec, _ in ins],
        out_specs=[spec for spec, _, _ in outs],
        scratch_shapes=list(scratch),
        compiler_params=pltpu.CompilerParams(
            collective_id=collective,
            has_side_effects=collective is not None,
            vmem_limit_bytes=limit * MIB,
        ),
        name=name,
    )(*[array for _, array in ins])


def shards(
    dp,
    mp,
    tokens,
    cotangent,
    domain,
    domain_weight,
    query_weight,
    key_weight,
    value_weight,
    beta_weight,
    conv_query,
    conv_key,
    conv_value,
    out_gain,
    out_weight,
    norm_first,
    norm_second,
    gate_weight,
    up_weight,
    down_weight,
):
    own, model = tokens.shape
    length = own * mp
    shard = query_weight.shape[0]
    taps = conv_query.shape[0]
    all_heads = beta_weight.shape[1]
    heads = all_heads // mp
    width = model // mp
    feed = gate_weight.shape[1]
    lanes = norm_first.shape[0]
    gains = out_gain.shape[0]
    conv_row, gain_row = all_heads, all_heads + 3 * taps + 2
    first_row, second_row = gain_row - 2, gain_row - 1
    small_rows = -(-(gain_row + 1) // 8) * 8
    rows_of = (conv_row, first_row, second_row, gain_row)
    flip = lanes % 128 == 0

    square = ((heads * (length // BLOCK), BLOCK, BLOCK), F32)
    stored = [
        ((length, model), BF16),
        ((length + 16, 3 * width), F32),
        *[square] * 6,
        ((length, width), F32),
        ((length, width), BF16),
    ]
    feed_shape = (feed, model) if flip else (dp, shard, feed)
    feed_block = (feed, shard) if flip else (shard, feed)
    feed_grad = (VM, feed_block, F32)
    feed_own = (
        (gate_weight.T, up_weight.T, down_weight) if flip else (gate_weight, up_weight, down_weight.T)
    )
    token_rows = ((mp, own, model), BF16)
    sizes = (feed_block,) * 3 + ((shard, width),) + ((shard, 3 * BLOCK),) * heads
    results = call(
        partial(block_kernel, dp, mp, taps, heads, gains, flip, rows_of),
        [
            (SM, domain), (SM, domain_weight),
            (VM, tokens), (VM, cotangent), (ANY, query_weight), (ANY, key_weight), (ANY, value_weight),
            (ANY, out_weight),
            (VM, beta_weight.T), (VM, conv_query), (VM, conv_key), (VM, conv_value),
            (VM, norm_first[None]), (VM, norm_second[None]), (VM, out_gain[None]),
            *[(ANY, a) for a in feed_own],
        ],
        [
            (VM, (own, model), BF16),
            (VM, (own, model), F32),
            (VM, (mp, shard, 4 * width), BF16),
            (VM, (small_rows, lanes), F32),
            *[feed_grad] * 3,
            (ANY, *token_rows), *[(ANY, feed_shape, BF16)] * 3,
            *[(ANY, *kind) for kind in stored],
        ],
        [pltpu.VMEM(*token_rows)] * 4
        + [
            pltpu.VMEM((own, model), BF16),
            pltpu.VMEM((dp, shard, 3 * width), BF16),
            pltpu.VMEM((dp // mp, shard, model), BF16),
            pltpu.VMEM((dp, shard, width), BF16),
            pltpu.VMEM((own, model), F32),
            pltpu.VMEM((BLOCK, model), BF16),
            pltpu.VMEM((taps, 3 * width), F32),
            pltpu.VMEM((1, model), F32),
            pltpu.VMEM((1, model), F32),
            pltpu.VMEM((1, BLOCK), F32),
            pltpu.VMEM((length, BLOCK), F32),
        ]
        + [pltpu.VMEM(feed_shape, BF16)] * 3
        + [
            pltpu.VMEM((mp, dp // mp, shard, width), BF16),
            *[pltpu.VMEM((dp, shard, 3 * BLOCK), BF16)] * heads,
        ]
        + ReduceScatter.buffers(mp, own, model) * 2
        + [b for size in sizes for b in ReduceScatter.buffers(dp, *size)]
        + ReduceScatter.buffers(dp, small_rows, lanes, F32)
        + [
            pltpu.VMEM((small_rows, lanes), F32),
            pltpu.VMEM((dp, small_rows, lanes), F32),
            pltpu.VMEM((small_rows, model), F32),
            pltpu.VMEM((dp, small_rows, lanes), F32),
            pltpu.VMEM((small_rows, lanes), F32),
            pltpu.VMEM((mp, small_rows, lanes), F32),
            pltpu.VMEM((shard, 4 * width), BF16),
        ]
        + Gather.scratch(mp, 4)
        + Gather.scratch(dp, 9)
        + ReduceScatter.scratch(mp, 4)
        + ReduceScatter.scratch(dp, 5 + heads)
        + Gather.scratch(mp, 2 + heads)
        + [pltpu.SemaphoreType.DMA((mp,))] * 4
        + [
            pltpu.SemaphoreType.DMA((10,)),
            pltpu.SemaphoreType.DMA((10,)),
            pltpu.SemaphoreType.DMA((4,)),
        ],
        0,
        "block",
        63,
    )
    output, input_grad, shared, small, d_gate, d_up, d_down = results[:7]
    small_shapes = [(all_heads, lanes)] + [(taps, lanes)] * 3 + [(1, lanes)] * 2 + [(1, gains)]
    results = call(
        partial(finish_kernel, mp, heads),
        [(VM, small)] + [(ANY, a) for a in (shared, output, input_grad, d_gate, d_up, d_down)],
        [
            (ANY, (own, model), BF16),
            (ANY, (own, model), F32),
            *[(ANY, feed_block, F32)] * 3,
            *[(ANY, (shard, model), F32)] * 4,
            *[(VM, shape, F32) for shape in small_shapes],
        ],
        [
            pltpu.VMEM((own, model), BF16),
            pltpu.VMEM((own, model), F32),
            *[pltpu.VMEM(feed_block, F32)] * 3,
            pltpu.VMEM((mp, shard, 4 * width), BF16),
            pltpu.VMEM((4, shard, model), F32),
            pltpu.SemaphoreType.DMA((15,)),
        ],
        None,
        "finish",
        60,
    )
    output, input_grad, d_gate, d_up, d_down = results[:5]
    d_query, d_key, d_value, d_outw = results[5:9]
    d_beta, d_conv_q, d_conv_k, d_conv_v, d_first, d_second, d_gain = results[9:]
    if flip:
        d_gate, d_up = d_gate.T, d_up.T
    else:
        d_down = d_down.T
    return (
        output,
        input_grad,
        d_query,
        d_key,
        d_value,
        d_beta.T,
        d_conv_q,
        d_conv_k,
        d_conv_v,
        d_gain[0],
        d_outw,
        d_first[0],
        d_second[0],
        d_gate,
        d_up,
        d_down,
    )


def solution(mesh):
    dp, mp = mesh.shape["dp"], mesh.shape["mp"]
    weight = P("dp", None)
    split = P(None, "dp")
    rows = P(("dp", "mp"), None)
    return jax.shard_map(
        partial(shards, dp, mp),
        mesh=mesh,
        in_specs=(
            rows, rows, P("dp"), P(), weight, weight, weight, weight, split, split, split,
            P("dp"), weight, P("dp"), P("dp"), P("dp", "mp"), P("dp", "mp"), P("mp", "dp"),
        ),
        out_specs=(
            rows, rows, weight, weight, weight, weight, split, split, split,
            P("dp"), weight, P("dp"), P("dp"), P("dp", "mp"), P("dp", "mp"), P("mp", "dp"),
        ),
        check_vma=False,
    )
```

```python
from functools import partial

import jax
import jax.numpy as jnp
from jax import lax
from jax.experimental import pallas as pl
from jax.experimental.pallas import tpu as pltpu
from jax.sharding import PartitionSpec as P

BLOCK = 128
MESH = pl.DeviceIdType.MESH
F32 = jnp.float32
BF16 = jnp.bfloat16
MIB = 1 << 20
VM = pl.BlockSpec(memory_space=pltpu.VMEM)
ANY = pl.BlockSpec(memory_space=pl.ANY)
SM = pl.BlockSpec(memory_space=pltpu.SMEM)


def dot(a, b, ta=False, tb=False):
    dims = (((0 if ta else 1,), (1 if tb else 0,)), ((), ()))
    return lax.dot_general(a, b, dims, preferred_element_type=F32)


def halves(a):
    high = a.astype(BF16)
    return high, (a - high.astype(F32)).astype(BF16)


def mm(a, b, ta=False, tb=False):
    ah, al = halves(a)
    bh, bl = halves(b)
    da, db = 0 if ta else 1, 1 if tb else 0
    left = jnp.concatenate([ah, al], axis=da)
    right = jnp.concatenate([bh, bh], axis=db)
    columns = b.shape[1 - db]
    if columns > BLOCK:
        return dot(left, right, ta, tb) + dot(ah, bl, ta, tb)
    rest = jnp.concatenate([bl, jnp.zeros_like(bl)], axis=db)
    both = dot(left, jnp.concatenate([right, rest], axis=1 - db), ta, tb)
    return both[:, :columns] + both[:, columns:]


def one_pass(a, b, ta=False, tb=False):
    return dot(a.astype(BF16), b.astype(BF16), ta, tb)


def each(function, *lists):
    return [function(*items) for items in zip(*lists)]


def iota2(size):
    return (
        lax.broadcasted_iota(jnp.int32, (size, size), 0),
        lax.broadcasted_iota(jnp.int32, (size, size), 1),
    )


def unit_lower_inverses(stricts):
    size = stricts[0].shape[0]
    row, col = iota2(size)
    pairs = (row >> 1) == (col >> 1)
    unit = jnp.where(row == col, 1.0, 0.0)
    inverses = each(lambda a: unit - jnp.where(pairs, a, 0.0), stricts)
    shift = 1
    while (1 << shift) < size:
        inside = (row >> (shift + 1)) == (col >> (shift + 1))
        apart = (row >> shift) != (col >> shift)
        corner = inside & apart
        moved = each(lambda x, a: mm(x, jnp.where(corner, a, 0.0)), inverses, stricts)
        moved = each(mm, moved, inverses)
        inverses = each(lambda x, t: x - t, inverses, moved)
        shift += 1
    return inverses


def sigmoid(a):
    return 1.0 / (1.0 + jnp.exp(-a))


class Gather:
    def __init__(self, axis, count, src, place, sems, slot):
        self.axis, self.src, self.place = axis, src, place
        self.outer = count // 2
        self.me = lax.axis_index(axis)
        self.a, self.b = self.me // 2, self.me % 2
        self.sa, self.ra, self.sb, self.rb, self.local = (s.at[slot] for s in sems)
        self.beside = self.a * 2 + 1 - self.b

    @staticmethod
    def scratch(count, slots):
        return [pltpu.SemaphoreType.DMA((slots, count // 2))] * 4 + [
            pltpu.SemaphoreType.DMA((slots, 1))
        ]

    def copy(self, src, block, send, recv, target):
        return pltpu.make_async_remote_copy(
            src_ref=src,
            dst_ref=self.place(block),
            send_sem=send,
            recv_sem=recv,
            device_id={self.axis: target},
            device_id_type=MESH,
        )

    def own(self):
        return pltpu.make_async_copy(self.src, self.place(self.me), self.local.at[0])

    def source(self, k):
        return (self.a + self.outer - k) % self.outer * 2 + self.b

    def source_beside(self, k):
        return (self.a + self.outer - k) % self.outer * 2 + 1 - self.b

    def to_outer(self, k):
        target = (self.a + k) % self.outer * 2 + self.b
        return self.copy(self.src, self.me, self.sa.at[k], self.ra.at[k], target)

    def to_beside(self, k):
        block = self.source(k)
        src = self.src if k == 0 else self.place(block)
        return self.copy(src, block, self.sb.at[k], self.rb.at[k], self.beside)

    def start_outer(self):
        for k in range(1, self.outer):
            self.to_outer(k).start()

    def start_beside(self):
        self.to_beside(0).start()
        self.own().start()

    def start(self):
        self.start_outer()
        self.start_beside()

    def forward(self, k):
        self.to_outer(k).wait_recv()
        self.to_beside(k).start()

    def forward_all(self):
        for k in range(1, self.outer):
            self.forward(k)

    def arrived(self, k):
        self.to_beside(k).wait_recv()

    def sent(self):
        for k in range(self.outer):
            if k:
                self.to_outer(k).wait_send()
            self.to_beside(k).wait_send()

    def finish(self):
        self.own().wait()
        for k in range(self.outer):
            self.arrived(k)
        self.sent()


class ReduceScatter:
    def __init__(self, axis, count, place, near, far, sems, slot):
        self.axis, self.place, self.near, self.far = axis, place, near, far
        self.outer = count // 2
        self.me = lax.axis_index(axis)
        self.a, self.b = self.me // 2, self.me % 2
        self.sa, self.ra, self.sb, self.rb = (s.at[slot] for s in sems)
        self.beside = self.a * 2 + 1 - self.b

    @staticmethod
    def scratch(count, slots):
        return [pltpu.SemaphoreType.DMA((slots, count // 2))] * 4

    @staticmethod
    def buffers(count, rows, columns, kind=BF16):
        return [pltpu.VMEM((count // 2, rows, columns), kind)] * 2

    def target(self, k):
        return (self.a + k) % self.outer

    def kept(self, k):
        return self.target(k) * 2 + self.b

    def given(self, k):
        return self.target(k) * 2 + 1 - self.b

    def to_beside(self, k):
        return pltpu.make_async_remote_copy(
            src_ref=self.place(self.given(k)),
            dst_ref=self.near.at[k],
            send_sem=self.sb.at[k],
            recv_sem=self.rb.at[k],
            device_id={self.axis: self.beside},
            device_id_type=MESH,
        )

    def to_outer(self, k):
        return pltpu.make_async_remote_copy(
            src_ref=self.place(self.kept(k)),
            dst_ref=self.far.at[k],
            send_sem=self.sa.at[k],
            recv_sem=self.ra.at[k],
            device_id={self.axis: self.target(k) * 2 + self.b},
            device_id_type=MESH,
        )

    def start(self):
        for k in [*range(1, self.outer), 0]:
            self.to_beside(k).start()

    def join(self, k):
        self.to_beside(k).wait_recv()
        block = self.place(self.kept(k))
        total = block[...].astype(F32) + self.near[k].astype(F32)
        if k == 0:
            return total
        block[...] = total.astype(block.dtype)
        self.to_outer(k).start()

    def join_all(self):
        for k in range(1, self.outer):
            self.join(k)

    def finish(self):
        total = self.join(0)
        for k in range(1, self.outer):
            self.to_outer(k).wait_recv()
            total = total + self.far[k].astype(F32)
        return total

    def sent(self):
        for k in range(self.outer):
            self.to_beside(k).wait_send()
            if k:
                self.to_outer(k).wait_send()


def leading(ref):
    return lambda i: ref.at[i]


def columns_of(ref, size):
    return lambda i: ref.at[:, pl.ds(pl.multiple_of(i * size, size), size)]


def greet(counts):
    barrier = pltpu.get_barrier_semaphore()
    for axis, count in counts:
        me = lax.axis_index(axis)
        for k in range(1, count):
            pl.semaphore_signal(
                barrier, inc=1, device_id={axis: (me + k) % count}, device_id_type=MESH
            )
    pl.semaphore_wait(barrier, sum(count - 1 for _, count in counts))


class Taker:
    def __init__(self, refs):
        self.refs, self.cursor = refs, 0

    def __call__(self, count):
        self.cursor += count
        return self.refs[self.cursor - count : self.cursor]

    def one(self):
        return self(1)[0]


def activated(p, conv, start, part, head, width, taps):
    columns = slice(part * width + head * BLOCK, part * width + (head + 1) * BLOCK)
    window = p[pl.ds(start, BLOCK + 8), columns]
    shifted = [window[8 - taps + 1 + j : 8 - taps + 1 + j + BLOCK] for j in range(taps)]
    pre = conv[0:1, columns] * shifted[0]
    for j in range(1, taps):
        pre = pre + conv[j : j + 1, columns] * shifted[j]
    gate = sigmoid(pre)
    return pre * gate, gate, shifted


def inverse_norm(s):
    return lax.rsqrt(jnp.sum(s * s, axis=-1, keepdims=True) + 1e-06)


def place_lanes(index, count, lanes, gains):
    row = lax.broadcasted_iota(jnp.int32, (lanes, count * gains), 0)
    col = lax.broadcasted_iota(jnp.int32, (lanes, count * gains), 1)
    return jnp.where((col == row + index * gains) & (row < gains), 1.0, 0.0)


def block_kernel(dp, mp, taps, heads, gains, flip, rows_of, *refs):
    take = Taker(refs)
    domain, domain_weight = take(2)
    tokens, cot = take(2)
    projections, smalls = take(4), take(7)
    gate_own, up_own, down_own = take(3)
    output, input_grad, shared_all, d_small, d_gate, d_up, d_down = take(7)
    cot_all, gate_all, up_all, down_all = take(4)
    stored = take(10)
    rows_all, ab_all, y_part, dh_part, low = take(5)
    qkv, out_rows, out_columns = take(3)
    y1, beta_rows, conv, first, second, gain, beta_pre = take(7)
    gate_part, up_part, down_part, out_part = take(4)
    head_parts = take(heads)
    near_y, far_y, near_h, far_h = take(4)
    buffers = [take(2) for _ in range(5 + heads)]
    small_own, small_all, small, small_part, small_low, small_sums = take(6)
    shared = take.one()
    first_part, first_in, first_low, first_sums, first_sems, share_first = take(6)
    sems_mp, sems_dp, reduce_sems, dp_sems, share_sems = take(5), take(5), take(4), take(4), take(5)
    rows_send, rows_recv, swap_send, swap_recv, saved_sem, load_sem, feed_sem = take(7)
    conv_row, first_row, second_row, gain_row = rows_of
    own, model = tokens.shape
    length = own * mp
    shard = model // dp
    width = heads * BLOCK
    blocks = length // BLOCK
    lanes = small_own.shape[1]
    feed = gate_own.shape[0] if flip else gate_own.shape[1]
    per = dp // mp
    column = lax.axis_index("mp")
    mine = pl.ds(pl.multiple_of(column * width, BLOCK), width)
    tile, wide_tile = 256, 512
    row, col = iota2(BLOCK)
    scale = BLOCK**-0.5
    group = 4 if blocks % 4 == 0 else 1
    loss_scale = jnp.zeros((1, 1), F32)
    for i in range(domain_weight.shape[0]):
        loss_scale = loss_scale + jnp.where(domain[0] == i, domain_weight[i], 0.0)

    small_own[...] = jnp.zeros_like(small_own)
    line = 0
    for ref in smalls:
        small_own[line : line + ref.shape[0], 0 : ref.shape[1]] = ref[...].astype(F32)
        line += ref.shape[0]

    greet((("dp", dp), ("mp", mp)))
    small_gather = Gather("dp", dp, small_own, leading(small_all), sems_dp, 0)
    places = [lambda d, i=i: qkv.at[d, :, i * width : (i + 1) * width] for i in range(3)]
    *qkv_gathers, out_gather = [
        Gather("dp", dp, src.at[:, mine], place, sems_dp, 1 + i)
        for i, (src, place) in enumerate(zip(projections, [*places, leading(out_columns)]))
    ]
    token_gather = Gather("mp", mp, tokens, leading(rows_all), sems_mp, 0)
    cot_gather = Gather("mp", mp, cot, leading(cot_all), sems_mp, 1)
    def feed_gather(src, dst, rows, slot):
        if flip:
            place = lambda d: dst.at[rows, pl.ds(pl.multiple_of(d * lanes, lanes), lanes)]
            return Gather("dp", dp, src.at[rows], place, sems_dp, slot)
        return Gather(
            "dp", dp, src.at[:, rows], lambda d: dst.at[d, :, rows], sems_dp, slot
        )

    whole, cut = slice(0, feed), feed // 256 * 128
    feed_gathers = [
        feed_gather(gate_own, gate_all, whole, 5),
        feed_gather(up_own, up_all, whole, 6),
        feed_gather(down_own, down_all, slice(0, cut), 7),
        feed_gather(down_own, down_all, slice(cut, feed), 8),
    ]
    small_gather.start()
    qkv_gathers[0].start()
    token_gather.start()
    small_gather.forward_all()
    qkv_gathers[0].forward(1)
    qkv_gathers[1].start()
    for k in range(2, qkv_gathers[0].outer):
        qkv_gathers[0].forward(k)
    qkv_gathers[1].forward(1)
    qkv_gathers[2].start()
    for k in range(2, qkv_gathers[1].outer):
        qkv_gathers[1].forward(k)
    token_gather.forward_all()
    qkv_gathers[2].forward(1)
    out_gather.start_outer()
    feed_gathers[0].start_outer()
    for k in range(2, qkv_gathers[2].outer):
        qkv_gathers[2].forward(k)
    cot_gather.start()
    small_gather.finish()

    for d in range(dp):
        small[:, d * lanes : (d + 1) * lanes] = small_all[d]
    beta_rows[...] = jnp.zeros_like(beta_rows)
    picked = []
    for head in range(heads):
        wanted = jnp.zeros((1, model), F32)
        for g in range(heads * mp):
            wanted = jnp.where(column * heads + head == g, small[g : g + 1], wanted)
        picked.append(wanted)
    beta_rows[0:16] = jnp.concatenate(
        picked + [jnp.zeros((16 - heads, model), F32)], axis=0
    ).astype(BF16)
    for i in range(3):
        for j in range(taps):
            at = conv_row + i * taps + j
            conv[j : j + 1, i * width : (i + 1) * width] = small[at : at + 1, mine]
    first[...] = small[first_row : first_row + 1]
    second[...] = small[second_row : second_row + 1]
    total = jnp.zeros((8, dp * gains), F32)
    for d in range(dp):
        line = jnp.broadcast_to(small_all[d, gain_row : gain_row + 1], (8, lanes))
        total = total + dot(line.astype(BF16), place_lanes(d, dp, lanes, gains).astype(BF16))
    gain[...] = total[0:1]

    token_gather.finish()
    h2_gather = Gather("mp", mp, low, leading(rows_all), sems_mp, 2)
    ab_gather = Gather("mp", mp, low, leading(ab_all), sems_mp, 3)
    reduce_part = ReduceScatter("mp", mp, leading(y_part), near_y, far_y, reduce_sems, 0)
    reduce_h2 = ReduceScatter("mp", mp, leading(dh_part), near_h, far_h, reduce_sems, 1)
    reduce_y = ReduceScatter("mp", mp, leading(y_part), near_y, far_y, reduce_sems, 2)
    reduce_h = ReduceScatter("mp", mp, leading(dh_part), near_h, far_h, reduce_sems, 3)
    over_dp = [
        ReduceScatter(
            "dp",
            dp,
            columns_of(part, shard) if flip and slot < 3 else leading(part),
            *pair,
            dp_sems,
            slot,
        )
        for slot, (part, pair) in enumerate(
            zip((gate_part, up_part, down_part, out_columns, *head_parts, small_part), buffers)
        )
    ]
    reduce_gate, reduce_up, reduce_down, reduce_out, *reduce_heads, reduce_small = over_dp

    def mixer_forward(
        h, p, inverse, w, scores, step, delta, state, o, m, u, offset, q_all
    ):
        saved = (h, p, inverse, w, scores, step, delta, state, o, m)
        for i in range(mp):
            x = rows_all[i].astype(F32)
            normed = x * lax.rsqrt(jnp.mean(x * x, axis=-1, keepdims=True) + 1e-06) * first[...]
            h[i * own : (i + 1) * own] = normed.astype(BF16)
        for g in qkv_gathers:
            g.finish()
        out_gather.start_beside()
        for g in feed_gathers:
            g.start_beside()

        p[0:8] = jnp.zeros((8, p.shape[1]), F32)
        p[length + 8 :] = jnp.zeros((8, p.shape[1]), F32)
        weight = qkv.reshape(model, 3 * width)

        @pl.loop(0, mp)
        def _(i):
            at = pl.ds(pl.multiple_of(i * own, own), own)
            low = h[at]
            p[pl.ds(pl.multiple_of(i * own + 8, 8), own)] = dot(low, weight[...])
            beta_pre[at] = dot(low, beta_rows[...], tb=True)

        def save(index):
            return pltpu.make_async_copy(saved[index], stored[index], saved_sem.at[index])

        for index in (0, 1):
            save(index).start()


        def prepare(i):
            chains = [(i * group + j, head) for j in range(group) for head in range(heads)]
            starts = [pl.multiple_of(c * BLOCK, BLOCK) for c, _ in chains]
            places = [head * blocks + c for c, head in chains]
            ks, kbs, vbs, qs = [], [], [], []
            for (c, head), start in zip(chains, starts):
                s, _, _ = activated(p, conv, start, 0, head, width, taps)
                qs.append(s * (inverse_norm(s) * scale))
                s, _, _ = activated(p, conv, start, 1, head, width, taps)
                k = s * inverse_norm(s)
                v, _, _ = activated(p, conv, start, 2, head, width, taps)
                beta = sigmoid(beta_pre[pl.ds(start, BLOCK), head : head + 1])
                ks.append(k)
                kbs.append(k * beta)
                vbs.append(v * beta)
            for place, q in zip(places, qs):
                q_all[place] = q
            stricts = each(lambda a, b: jnp.where(row > col, mm(a, b, tb=True), 0.0), kbs, ks)
            for place, a in zip(places, each(lambda q, k: mm(q, k, tb=True), qs, ks)):
                scores[place] = jnp.where(row >= col, a, 0.0)
            xs = unit_lower_inverses(stricts)
            for place, x in zip(places, xs):
                inverse[place] = x
            wus = each(lambda x, a, b: mm(x, jnp.concatenate([a, b], axis=1)), xs, kbs, vbs)
            for place, wu in zip(places, wus):
                w[place] = wu[:, :BLOCK]
                u[place] = wu[:, BLOCK:]
            for place, gb in zip(places, each(lambda k, wu: mm(k, wu, ta=True), ks, wus)):
                step[place] = gb[:, :BLOCK]
                offset[place] = gb[:, BLOCK:]

        def swap(k, block, source):
            columns = pl.ds(pl.multiple_of(source * width, BLOCK), width)
            return pltpu.make_async_remote_copy(
                src_ref=out_columns.at[pl.ds(block * per, per)],
                dst_ref=out_rows.at[:, :, columns],
                send_sem=rows_send.at[k],
                recv_sem=rows_recv.at[k],
                device_id={"mp": (column + k) % mp},
                device_id_type=MESH,
            )

        half = blocks // group // 2
        pl.loop(0, half)(prepare)
        out_gather.forward_all()
        feed_gathers[1].start_outer()
        pl.loop(half, blocks // group)(prepare)
        for index in (2, 3, 4, 5):
            save(index).start()
        feed_gathers[0].forward_all()
        cot_gather.forward_all()
        out_gather.finish()
        for k in range(1, mp):
            swap(k, (column + k) % mp, column).start()
        out_rows[:, :, mine] = out_columns[pl.ds(column * per, per)]

        def advance(c, states):
            places = [head * blocks + c for head in range(heads)]
            for place, s in zip(places, states):
                state[place] = s
            moved = each(lambda place, s: mm(step[place], s), places, states)
            return tuple(each(lambda place, s, t: s - t + offset[place], places, states, moved))

        states = tuple(jnp.zeros((BLOCK, BLOCK), F32) for _ in range(heads))
        for c in range(blocks):
            states = advance(c, states)
        save(7).start()

        for k in range(1, mp):
            swap(k, column, (column + mp - k) % mp).wait_recv()
        out_weight = out_rows.reshape(width, model)

        def outputs(index):
            per = own // BLOCK
            chains = [(index * per + j, head) for j in range(per) for head in range(heads)]
            places = [head * blocks + c for c, head in chains]
            boths = each(
                lambda at: mm(jnp.concatenate([w[at], q_all[at]], axis=0), state[at]), places
            )
            ds = each(lambda at, both: u[at] - both[:BLOCK], places, boths)
            for place, d in zip(places, ds):
                delta[place] = d
            outs = each(lambda at, d: mm(scores[at], d), places, ds)
            outs = each(lambda both, out: both[BLOCK:] + out, boths, outs)
            for (c, head), out in zip(chains, outs):
                rows = pl.ds(pl.multiple_of(c * BLOCK, BLOCK), BLOCK)
                at = slice(head * BLOCK, (head + 1) * BLOCK)
                o[rows, at] = out
                r = lax.rsqrt(jnp.mean(out * out, axis=-1, keepdims=True) + 1e-05)
                m[rows, at] = (out * r * gain[...]).astype(BF16)
            at = pl.ds(pl.multiple_of(index * own, own), own)
            y_part[index] = dot(m[at], out_weight[...]).astype(BF16)

        for k in [*range(1, reduce_part.outer), 0]:
            outputs(reduce_part.given(k))
            reduce_part.to_beside(k).start()
            outputs(reduce_part.kept(k))
            if k:
                reduce_part.join(k)
        for index in (6, 8, 9):
            save(index).start()
        feed_gathers[2].start_outer()
        feed_gathers[3].start_outer()
        feed_gathers[1].forward_all()
        y = tokens[...].astype(F32) + reduce_part.finish()
        y1[...] = y
        low[...] = (
            y * lax.rsqrt(jnp.mean(y * y, axis=-1, keepdims=True) + 1e-06) * second[...]
        ).astype(BF16)
        h2_gather.start()
        for g in feed_gathers[2:]:
            g.forward_all()
        reduce_part.sent()
        for k in range(1, mp):
            swap(k, (column + k) % mp, column).wait_send()
        for index in range(10):
            save(index).wait()

    square = pltpu.VMEM((heads * blocks, BLOCK, BLOCK), F32)
    mixer_buffers = [
        pltpu.VMEM((length, model), BF16),
        pltpu.VMEM((length + 16, 3 * width), F32),
        *[square] * 6,
        pltpu.VMEM((length, width), F32),
        pltpu.VMEM((length, width), BF16),
    ]
    pl.run_scoped(mixer_forward, *mixer_buffers, square, square, square)

    def feed_forward(gate, up, down, gb, z, dg, du):
        def load(index):
            src, dst = ((gate_all, gate), (up_all, up), (down_all, down), (cot_all, gb))[index]
            return pltpu.make_async_copy(src, dst, feed_sem.at[index])

        gate_w, up_w, down_w = (
            a if flip else a.reshape(model, feed) for a in (gate, up, down)
        )

        def hidden_rows(index):
            at = pl.ds(pl.multiple_of(index * own, own), own)
            x = rows_all[index]
            g = dot(x, gate_w[...], tb=flip)
            u = dot(x, up_w[...], tb=flip)
            sg = sigmoid(g)
            silu = g * sg
            z[at] = (silu * u).astype(BF16)
            dg[at] = (u * (sg + silu * (1.0 - sg))).astype(BF16)
            du[at] = silu.astype(BF16)

        def result_rows(index):
            at = pl.ds(pl.multiple_of(index * own, own), own)
            dz = dot(gb[index], down_w[...], tb=flip)
            dgl = (dz * dg[at].astype(F32)).astype(BF16)
            dul = (dz * du[at].astype(F32)).astype(BF16)
            dg[at] = dgl
            du[at] = dul
            dh_part[index] = (
                dot(dgl, gate_w[...], tb=not flip) + dot(dul, up_w[...], tb=not flip)
            ).astype(BF16)
            y_part[index] = dot(z[at], down_w[...], tb=not flip).astype(BF16)

        def weight_gradient(part, left, right, reduce):
            @pl.loop(0, model // wide_tile)
            def _(i):
                at = pl.ds(pl.multiple_of(i * wide_tile, wide_tile), wide_tile)
                x = left[:, :, at].reshape(length, wide_tile)
                if flip:
                    part[:, at] = dot(right[...], x, ta=True).astype(BF16)
                else:
                    total = dot(x, right[...], ta=True).astype(BF16)
                    count = wide_tile // shard
                    part[pl.ds(i * count, count)] = total.reshape(count, shard, feed)

            reduce.start()

        outer = h2_gather.outer
        cot_gather.finish()
        load(3).start()
        for index in range(2):
            feed_gathers[index].finish()
            load(index).start()
        for index in (3, 0, 1):
            load(index).wait()
        gb[...] = (gb[...].astype(F32) * loss_scale).astype(BF16)
        h2_gather.own().wait()
        hidden_rows(h2_gather.me)
        h2_gather.arrived(0)
        hidden_rows(h2_gather.beside)
        for k in range(1, outer):
            h2_gather.forward(k)
            hidden_rows(h2_gather.source(k))
            h2_gather.arrived(k)
            hidden_rows(h2_gather.source_beside(k))
        for g in feed_gathers[2:]:
            g.finish()
        load(2).start()
        load(2).wait()
        for k in [*range(1, outer), 0]:
            result_rows(reduce_h2.given(k))
            reduce_h2.to_beside(k).start()
            reduce_y.to_beside(k).start()
            result_rows(reduce_h2.kept(k))
            if k:
                reduce_h2.join(k)
        weight_gradient(down_part, gb, z, reduce_down)
        weight_gradient(gate_part, rows_all, dg, reduce_gate)
        weight_gradient(up_part, rows_all, du, reduce_up)

    weights = pltpu.VMEM((feed, model) if flip else (dp, shard, feed), BF16)
    hidden = pltpu.VMEM((length, feed), BF16)
    pl.run_scoped(
        feed_forward,
        weights,
        weights,
        weights,
        pltpu.VMEM((mp, own, model), BF16),
        hidden,
        hidden,
        hidden,
    )
    h2_gather.sent()

    def mixer(
        h, p, inverse, w, scores, step, delta, state, o, m, ds_all, dp_low, db_low,
    ):
        do, entry, dc = o, w, p
        targets = (h, p, inverse, w, scores, step, delta, state, o, m)

        def load(index):
            return pltpu.make_async_copy(stored[index], targets[index], load_sem.at[index])

        for index in (1, 4, 3, 8, 9, 5, 2, 6, 7, 0):
            load(index).start()

        dh = reduce_h2.finish()
        y = y1[...]
        r = lax.rsqrt(jnp.mean(y * y, axis=-1, keepdims=True) + 1e-06)
        small[...] = jnp.zeros_like(small)
        small[second_row : second_row + 1] = jnp.sum(dh * y * r, axis=0, keepdims=True)
        scaled = second[...] * dh
        grad = (
            cot[...].astype(F32) * loss_scale
            + r * scaled
            - y * (r * r * r * jnp.mean(y * scaled, axis=-1, keepdims=True))
        )
        input_grad[...] = grad
        low[...] = grad.astype(BF16)
        ab_gather.start()
        reduce_h2.sent()
        reduce_down.join_all()

        for index in (1, 4, 3):
            load(index).wait()
        dc[length + 8 :] = jnp.zeros((8, dc.shape[1]), F32)

        def chains_of(i, size):
            chains = [(i * size + j, head) for j in range(size) for head in range(heads)]
            starts = [pl.multiple_of(c * BLOCK, BLOCK) for c, _ in chains]
            places = [head * blocks + c for c, head in chains]
            return chains, starts, places

        def lane(head):
            return slice(head * BLOCK, (head + 1) * BLOCK)

        @pl.loop(0, blocks // group)
        def _(i):
            chains, starts, places = chains_of(i, group)
            moved = each(lambda at: mm(scores[at], w[at]), places)
            for (c, head), start, place, t in zip(chains, starts, places, moved):
                s, _, _ = activated(p, conv, start, 0, head, width, taps)
                ds_all[place] = s * (inverse_norm(s) * scale) - t

        for index in (8, 9, 5):
            load(index).wait()
        out_weight = out_rows.reshape(width, model)

        def output_gradients(index, d_gain):
            dm = dot(ab_all[index], out_weight[...], tb=True)
            at = pl.ds(pl.multiple_of(index * own, own), own)
            for head in range(heads):
                x = o[at, lane(head)]
                g = dm[:, lane(head)]
                r = lax.rsqrt(jnp.mean(x * x, axis=-1, keepdims=True) + 1e-05)
                d_gain = d_gain + jnp.sum(g * x * r, axis=0, keepdims=True)
                scaled = g * gain[...]
                do[at, lane(head)] = r * scaled - x * (
                    r * r * r * jnp.mean(x * scaled, axis=-1, keepdims=True)
                )
            return d_gain

        ab_gather.own().wait()
        d_gain = output_gradients(ab_gather.me, jnp.zeros((1, BLOCK), F32))
        ab_gather.arrived(0)
        d_gain = output_gradients(ab_gather.beside, d_gain)
        for k in range(1, ab_gather.outer):
            ab_gather.forward(k)
            if k == 1:
                reduce_y.join_all()
            d_gain = output_gradients(ab_gather.source(k), d_gain)
            ab_gather.arrived(k)
            d_gain = output_gradients(ab_gather.source_beside(k), d_gain)
        ab_gather.sent()
        for d in range(dp):
            moved = mm(
                jnp.broadcast_to(d_gain, (8, BLOCK)), place_lanes(d, dp, lanes, gains), tb=True
            )
            small_part[d, gain_row : gain_row + 1] = moved[0:1]
        @pl.loop(0, mp)
        def _(i):
            x = ab_all[:, :, pl.ds(pl.multiple_of(i * width, BLOCK), width)].reshape(length, width)
            out_part[i] = dot(m[...], x, ta=True).astype(BF16).reshape(per, shard, width)

        def swap(k, block):
            return pltpu.make_async_remote_copy(
                src_ref=out_part.at[block],
                dst_ref=out_columns.at[pl.ds(column * per, per)],
                send_sem=swap_send.at[k],
                recv_sem=swap_recv.at[k],
                device_id={"mp": (column + k) % mp},
                device_id_type=MESH,
            )

        def swap_in(k):
            source = (column + mp - k) % mp
            return pltpu.make_async_remote_copy(
                src_ref=out_part.at[source],
                dst_ref=out_columns.at[pl.ds(source * per, per)],
                send_sem=swap_send.at[k],
                recv_sem=swap_recv.at[k],
                device_id={"mp": (column + k) % mp},
                device_id_type=MESH,
            )

        for k in range(1, mp):
            swap(k, (column + k) % mp).start()
        out_columns[pl.ds(column * per, per)] = out_part[column]

        @pl.loop(0, blocks // group)
        def _(i):
            chains, starts, places = chains_of(i, group)
            grads = [do[pl.ds(start, BLOCK), lane(head)] for (_, head), start in zip(chains, starts)]
            for place, t in zip(places, each(lambda at, g: mm(ds_all[at], g, ta=True), places, grads)):
                entry[place] = t

        def retreat(i, grads):
            places = [head * blocks + blocks - 1 - i for head in range(heads)]
            for place, g in zip(places, grads):
                ds_all[place] = g
            moved = each(lambda at, g: mm(step[at], g, ta=True), places, grads)
            return tuple(each(lambda at, g, t: g - t + entry[at], places, grads, moved))

        grads = tuple(jnp.zeros((BLOCK, BLOCK), F32) for _ in range(heads))
        for i in range(blocks):
            grads = retreat(i, grads)
        for index in (2, 6, 7, 0):
            load(index).wait()
        reduce_gate.join_all()
        d_conv = small
        conv_lanes = pl.ds(pl.multiple_of(column * width, BLOCK), width)

        def through(parts, grad, start, part, head):
            s, gate, shifted = parts
            columns = slice(part * width + head * BLOCK, part * width + (head + 1) * BLOCK)
            d_pre = grad * (gate + s * (1.0 - gate))
            dc[pl.ds(pl.multiple_of(start + 8, 8), BLOCK), columns] = d_pre
            at = pl.ds(pl.multiple_of(column * width + head * BLOCK, BLOCK), BLOCK)
            for j in range(taps):
                line = conv_row + part * taps + j
                d_conv[line : line + 1, at] += jnp.sum(d_pre * shifted[j], axis=0, keepdims=True)

        def gradients(i, only):
            chains = [((steps - 1 - i) * size + j, only) for j in range(size)]
            starts = [pl.multiple_of(c * BLOCK, BLOCK) for c, _ in chains]
            places = [head * blocks + c for c, head in chains]
            qparts, kparts, vparts = (
                [
                    activated(p, conv, start, part, head, width, taps)
                    for (_, head), start in zip(chains, starts)
                ]
                for part in range(3)
            )
            rqs = [inverse_norm(s) for s, _, _ in qparts]
            rks = [inverse_norm(s) for s, _, _ in kparts]
            qs = [part[0] * (r * scale) for part, r in zip(qparts, rqs)]
            ks = [part[0] * r for part, r in zip(kparts, rks)]
            betas = [
                sigmoid(beta_pre[pl.ds(start, BLOCK), head : head + 1])
                for (_, head), start in zip(chains, starts)
            ]
            kbs = each(lambda k, beta: k * beta, ks, betas)
            d_os = [do[pl.ds(start, BLOCK), lane(head)] for (_, head), start in zip(chains, starts)]
            deltas = [delta[at] for at in places]
            s_ins = [state[at] for at in places]
            ds_outs = [ds_all[at] for at in places]
            t1 = each(lambda at, g: one_pass(scores[at], g, ta=True), places, d_os)
            t2 = each(one_pass, ks, ds_outs)
            d_scores = each(
                lambda g, d: jnp.where(row >= col, one_pass(g, d, tb=True), 0.0), d_os, deltas
            )
            dq1 = each(lambda g, s: one_pass(g, s, tb=True), d_os, s_ins)
            es = each(lambda at, a, b: one_pass(inverse[at], a + b, ta=True), places, t1, t2)
            dq2 = each(one_pass, d_scores, ks)
            dk1 = each(lambda a, q: one_pass(a, q, ta=True), d_scores, qs)
            d_stricts = each(
                lambda e, d: jnp.where(row > col, -one_pass(e, d, tb=True), 0.0), es, deltas
            )
            dk2 = each(lambda d, s: one_pass(d, s, tb=True), deltas, ds_outs)
            f2 = each(lambda e, s: one_pass(e, s, tb=True), es, s_ins)
            f1 = each(one_pass, d_stricts, ks)
            dk3 = each(lambda a, kb: one_pass(a, kb, ta=True), d_stricts, kbs)
            fs = each(lambda a, b: a - b, f1, f2)
            dks = each(
                lambda a, b, c, beta, f: a + b + c + beta * f, dk1, dk2, dk3, betas, fs
            )
            for n, ((c, head), start) in enumerate(zip(chains, starts)):
                beta, e, f = betas[n], es[n], fs[n]
                d_beta = jnp.sum(f * ks[n] + e * vparts[n][0], axis=-1, keepdims=True)
                d_beta = jnp.where(col == head, d_beta * beta * (1.0 - beta), 0.0)
                if head:
                    d_beta = d_beta + db_low[pl.ds(start, BLOCK)].astype(F32)
                db_low[pl.ds(start, BLOCK)] = d_beta.astype(BF16)
                sq, rq, gq_in = qparts[n][0], rqs[n], (dq1[n] + dq2[n]) * scale
                through(
                    qparts[n],
                    rq * gq_in - sq * (rq * rq * rq * jnp.sum(sq * gq_in, axis=-1, keepdims=True)),
                    start, 0, head,
                )
                sk, rk, dk = kparts[n][0], rks[n], dks[n]
                through(
                    kparts[n],
                    rk * dk - sk * (rk * rk * rk * jnp.sum(sk * dk, axis=-1, keepdims=True)),
                    start, 1, head,
                )
                through(vparts[n], beta * e, start, 2, head)
        size = 4 if blocks % 4 == 0 else 1
        steps = blocks // size

        def before_convolution(head):
            @pl.loop(0, blocks)
            def _(c):
                start = pl.multiple_of(c * BLOCK, BLOCK)
                for part in range(3):
                    at = slice(part * width + head * BLOCK, part * width + (head + 1) * BLOCK)
                    window = dc[pl.ds(pl.multiple_of(start + 8, 8), BLOCK + 8), at]
                    total = conv[taps - 1 : taps, at] * window[0:BLOCK]
                    for j in range(taps - 1):
                        ahead = taps - 1 - j
                        total = total + conv[j : j + 1, at] * window[ahead : ahead + BLOCK]
                    dp_low[pl.ds(start, BLOCK), at] = total.astype(BF16)

        def projection_gradient(i, size, head):
            x = h[:, pl.ds(pl.multiple_of(i * size, size), size)]
            right = jnp.concatenate(
                [
                    dp_low[:, part * width + head * BLOCK : part * width + (head + 1) * BLOCK]
                    for part in range(3)
                ],
                axis=1,
            )
            total = dot(x, right, ta=True).astype(BF16)
            count = size // shard
            head_parts[head][pl.ds(i * count, count)] = total.reshape(count, shard, 3 * BLOCK)

        for head, reduce in enumerate(reduce_heads):
            pl.loop(0, steps)(partial(gradients, only=head))
            before_convolution(head)
            if flip:
                for k in [*range(1, reduce.outer), 0]:
                    projection_gradient(reduce.target(k), 2 * shard, head)
                    reduce.to_beside(k).start()
            else:
                pl.loop(0, model // tile)(partial(projection_gradient, size=tile, head=head))
                reduce.start()
            if head == 0:
                reduce_up.join_all()
                for k in range(1, mp):
                    swap_in(k).wait_recv()
                reduce_out.start()
            else:
                reduce_heads[head - 1].join_all()
        weight = qkv.reshape(model, 3 * width)

        def rows(index):
            at = pl.ds(pl.multiple_of(index * own, own), own)
            dh_part[index] = (
                dot(dp_low[at], weight[...], tb=True) + dot(db_low[at], beta_rows[...])
            ).astype(BF16)

        for k in [*range(1, reduce_h.outer), 0]:
            rows(reduce_h.given(k))
            reduce_h.to_beside(k).start()
            rows(reduce_h.kept(k))
            if k:
                reduce_h.join(k)
        reduce_out.join_all()
        reduce_heads[-1].join(1)
        d_beta = dot(db_low[...], h[...], ta=True)
        for g in range(heads * mp):
            line = d_beta[g % heads : g % heads + 1]
            small[g : g + 1] = jnp.where(column == g // heads, line, 0.0)
        for d in range(dp):
            small_part[d, 0:gain_row] = small[0:gain_row, d * lanes : (d + 1) * lanes]
            small_part[d, gain_row + 1 :] = jnp.zeros((small_part.shape[1] - gain_row - 1, lanes), F32)
        reduce_small.start()
        for k in range(1, mp):
            swap(k, (column + k) % mp).wait_send()

    pl.run_scoped(
        mixer,
        *mixer_buffers,
        square,
        pltpu.VMEM((length, 3 * width), BF16),
        pltpu.VMEM((length, BLOCK), BF16),
    )
    for reduce, result in ((reduce_gate, d_gate), (reduce_up, d_up), (reduce_down, d_down)):
        result[...] = reduce.finish()
    output[...] = (y1[...] + reduce_y.finish()).astype(BF16)
    for k in range(2, reduce_heads[-1].outer):
        reduce_heads[-1].join(k)
    def share(slot, reduce):
        size = reduce.near.shape[2]
        low_at = shared.at[:, slot * 3 * BLOCK : slot * 3 * BLOCK + size]
        low_at[...] = reduce.finish().astype(BF16)
        gather = Gather(
            "mp",
            mp,
            low_at,
            lambda i: shared_all.at[i, :, slot * 3 * BLOCK : slot * 3 * BLOCK + size],
            share_sems,
            slot,
        )
        gather.start()
        return gather

    reduce_small.join_all()
    gathers = [share(heads, reduce_out)]
    for head in range(heads - 1):
        gathers.append(share(head, reduce_heads[head]))
    small_low[...] = reduce_small.finish()
    narrow = Gather("mp", mp, small_low, leading(small_sums), share_sems, heads + 1)
    narrow.start()
    dh = reduce_h.finish()
    x = tokens[...].astype(F32)
    s = lax.rsqrt(jnp.mean(x * x, axis=-1, keepdims=True) + 1e-06)
    d_first = jnp.sum(dh * x * s, axis=0, keepdims=True)
    for d in range(dp):
        line = d_first[:, d * lanes : (d + 1) * lanes]
        first_part[d] = jnp.broadcast_to(line, (8, lanes))
    place = lax.axis_index("dp")

    def first_copy(k):
        return pltpu.make_async_remote_copy(
            src_ref=first_part.at[(place + k) % dp],
            dst_ref=first_in.at[k],
            send_sem=first_sems.at[0, k],
            recv_sem=first_sems.at[1, k],
            device_id={"dp": (place + k) % dp},
            device_id_type=MESH,
        )

    def first_share(k, source):
        return pltpu.make_async_remote_copy(
            src_ref=first_low,
            dst_ref=first_sums.at[source],
            send_sem=share_first.at[0, k],
            recv_sem=share_first.at[1, k],
            device_id={"mp": (column + k) % mp},
            device_id_type=MESH,
        )

    for k in range(1, dp):
        first_copy(k).start()
    scaled = first[...] * dh
    input_grad[...] += s * scaled - x * (
        s * s * s * jnp.mean(x * scaled, axis=-1, keepdims=True)
    )
    gathers.append(share(heads - 1, reduce_heads[-1]))
    total = first_part[place]
    for k in range(1, dp):
        first_copy(k).wait_recv()
        total = total + first_in[k]
    first_low[...] = total
    for k in range(1, mp):
        first_share(k, column).start()
    first_sums[column] = total
    for g in gathers[:-1]:
        g.forward_all()
    narrow.forward_all()
    gathers[-1].forward_all()
    narrow.finish()
    small_total = small_sums[0]
    for i in range(1, mp):
        small_total = small_total + small_sums[i]
    d_small[...] = small_total
    for k in range(1, mp):
        first_share(k, (column + mp - k) % mp).wait_recv()
    total = first_sums[0]
    for i in range(1, mp):
        total = total + first_sums[i]
    d_small[first_row : first_row + 1] = total[0:1]
    for g in gathers:
        g.finish()
    for k in range(1, dp):
        first_copy(k).wait_send()
    for k in range(1, mp):
        first_share(k, column).wait_send()
    ab_gather_done = (reduce_y, reduce_h, *over_dp)
    for reduce in ab_gather_done:
        reduce.sent()


def finish_kernel(mp, heads, *refs):
    take = Taker(refs)
    small, shared_in, *passed_in = take(7)
    passed, models, smalls = take(5), take(4), take(7)
    held = take(5)
    shared, wide, sems = take(3)
    width = heads * BLOCK
    loads = [
        pltpu.make_async_copy(src, dst, sems.at[i])
        for i, (src, dst) in enumerate(zip(passed_in, held))
    ]
    copies = [
        pltpu.make_async_copy(src, dst, sems.at[10 + i])
        for i, (src, dst) in enumerate(zip(held, passed))
    ]
    load = pltpu.make_async_copy(shared_in, shared, sems.at[5])
    load.start()
    for copy in loads:
        copy.start()
    line = 0
    for ref in smalls:
        ref[...] = small[line : line + ref.shape[0], 0 : ref.shape[1]]
        line += ref.shape[0]
    load.wait()
    for index, result in enumerate(models):
        for i in range(mp):
            for head in range(heads):
                at = head * 3 * BLOCK + index * BLOCK if index < 3 else 3 * width + head * BLOCK
                to = i * width + head * BLOCK
                wide[index, :, to : to + BLOCK] = shared[i, :, at : at + BLOCK].astype(F32)
        copies.append(pltpu.make_async_copy(wide.at[index], result, sems.at[6 + index]))
        copies[-1].start()
    for first, second in zip(loads, copies):
        first.wait()
        second.start()
    for copy in copies:
        copy.wait()


def call(kernel, ins, outs, scratch, collective, name, limit):
    return pl.pallas_call(
        kernel,
        out_shape=[jax.ShapeDtypeStruct(shape, kind) for _, shape, kind in outs],
        in_specs=[spec for spec, _ in ins],
        out_specs=[spec for spec, _, _ in outs],
        scratch_shapes=list(scratch),
        compiler_params=pltpu.CompilerParams(
            collective_id=collective,
            has_side_effects=collective is not None,
            vmem_limit_bytes=limit * MIB,
        ),
        name=name,
    )(*[array for _, array in ins])


def shards(
    dp,
    mp,
    tokens,
    cotangent,
    domain,
    domain_weight,
    query_weight,
    key_weight,
    value_weight,
    beta_weight,
    conv_query,
    conv_key,
    conv_value,
    out_gain,
    out_weight,
    norm_first,
    norm_second,
    gate_weight,
    up_weight,
    down_weight,
):
    own, model = tokens.shape
    length = own * mp
    shard = query_weight.shape[0]
    taps = conv_query.shape[0]
    all_heads = beta_weight.shape[1]
    heads = all_heads // mp
    width = model // mp
    feed = gate_weight.shape[1]
    lanes = norm_first.shape[0]
    gains = out_gain.shape[0]
    conv_row, gain_row = all_heads, all_heads + 3 * taps + 2
    first_row, second_row = gain_row - 2, gain_row - 1
    small_rows = -(-(gain_row + 1) // 8) * 8
    rows_of = (conv_row, first_row, second_row, gain_row)
    flip = lanes % 128 == 0

    square = ((heads * (length // BLOCK), BLOCK, BLOCK), F32)
    stored = [
        ((length, model), BF16),
        ((length + 16, 3 * width), F32),
        *[square] * 6,
        ((length, width), F32),
        ((length, width), BF16),
    ]
    feed_shape = (feed, model) if flip else (dp, shard, feed)
    feed_block = (feed, shard) if flip else (shard, feed)
    feed_grad = (VM, feed_block, F32)
    feed_own = (
        (gate_weight.T, up_weight.T, down_weight) if flip else (gate_weight, up_weight, down_weight.T)
    )
    token_rows = ((mp, own, model), BF16)
    sizes = (feed_block,) * 3 + ((shard, width),) + ((shard, 3 * BLOCK),) * heads
    results = call(
        partial(block_kernel, dp, mp, taps, heads, gains, flip, rows_of),
        [
            (SM, domain), (SM, domain_weight),
            (VM, tokens), (VM, cotangent), (ANY, query_weight), (ANY, key_weight), (ANY, value_weight),
            (ANY, out_weight),
            (VM, beta_weight.T), (VM, conv_query), (VM, conv_key), (VM, conv_value),
            (VM, norm_first[None]), (VM, norm_second[None]), (VM, out_gain[None]),
            *[(ANY, a) for a in feed_own],
        ],
        [
            (VM, (own, model), BF16),
            (VM, (own, model), F32),
            (VM, (mp, shard, 4 * width), BF16),
            (VM, (small_rows, lanes), F32),
            *[feed_grad] * 3,
            (ANY, *token_rows), *[(ANY, feed_shape, BF16)] * 3,
            *[(ANY, *kind) for kind in stored],
        ],
        [pltpu.VMEM(*token_rows)] * 4
        + [
            pltpu.VMEM((own, model), BF16),
            pltpu.VMEM((dp, shard, 3 * width), BF16),
            pltpu.VMEM((dp // mp, shard, model), BF16),
            pltpu.VMEM((dp, shard, width), BF16),
            pltpu.VMEM((own, model), F32),
            pltpu.VMEM((BLOCK, model), BF16),
            pltpu.VMEM((taps, 3 * width), F32),
            pltpu.VMEM((1, model), F32),
            pltpu.VMEM((1, model), F32),
            pltpu.VMEM((1, BLOCK), F32),
            pltpu.VMEM((length, BLOCK), F32),
        ]
        + [pltpu.VMEM(feed_shape, BF16)] * 3
        + [
            pltpu.VMEM((mp, dp // mp, shard, width), BF16),
            *[pltpu.VMEM((dp, shard, 3 * BLOCK), BF16)] * heads,
        ]
        + ReduceScatter.buffers(mp, own, model) * 2
        + [b for size in sizes for b in ReduceScatter.buffers(dp, *size)]
        + ReduceScatter.buffers(dp, small_rows, lanes, F32)
        + [
            pltpu.VMEM((small_rows, lanes), F32),
            pltpu.VMEM((dp, small_rows, lanes), F32),
            pltpu.VMEM((small_rows, model), F32),
            pltpu.VMEM((dp, small_rows, lanes), F32),
            pltpu.VMEM((small_rows, lanes), F32),
            pltpu.VMEM((mp, small_rows, lanes), F32),
            pltpu.VMEM((shard, 4 * width), BF16),
            pltpu.VMEM((dp, 8, lanes), F32),
            pltpu.VMEM((dp, 8, lanes), F32),
            pltpu.VMEM((8, lanes), F32),
            pltpu.VMEM((mp, 8, lanes), F32),
            pltpu.SemaphoreType.DMA((2, dp)),
            pltpu.SemaphoreType.DMA((2, mp)),
        ]
        + Gather.scratch(mp, 4)
        + Gather.scratch(dp, 9)
        + ReduceScatter.scratch(mp, 4)
        + ReduceScatter.scratch(dp, 5 + heads)
        + Gather.scratch(mp, 2 + heads)
        + [pltpu.SemaphoreType.DMA((mp,))] * 4
        + [
            pltpu.SemaphoreType.DMA((10,)),
            pltpu.SemaphoreType.DMA((10,)),
            pltpu.SemaphoreType.DMA((4,)),
        ],
        0,
        "block",
        63,
    )
    output, input_grad, shared, small, d_gate, d_up, d_down = results[:7]
    small_shapes = [(all_heads, lanes)] + [(taps, lanes)] * 3 + [(1, lanes)] * 2 + [(1, gains)]
    results = call(
        partial(finish_kernel, mp, heads),
        [(VM, small)] + [(ANY, a) for a in (shared, output, input_grad, d_gate, d_up, d_down)],
        [
            (ANY, (own, model), BF16),
            (ANY, (own, model), F32),
            *[(ANY, feed_block, F32)] * 3,
            *[(ANY, (shard, model), F32)] * 4,
            *[(VM, shape, F32) for shape in small_shapes],
        ],
        [
            pltpu.VMEM((own, model), BF16),
            pltpu.VMEM((own, model), F32),
            *[pltpu.VMEM(feed_block, F32)] * 3,
            pltpu.VMEM((mp, shard, 4 * width), BF16),
            pltpu.VMEM((4, shard, model), F32),
            pltpu.SemaphoreType.DMA((15,)),
        ],
        None,
        "finish",
        60,
    )
    output, input_grad, d_gate, d_up, d_down = results[:5]
    d_query, d_key, d_value, d_outw = results[5:9]
    d_beta, d_conv_q, d_conv_k, d_conv_v, d_first, d_second, d_gain = results[9:]
    if flip:
        d_gate, d_up = d_gate.T, d_up.T
    else:
        d_down = d_down.T
    return (
        output,
        input_grad,
        d_query,
        d_key,
        d_value,
        d_beta.T,
        d_conv_q,
        d_conv_k,
        d_conv_v,
        d_gain[0],
        d_outw,
        d_first[0],
        d_second[0],
        d_gate,
        d_up,
        d_down,
    )


def solution(mesh):
    dp, mp = mesh.shape["dp"], mesh.shape["mp"]
    weight = P("dp", None)
    split = P(None, "dp")
    rows = P(("dp", "mp"), None)
    return jax.shard_map(
        partial(shards, dp, mp),
        mesh=mesh,
        in_specs=(
            rows, rows, P("dp"), P(), weight, weight, weight, weight, split, split, split,
            P("dp"), weight, P("dp"), P("dp"), P("dp", "mp"), P("dp", "mp"), P("mp", "dp"),
        ),
        out_specs=(
            rows, rows, weight, weight, weight, weight, split, split, split,
            P("dp"), weight, P("dp"), P("dp"), P("dp", "mp"), P("dp", "mp"), P("mp", "dp"),
        ),
        check_vma=False,
    )
```

```python
from functools import partial

import jax
import jax.numpy as jnp
from jax import lax
from jax.experimental import pallas as pl
from jax.experimental.pallas import tpu as pltpu
from jax.sharding import PartitionSpec as P

BLOCK = 128
MESH = pl.DeviceIdType.MESH
F32 = jnp.float32
BF16 = jnp.bfloat16
MIB = 1 << 20
VM = pl.BlockSpec(memory_space=pltpu.VMEM)
ANY = pl.BlockSpec(memory_space=pl.ANY)
SM = pl.BlockSpec(memory_space=pltpu.SMEM)


def dot(a, b, ta=False, tb=False):
    dims = (((0 if ta else 1,), (1 if tb else 0,)), ((), ()))
    return lax.dot_general(a, b, dims, preferred_element_type=F32)


def halves(a):
    high = a.astype(BF16)
    return high, (a - high.astype(F32)).astype(BF16)


def mm(a, b, ta=False, tb=False):
    ah, al = halves(a)
    bh, bl = halves(b)
    da, db = 0 if ta else 1, 1 if tb else 0
    left = jnp.concatenate([ah, al], axis=da)
    right = jnp.concatenate([bh, bh], axis=db)
    columns = b.shape[1 - db]
    if columns > BLOCK:
        return dot(left, right, ta, tb) + dot(ah, bl, ta, tb)
    rest = jnp.concatenate([bl, jnp.zeros_like(bl)], axis=db)
    both = dot(left, jnp.concatenate([right, rest], axis=1 - db), ta, tb)
    return both[:, :columns] + both[:, columns:]


def one_pass(a, b, ta=False, tb=False):
    return dot(a.astype(BF16), b.astype(BF16), ta, tb)


def each(function, *lists):
    return [function(*items) for items in zip(*lists)]


def iota2(size):
    return (
        lax.broadcasted_iota(jnp.int32, (size, size), 0),
        lax.broadcasted_iota(jnp.int32, (size, size), 1),
    )


def unit_lower_inverses(stricts):
    size = stricts[0].shape[0]
    row, col = iota2(size)
    pairs = (row >> 1) == (col >> 1)
    unit = jnp.where(row == col, 1.0, 0.0)
    inverses = each(lambda a: unit - jnp.where(pairs, a, 0.0), stricts)
    shift = 1
    while (1 << shift) < size:
        inside = (row >> (shift + 1)) == (col >> (shift + 1))
        apart = (row >> shift) != (col >> shift)
        corner = inside & apart
        moved = each(lambda x, a: mm(x, jnp.where(corner, a, 0.0)), inverses, stricts)
        moved = each(mm, moved, inverses)
        inverses = each(lambda x, t: x - t, inverses, moved)
        shift += 1
    return inverses


def sigmoid(a):
    return 1.0 / (1.0 + jnp.exp(-a))


class Gather:
    def __init__(self, axis, count, src, place, sems, slot):
        self.axis, self.src, self.place = axis, src, place
        self.outer = count // 2
        self.me = lax.axis_index(axis)
        self.a, self.b = self.me // 2, self.me % 2
        self.sa, self.ra, self.sb, self.rb, self.local = (s.at[slot] for s in sems)
        self.beside = self.a * 2 + 1 - self.b

    @staticmethod
    def scratch(count, slots):
        return [pltpu.SemaphoreType.DMA((slots, count // 2))] * 4 + [
            pltpu.SemaphoreType.DMA((slots, 1))
        ]

    def copy(self, src, block, send, recv, target):
        return pltpu.make_async_remote_copy(
            src_ref=src,
            dst_ref=self.place(block),
            send_sem=send,
            recv_sem=recv,
            device_id={self.axis: target},
            device_id_type=MESH,
        )

    def own(self):
        return pltpu.make_async_copy(self.src, self.place(self.me), self.local.at[0])

    def source(self, k):
        return (self.a + self.outer - k) % self.outer * 2 + self.b

    def source_beside(self, k):
        return (self.a + self.outer - k) % self.outer * 2 + 1 - self.b

    def to_outer(self, k):
        target = (self.a + k) % self.outer * 2 + self.b
        return self.copy(self.src, self.me, self.sa.at[k], self.ra.at[k], target)

    def to_beside(self, k):
        block = self.source(k)
        src = self.src if k == 0 else self.place(block)
        return self.copy(src, block, self.sb.at[k], self.rb.at[k], self.beside)

    def start_outer(self):
        for k in range(1, self.outer):
            self.to_outer(k).start()

    def start_beside(self):
        self.to_beside(0).start()
        self.own().start()

    def start(self):
        self.start_outer()
        self.start_beside()

    def forward(self, k):
        self.to_outer(k).wait_recv()
        self.to_beside(k).start()

    def forward_all(self):
        for k in range(1, self.outer):
            self.forward(k)

    def arrived(self, k):
        self.to_beside(k).wait_recv()

    def sent(self):
        for k in range(self.outer):
            if k:
                self.to_outer(k).wait_send()
            self.to_beside(k).wait_send()

    def finish(self):
        self.own().wait()
        for k in range(self.outer):
            self.arrived(k)
        self.sent()


class ReduceScatter:
    def __init__(self, axis, count, place, near, far, sems, slot):
        self.axis, self.place, self.near, self.far = axis, place, near, far
        self.outer = count // 2
        self.me = lax.axis_index(axis)
        self.a, self.b = self.me // 2, self.me % 2
        self.sa, self.ra, self.sb, self.rb = (s.at[slot] for s in sems)
        self.beside = self.a * 2 + 1 - self.b

    @staticmethod
    def scratch(count, slots):
        return [pltpu.SemaphoreType.DMA((slots, count // 2))] * 4

    @staticmethod
    def buffers(count, rows, columns, kind=BF16):
        return [pltpu.VMEM((count // 2, rows, columns), kind)] * 2

    def target(self, k):
        return (self.a + k) % self.outer

    def kept(self, k):
        return self.target(k) * 2 + self.b

    def given(self, k):
        return self.target(k) * 2 + 1 - self.b

    def to_beside(self, k):
        return pltpu.make_async_remote_copy(
            src_ref=self.place(self.given(k)),
            dst_ref=self.near.at[k],
            send_sem=self.sb.at[k],
            recv_sem=self.rb.at[k],
            device_id={self.axis: self.beside},
            device_id_type=MESH,
        )

    def to_outer(self, k):
        return pltpu.make_async_remote_copy(
            src_ref=self.place(self.kept(k)),
            dst_ref=self.far.at[k],
            send_sem=self.sa.at[k],
            recv_sem=self.ra.at[k],
            device_id={self.axis: self.target(k) * 2 + self.b},
            device_id_type=MESH,
        )

    def start(self):
        for k in [*range(1, self.outer), 0]:
            self.to_beside(k).start()

    def join(self, k):
        self.to_beside(k).wait_recv()
        block = self.place(self.kept(k))
        total = block[...].astype(F32) + self.near[k].astype(F32)
        if k == 0:
            return total
        block[...] = total.astype(block.dtype)
        self.to_outer(k).start()

    def join_all(self):
        for k in range(1, self.outer):
            self.join(k)

    def finish(self):
        total = self.join(0)
        for k in range(1, self.outer):
            self.to_outer(k).wait_recv()
            total = total + self.far[k].astype(F32)
        return total

    def sent(self):
        for k in range(self.outer):
            self.to_beside(k).wait_send()
            if k:
                self.to_outer(k).wait_send()


def leading(ref):
    return lambda i: ref.at[i]


def columns_of(ref, size):
    return lambda i: ref.at[:, pl.ds(pl.multiple_of(i * size, size), size)]


def greet(counts):
    barrier = pltpu.get_barrier_semaphore()
    for axis, count in counts:
        me = lax.axis_index(axis)
        for k in range(1, count):
            pl.semaphore_signal(
                barrier, inc=1, device_id={axis: (me + k) % count}, device_id_type=MESH
            )
    pl.semaphore_wait(barrier, sum(count - 1 for _, count in counts))


class Taker:
    def __init__(self, refs):
        self.refs, self.cursor = refs, 0

    def __call__(self, count):
        self.cursor += count
        return self.refs[self.cursor - count : self.cursor]

    def one(self):
        return self(1)[0]


def activated(p, conv, start, part, head, width, taps):
    columns = slice(part * width + head * BLOCK, part * width + (head + 1) * BLOCK)
    window = p[pl.ds(start, BLOCK + 8), columns]
    shifted = [window[8 - taps + 1 + j : 8 - taps + 1 + j + BLOCK] for j in range(taps)]
    pre = conv[0:1, columns] * shifted[0]
    for j in range(1, taps):
        pre = pre + conv[j : j + 1, columns] * shifted[j]
    gate = sigmoid(pre)
    return pre * gate, gate, shifted


def inverse_norm(s):
    return lax.rsqrt(jnp.sum(s * s, axis=-1, keepdims=True) + 1e-06)


def place_lanes(index, count, lanes, gains):
    row = lax.broadcasted_iota(jnp.int32, (lanes, count * gains), 0)
    col = lax.broadcasted_iota(jnp.int32, (lanes, count * gains), 1)
    return jnp.where((col == row + index * gains) & (row < gains), 1.0, 0.0)


def block_kernel(dp, mp, taps, heads, gains, flip, rows_of, *refs):
    take = Taker(refs)
    domain, domain_weight = take(2)
    tokens, cot = take(2)
    projections, smalls = take(4), take(7)
    gate_own, up_own, down_own = take(3)
    output, input_grad, shared_all, d_small, d_gate, d_up, d_down = take(7)
    cot_all, gate_all, up_all, down_all = take(4)
    stored = take(10)
    rows_all, ab_all, y_part, dh_part, low = take(5)
    qkv, out_rows, out_columns = take(3)
    y1, beta_rows, conv, first, second, gain, beta_pre = take(7)
    gate_part, up_part, down_part, out_part = take(4)
    head_parts = take(heads)
    near_y, far_y, near_h, far_h = take(4)
    buffers = [take(2) for _ in range(5 + heads)]
    small_own, small_all, small, small_part, small_low, small_sums = take(6)
    shared = take.one()
    sems_mp, sems_dp, reduce_sems, dp_sems, share_sems = take(5), take(5), take(4), take(4), take(5)
    rows_send, rows_recv, swap_send, swap_recv, saved_sem, load_sem, feed_sem = take(7)
    conv_row, first_row, second_row, gain_row = rows_of
    own, model = tokens.shape
    length = own * mp
    shard = model // dp
    width = heads * BLOCK
    blocks = length // BLOCK
    lanes = small_own.shape[1]
    feed = gate_own.shape[0] if flip else gate_own.shape[1]
    per = dp // mp
    column = lax.axis_index("mp")
    mine = pl.ds(pl.multiple_of(column * width, BLOCK), width)
    tile, wide_tile = 256, 512
    row, col = iota2(BLOCK)
    scale = BLOCK**-0.5
    group = 4 if blocks % 4 == 0 else 1
    loss_scale = jnp.zeros((1, 1), F32)
    for i in range(domain_weight.shape[0]):
        loss_scale = loss_scale + jnp.where(domain[0] == i, domain_weight[i], 0.0)

    small_own[...] = jnp.zeros_like(small_own)
    line = 0
    for ref in smalls:
        small_own[line : line + ref.shape[0], 0 : ref.shape[1]] = ref[...].astype(F32)
        line += ref.shape[0]

    greet((("dp", dp), ("mp", mp)))
    small_gather = Gather("dp", dp, small_own, leading(small_all), sems_dp, 0)
    places = [lambda d, i=i: qkv.at[d, :, i * width : (i + 1) * width] for i in range(3)]
    *qkv_gathers, out_gather = [
        Gather("dp", dp, src.at[:, mine], place, sems_dp, 1 + i)
        for i, (src, place) in enumerate(zip(projections, [*places, leading(out_columns)]))
    ]
    token_gather = Gather("mp", mp, tokens, leading(rows_all), sems_mp, 0)
    cot_gather = Gather("mp", mp, cot, leading(cot_all), sems_mp, 1)
    def feed_gather(src, dst, rows, slot):
        if flip:
            place = lambda d: dst.at[rows, pl.ds(pl.multiple_of(d * lanes, lanes), lanes)]
            return Gather("dp", dp, src.at[rows], place, sems_dp, slot)
        return Gather(
            "dp", dp, src.at[:, rows], lambda d: dst.at[d, :, rows], sems_dp, slot
        )

    whole, cut = slice(0, feed), feed // 256 * 128
    feed_gathers = [
        feed_gather(gate_own, gate_all, whole, 5),
        feed_gather(up_own, up_all, whole, 6),
        feed_gather(down_own, down_all, slice(0, cut), 7),
        feed_gather(down_own, down_all, slice(cut, feed), 8),
    ]
    small_gather.start()
    qkv_gathers[0].start()
    token_gather.start()
    small_gather.forward_all()
    qkv_gathers[0].forward(1)
    qkv_gathers[1].start()
    for k in range(2, qkv_gathers[0].outer):
        qkv_gathers[0].forward(k)
    qkv_gathers[1].forward(1)
    qkv_gathers[2].start()
    for k in range(2, qkv_gathers[1].outer):
        qkv_gathers[1].forward(k)
    token_gather.forward_all()
    qkv_gathers[2].forward(1)
    out_gather.start_outer()
    feed_gathers[0].start_outer()
    for k in range(2, qkv_gathers[2].outer):
        qkv_gathers[2].forward(k)
    cot_gather.start()
    small_gather.finish()

    for d in range(dp):
        small[:, d * lanes : (d + 1) * lanes] = small_all[d]
    beta_rows[...] = jnp.zeros_like(beta_rows)
    picked = []
    for head in range(heads):
        wanted = jnp.zeros((1, model), F32)
        for g in range(heads * mp):
            wanted = jnp.where(column * heads + head == g, small[g : g + 1], wanted)
        picked.append(wanted)
    beta_rows[0:16] = jnp.concatenate(
        picked + [jnp.zeros((16 - heads, model), F32)], axis=0
    ).astype(BF16)
    for i in range(3):
        for j in range(taps):
            at = conv_row + i * taps + j
            conv[j : j + 1, i * width : (i + 1) * width] = small[at : at + 1, mine]
    first[...] = small[first_row : first_row + 1]
    second[...] = small[second_row : second_row + 1]
    total = jnp.zeros((8, dp * gains), F32)
    for d in range(dp):
        line = jnp.broadcast_to(small_all[d, gain_row : gain_row + 1], (8, lanes))
        total = total + dot(line.astype(BF16), place_lanes(d, dp, lanes, gains).astype(BF16))
    gain[...] = total[0:1]

    token_gather.finish()
    h2_gather = Gather("mp", mp, low, leading(rows_all), sems_mp, 2)
    ab_gather = Gather("mp", mp, low, leading(ab_all), sems_mp, 3)
    reduce_part = ReduceScatter("mp", mp, leading(y_part), near_y, far_y, reduce_sems, 0)
    reduce_h2 = ReduceScatter("mp", mp, leading(dh_part), near_h, far_h, reduce_sems, 1)
    reduce_y = ReduceScatter("mp", mp, leading(y_part), near_y, far_y, reduce_sems, 2)
    reduce_h = ReduceScatter("mp", mp, leading(dh_part), near_h, far_h, reduce_sems, 3)
    over_dp = [
        ReduceScatter(
            "dp",
            dp,
            columns_of(part, shard) if flip and slot < 3 else leading(part),
            *pair,
            dp_sems,
            slot,
        )
        for slot, (part, pair) in enumerate(
            zip((gate_part, up_part, down_part, out_columns, *head_parts, small_part), buffers)
        )
    ]
    reduce_gate, reduce_up, reduce_down, reduce_out, *reduce_heads, reduce_small = over_dp

    def mixer_forward(
        h, p, inverse, w, scores, step, delta, state, o, m, u, offset, q_all
    ):
        saved = (h, p, inverse, w, scores, step, delta, state, o, m)
        for i in range(mp):
            x = rows_all[i].astype(F32)
            normed = x * lax.rsqrt(jnp.mean(x * x, axis=-1, keepdims=True) + 1e-06) * first[...]
            h[i * own : (i + 1) * own] = normed.astype(BF16)
        for g in qkv_gathers:
            g.finish()
        out_gather.start_beside()
        for g in feed_gathers:
            g.start_beside()

        p[0:8] = jnp.zeros((8, p.shape[1]), F32)
        p[length + 8 :] = jnp.zeros((8, p.shape[1]), F32)
        weight = qkv.reshape(model, 3 * width)

        @pl.loop(0, mp)
        def _(i):
            at = pl.ds(pl.multiple_of(i * own, own), own)
            low = h[at]
            p[pl.ds(pl.multiple_of(i * own + 8, 8), own)] = dot(low, weight[...])
            beta_pre[at] = dot(low, beta_rows[...], tb=True)

        def save(index):
            return pltpu.make_async_copy(saved[index], stored[index], saved_sem.at[index])

        for index in (0, 1):
            save(index).start()


        def prepare(i):
            chains = [(i * group + j, head) for j in range(group) for head in range(heads)]
            starts = [pl.multiple_of(c * BLOCK, BLOCK) for c, _ in chains]
            places = [head * blocks + c for c, head in chains]
            ks, kbs, vbs, qs = [], [], [], []
            for (c, head), start in zip(chains, starts):
                s, _, _ = activated(p, conv, start, 0, head, width, taps)
                qs.append(s * (inverse_norm(s) * scale))
                s, _, _ = activated(p, conv, start, 1, head, width, taps)
                k = s * inverse_norm(s)
                v, _, _ = activated(p, conv, start, 2, head, width, taps)
                beta = sigmoid(beta_pre[pl.ds(start, BLOCK), head : head + 1])
                ks.append(k)
                kbs.append(k * beta)
                vbs.append(v * beta)
            for place, q in zip(places, qs):
                q_all[place] = q
            stricts = each(lambda a, b: jnp.where(row > col, mm(a, b, tb=True), 0.0), kbs, ks)
            for place, a in zip(places, each(lambda q, k: mm(q, k, tb=True), qs, ks)):
                scores[place] = jnp.where(row >= col, a, 0.0)
            xs = unit_lower_inverses(stricts)
            for place, x in zip(places, xs):
                inverse[place] = x
            wus = each(lambda x, a, b: mm(x, jnp.concatenate([a, b], axis=1)), xs, kbs, vbs)
            for place, wu in zip(places, wus):
                w[place] = wu[:, :BLOCK]
                u[place] = wu[:, BLOCK:]
            for place, gb in zip(places, each(lambda k, wu: mm(k, wu, ta=True), ks, wus)):
                step[place] = gb[:, :BLOCK]
                offset[place] = gb[:, BLOCK:]

        def swap(k, block, source):
            columns = pl.ds(pl.multiple_of(source * width, BLOCK), width)
            return pltpu.make_async_remote_copy(
                src_ref=out_columns.at[pl.ds(block * per, per)],
                dst_ref=out_rows.at[:, :, columns],
                send_sem=rows_send.at[k],
                recv_sem=rows_recv.at[k],
                device_id={"mp": (column + k) % mp},
                device_id_type=MESH,
            )

        half = blocks // group // 2
        pl.loop(0, half)(prepare)
        out_gather.forward_all()
        pl.loop(half, blocks // group)(prepare)
        for index in (2, 3, 4, 5):
            save(index).start()
        feed_gathers[0].forward_all()
        feed_gathers[1].start_outer()
        cot_gather.forward_all()
        out_gather.finish()
        for k in range(1, mp):
            swap(k, (column + k) % mp, column).start()
        out_rows[:, :, mine] = out_columns[pl.ds(column * per, per)]

        def advance(c, states):
            places = [head * blocks + c for head in range(heads)]
            for place, s in zip(places, states):
                state[place] = s
            moved = each(lambda place, s: mm(step[place], s), places, states)
            return tuple(each(lambda place, s, t: s - t + offset[place], places, states, moved))

        states = tuple(jnp.zeros((BLOCK, BLOCK), F32) for _ in range(heads))
        for c in range(blocks):
            states = advance(c, states)
        save(7).start()

        for k in range(1, mp):
            swap(k, column, (column + mp - k) % mp).wait_recv()
        out_weight = out_rows.reshape(width, model)

        def outputs(index):
            per = own // BLOCK
            chains = [(index * per + j, head) for j in range(per) for head in range(heads)]
            places = [head * blocks + c for c, head in chains]
            boths = each(
                lambda at: mm(jnp.concatenate([w[at], q_all[at]], axis=0), state[at]), places
            )
            ds = each(lambda at, both: u[at] - both[:BLOCK], places, boths)
            for place, d in zip(places, ds):
                delta[place] = d
            outs = each(lambda at, d: mm(scores[at], d), places, ds)
            outs = each(lambda both, out: both[BLOCK:] + out, boths, outs)
            for (c, head), out in zip(chains, outs):
                rows = pl.ds(pl.multiple_of(c * BLOCK, BLOCK), BLOCK)
                at = slice(head * BLOCK, (head + 1) * BLOCK)
                o[rows, at] = out
                r = lax.rsqrt(jnp.mean(out * out, axis=-1, keepdims=True) + 1e-05)
                m[rows, at] = (out * r * gain[...]).astype(BF16)
            at = pl.ds(pl.multiple_of(index * own, own), own)
            y_part[index] = dot(m[at], out_weight[...]).astype(BF16)

        for k in [*range(1, reduce_part.outer), 0]:
            outputs(reduce_part.given(k))
            reduce_part.to_beside(k).start()
            outputs(reduce_part.kept(k))
            if k:
                reduce_part.join(k)
        for index in (6, 8, 9):
            save(index).start()
        feed_gathers[2].start_outer()
        feed_gathers[3].start_outer()
        feed_gathers[1].forward_all()
        y = tokens[...].astype(F32) + reduce_part.finish()
        y1[...] = y
        low[...] = (
            y * lax.rsqrt(jnp.mean(y * y, axis=-1, keepdims=True) + 1e-06) * second[...]
        ).astype(BF16)
        h2_gather.start()
        for g in feed_gathers[2:]:
            g.forward_all()
        reduce_part.sent()
        for k in range(1, mp):
            swap(k, (column + k) % mp, column).wait_send()
        for index in range(10):
            save(index).wait()

    square = pltpu.VMEM((heads * blocks, BLOCK, BLOCK), F32)
    mixer_buffers = [
        pltpu.VMEM((length, model), BF16),
        pltpu.VMEM((length + 16, 3 * width), F32),
        *[square] * 6,
        pltpu.VMEM((length, width), F32),
        pltpu.VMEM((length, width), BF16),
    ]
    pl.run_scoped(mixer_forward, *mixer_buffers, square, square, square)

    def feed_forward(gate, up, down, gb, z, dg, du):
        def load(index):
            src, dst = ((gate_all, gate), (up_all, up), (down_all, down), (cot_all, gb))[index]
            return pltpu.make_async_copy(src, dst, feed_sem.at[index])

        gate_w, up_w, down_w = (
            a if flip else a.reshape(model, feed) for a in (gate, up, down)
        )

        def hidden_rows(index):
            at = pl.ds(pl.multiple_of(index * own, own), own)
            x = rows_all[index]
            g = dot(x, gate_w[...], tb=flip)
            u = dot(x, up_w[...], tb=flip)
            sg = sigmoid(g)
            silu = g * sg
            z[at] = (silu * u).astype(BF16)
            dg[at] = (u * (sg + silu * (1.0 - sg))).astype(BF16)
            du[at] = silu.astype(BF16)

        def result_rows(index):
            at = pl.ds(pl.multiple_of(index * own, own), own)
            dz = dot(gb[index], down_w[...], tb=flip)
            dgl = (dz * dg[at].astype(F32)).astype(BF16)
            dul = (dz * du[at].astype(F32)).astype(BF16)
            dg[at] = dgl
            du[at] = dul
            dh_part[index] = (
                dot(dgl, gate_w[...], tb=not flip) + dot(dul, up_w[...], tb=not flip)
            ).astype(BF16)
            y_part[index] = dot(z[at], down_w[...], tb=not flip).astype(BF16)

        def weight_gradient(part, left, right, reduce):
            @pl.loop(0, model // wide_tile)
            def _(i):
                at = pl.ds(pl.multiple_of(i * wide_tile, wide_tile), wide_tile)
                x = left[:, :, at].reshape(length, wide_tile)
                if flip:
                    part[:, at] = dot(right[...], x, ta=True).astype(BF16)
                else:
                    total = dot(x, right[...], ta=True).astype(BF16)
                    count = wide_tile // shard
                    part[pl.ds(i * count, count)] = total.reshape(count, shard, feed)

            reduce.start()

        outer = h2_gather.outer
        cot_gather.finish()
        load(3).start()
        for index in range(2):
            feed_gathers[index].finish()
            load(index).start()
        for index in (3, 0, 1):
            load(index).wait()
        gb[...] = (gb[...].astype(F32) * loss_scale).astype(BF16)
        h2_gather.own().wait()
        hidden_rows(h2_gather.me)
        h2_gather.arrived(0)
        hidden_rows(h2_gather.beside)
        for k in range(1, outer):
            h2_gather.forward(k)
            hidden_rows(h2_gather.source(k))
            h2_gather.arrived(k)
            hidden_rows(h2_gather.source_beside(k))
        for g in feed_gathers[2:]:
            g.finish()
        load(2).start()
        load(2).wait()
        for k in [*range(1, outer), 0]:
            result_rows(reduce_h2.given(k))
            reduce_h2.to_beside(k).start()
            reduce_y.to_beside(k).start()
            result_rows(reduce_h2.kept(k))
            if k:
                reduce_h2.join(k)
        weight_gradient(down_part, gb, z, reduce_down)
        weight_gradient(gate_part, rows_all, dg, reduce_gate)
        weight_gradient(up_part, rows_all, du, reduce_up)

    weights = pltpu.VMEM((feed, model) if flip else (dp, shard, feed), BF16)
    hidden = pltpu.VMEM((length, feed), BF16)
    pl.run_scoped(
        feed_forward,
        weights,
        weights,
        weights,
        pltpu.VMEM((mp, own, model), BF16),
        hidden,
        hidden,
        hidden,
    )
    h2_gather.sent()

    def mixer(
        h, p, inverse, w, scores, step, delta, state, o, m, ds_all, dp_low, db_low,
    ):
        do, entry, dc = o, w, p
        targets = (h, p, inverse, w, scores, step, delta, state, o, m)

        def load(index):
            return pltpu.make_async_copy(stored[index], targets[index], load_sem.at[index])

        for index in (1, 4, 3, 8, 9, 5, 2, 6, 7, 0):
            load(index).start()

        dh = reduce_h2.finish()
        y = y1[...]
        r = lax.rsqrt(jnp.mean(y * y, axis=-1, keepdims=True) + 1e-06)
        small[...] = jnp.zeros_like(small)
        small[second_row : second_row + 1] = jnp.sum(dh * y * r, axis=0, keepdims=True)
        scaled = second[...] * dh
        grad = (
            cot[...].astype(F32) * loss_scale
            + r * scaled
            - y * (r * r * r * jnp.mean(y * scaled, axis=-1, keepdims=True))
        )
        input_grad[...] = grad
        low[...] = grad.astype(BF16)
        ab_gather.start()
        reduce_h2.sent()
        reduce_down.join_all()

        for index in (1, 4, 3):
            load(index).wait()
        dc[length + 8 :] = jnp.zeros((8, dc.shape[1]), F32)

        def chains_of(i, size):
            chains = [(i * size + j, head) for j in range(size) for head in range(heads)]
            starts = [pl.multiple_of(c * BLOCK, BLOCK) for c, _ in chains]
            places = [head * blocks + c for c, head in chains]
            return chains, starts, places

        def lane(head):
            return slice(head * BLOCK, (head + 1) * BLOCK)

        @pl.loop(0, blocks // group)
        def _(i):
            chains, starts, places = chains_of(i, group)
            moved = each(lambda at: mm(scores[at], w[at]), places)
            for (c, head), start, place, t in zip(chains, starts, places, moved):
                s, _, _ = activated(p, conv, start, 0, head, width, taps)
                ds_all[place] = s * (inverse_norm(s) * scale) - t

        for index in (8, 9, 5):
            load(index).wait()
        out_weight = out_rows.reshape(width, model)

        def output_gradients(index, d_gain):
            dm = dot(ab_all[index], out_weight[...], tb=True)
            at = pl.ds(pl.multiple_of(index * own, own), own)
            for head in range(heads):
                x = o[at, lane(head)]
                g = dm[:, lane(head)]
                r = lax.rsqrt(jnp.mean(x * x, axis=-1, keepdims=True) + 1e-05)
                d_gain = d_gain + jnp.sum(g * x * r, axis=0, keepdims=True)
                scaled = g * gain[...]
                do[at, lane(head)] = r * scaled - x * (
                    r * r * r * jnp.mean(x * scaled, axis=-1, keepdims=True)
                )
            return d_gain

        ab_gather.own().wait()
        d_gain = output_gradients(ab_gather.me, jnp.zeros((1, BLOCK), F32))
        ab_gather.arrived(0)
        d_gain = output_gradients(ab_gather.beside, d_gain)
        for k in range(1, ab_gather.outer):
            ab_gather.forward(k)
            if k == 1:
                reduce_y.join_all()
            d_gain = output_gradients(ab_gather.source(k), d_gain)
            ab_gather.arrived(k)
            d_gain = output_gradients(ab_gather.source_beside(k), d_gain)
        ab_gather.sent()
        for d in range(dp):
            moved = mm(
                jnp.broadcast_to(d_gain, (8, BLOCK)), place_lanes(d, dp, lanes, gains), tb=True
            )
            small_part[d, gain_row : gain_row + 1] = moved[0:1]
        @pl.loop(0, mp)
        def _(i):
            x = ab_all[:, :, pl.ds(pl.multiple_of(i * width, BLOCK), width)].reshape(length, width)
            out_part[i] = dot(m[...], x, ta=True).astype(BF16).reshape(per, shard, width)

        def swap(k, block):
            return pltpu.make_async_remote_copy(
                src_ref=out_part.at[block],
                dst_ref=out_columns.at[pl.ds(column * per, per)],
                send_sem=swap_send.at[k],
                recv_sem=swap_recv.at[k],
                device_id={"mp": (column + k) % mp},
                device_id_type=MESH,
            )

        def swap_in(k):
            source = (column + mp - k) % mp
            return pltpu.make_async_remote_copy(
                src_ref=out_part.at[source],
                dst_ref=out_columns.at[pl.ds(source * per, per)],
                send_sem=swap_send.at[k],
                recv_sem=swap_recv.at[k],
                device_id={"mp": (column + k) % mp},
                device_id_type=MESH,
            )

        for k in range(1, mp):
            swap(k, (column + k) % mp).start()
        out_columns[pl.ds(column * per, per)] = out_part[column]

        @pl.loop(0, blocks // group)
        def _(i):
            chains, starts, places = chains_of(i, group)
            grads = [do[pl.ds(start, BLOCK), lane(head)] for (_, head), start in zip(chains, starts)]
            for place, t in zip(places, each(lambda at, g: mm(ds_all[at], g, ta=True), places, grads)):
                entry[place] = t

        def retreat(i, grads):
            places = [head * blocks + blocks - 1 - i for head in range(heads)]
            for place, g in zip(places, grads):
                ds_all[place] = g
            moved = each(lambda at, g: mm(step[at], g, ta=True), places, grads)
            return tuple(each(lambda at, g, t: g - t + entry[at], places, grads, moved))

        grads = tuple(jnp.zeros((BLOCK, BLOCK), F32) for _ in range(heads))
        for i in range(blocks):
            grads = retreat(i, grads)
        for index in (2, 6, 7, 0):
            load(index).wait()
        reduce_gate.join_all()
        d_conv = small
        conv_lanes = pl.ds(pl.multiple_of(column * width, BLOCK), width)

        def through(parts, grad, start, part, head):
            s, gate, shifted = parts
            columns = slice(part * width + head * BLOCK, part * width + (head + 1) * BLOCK)
            d_pre = grad * (gate + s * (1.0 - gate))
            dc[pl.ds(pl.multiple_of(start + 8, 8), BLOCK), columns] = d_pre
            at = pl.ds(pl.multiple_of(column * width + head * BLOCK, BLOCK), BLOCK)
            for j in range(taps):
                line = conv_row + part * taps + j
                d_conv[line : line + 1, at] += jnp.sum(d_pre * shifted[j], axis=0, keepdims=True)

        def gradients(i, only):
            chains = [((steps - 1 - i) * size + j, only) for j in range(size)]
            starts = [pl.multiple_of(c * BLOCK, BLOCK) for c, _ in chains]
            places = [head * blocks + c for c, head in chains]
            qparts, kparts, vparts = (
                [
                    activated(p, conv, start, part, head, width, taps)
                    for (_, head), start in zip(chains, starts)
                ]
                for part in range(3)
            )
            rqs = [inverse_norm(s) for s, _, _ in qparts]
            rks = [inverse_norm(s) for s, _, _ in kparts]
            qs = [part[0] * (r * scale) for part, r in zip(qparts, rqs)]
            ks = [part[0] * r for part, r in zip(kparts, rks)]
            betas = [
                sigmoid(beta_pre[pl.ds(start, BLOCK), head : head + 1])
                for (_, head), start in zip(chains, starts)
            ]
            kbs = each(lambda k, beta: k * beta, ks, betas)
            d_os = [do[pl.ds(start, BLOCK), lane(head)] for (_, head), start in zip(chains, starts)]
            deltas = [delta[at] for at in places]
            s_ins = [state[at] for at in places]
            ds_outs = [ds_all[at] for at in places]
            t1 = each(lambda at, g: one_pass(scores[at], g, ta=True), places, d_os)
            t2 = each(one_pass, ks, ds_outs)
            d_scores = each(
                lambda g, d: jnp.where(row >= col, one_pass(g, d, tb=True), 0.0), d_os, deltas
            )
            dq1 = each(lambda g, s: one_pass(g, s, tb=True), d_os, s_ins)
            es = each(lambda at, a, b: one_pass(inverse[at], a + b, ta=True), places, t1, t2)
            dq2 = each(one_pass, d_scores, ks)
            dk1 = each(lambda a, q: one_pass(a, q, ta=True), d_scores, qs)
            d_stricts = each(
                lambda e, d: jnp.where(row > col, -one_pass(e, d, tb=True), 0.0), es, deltas
            )
            dk2 = each(lambda d, s: one_pass(d, s, tb=True), deltas, ds_outs)
            f2 = each(lambda e, s: one_pass(e, s, tb=True), es, s_ins)
            f1 = each(one_pass, d_stricts, ks)
            dk3 = each(lambda a, kb: one_pass(a, kb, ta=True), d_stricts, kbs)
            fs = each(lambda a, b: a - b, f1, f2)
            dks = each(
                lambda a, b, c, beta, f: a + b + c + beta * f, dk1, dk2, dk3, betas, fs
            )
            for n, ((c, head), start) in enumerate(zip(chains, starts)):
                beta, e, f = betas[n], es[n], fs[n]
                d_beta = jnp.sum(f * ks[n] + e * vparts[n][0], axis=-1, keepdims=True)
                d_beta = jnp.where(col == head, d_beta * beta * (1.0 - beta), 0.0)
                if head:
                    d_beta = d_beta + db_low[pl.ds(start, BLOCK)].astype(F32)
                db_low[pl.ds(start, BLOCK)] = d_beta.astype(BF16)
                sq, rq, gq_in = qparts[n][0], rqs[n], (dq1[n] + dq2[n]) * scale
                through(
                    qparts[n],
                    rq * gq_in - sq * (rq * rq * rq * jnp.sum(sq * gq_in, axis=-1, keepdims=True)),
                    start, 0, head,
                )
                sk, rk, dk = kparts[n][0], rks[n], dks[n]
                through(
                    kparts[n],
                    rk * dk - sk * (rk * rk * rk * jnp.sum(sk * dk, axis=-1, keepdims=True)),
                    start, 1, head,
                )
                through(vparts[n], beta * e, start, 2, head)
        size = 4 if blocks % 4 == 0 else 1
        steps = blocks // size

        def before_convolution(head):
            @pl.loop(0, blocks)
            def _(c):
                start = pl.multiple_of(c * BLOCK, BLOCK)
                for part in range(3):
                    at = slice(part * width + head * BLOCK, part * width + (head + 1) * BLOCK)
                    window = dc[pl.ds(pl.multiple_of(start + 8, 8), BLOCK + 8), at]
                    total = conv[taps - 1 : taps, at] * window[0:BLOCK]
                    for j in range(taps - 1):
                        ahead = taps - 1 - j
                        total = total + conv[j : j + 1, at] * window[ahead : ahead + BLOCK]
                    dp_low[pl.ds(start, BLOCK), at] = total.astype(BF16)

        def projection_gradient(i, size, head):
            x = h[:, pl.ds(pl.multiple_of(i * size, size), size)]
            right = jnp.concatenate(
                [
                    dp_low[:, part * width + head * BLOCK : part * width + (head + 1) * BLOCK]
                    for part in range(3)
                ],
                axis=1,
            )
            total = dot(x, right, ta=True).astype(BF16)
            count = size // shard
            head_parts[head][pl.ds(i * count, count)] = total.reshape(count, shard, 3 * BLOCK)

        for head, reduce in enumerate(reduce_heads):
            pl.loop(0, steps)(partial(gradients, only=head))
            before_convolution(head)
            if flip:
                for k in [*range(1, reduce.outer), 0]:
                    projection_gradient(reduce.target(k), 2 * shard, head)
                    reduce.to_beside(k).start()
            else:
                pl.loop(0, model // tile)(partial(projection_gradient, size=tile, head=head))
                reduce.start()
            if head == 0:
                reduce_up.join_all()
                for k in range(1, mp):
                    swap_in(k).wait_recv()
                reduce_out.start()
            else:
                reduce_heads[head - 1].join_all()
        weight = qkv.reshape(model, 3 * width)

        def rows(index):
            at = pl.ds(pl.multiple_of(index * own, own), own)
            dh_part[index] = (
                dot(dp_low[at], weight[...], tb=True) + dot(db_low[at], beta_rows[...])
            ).astype(BF16)

        for k in [*range(1, reduce_h.outer), 0]:
            rows(reduce_h.given(k))
            reduce_h.to_beside(k).start()
            rows(reduce_h.kept(k))
            if k:
                reduce_h.join(k)
        reduce_out.join_all()
        reduce_heads[-1].join(1)
        d_beta = dot(db_low[...], h[...], ta=True)
        for g in range(heads * mp):
            line = d_beta[g % heads : g % heads + 1]
            small[g : g + 1] = jnp.where(column == g // heads, line, 0.0)
        for k in range(1, mp):
            swap(k, (column + k) % mp).wait_send()

    pl.run_scoped(
        mixer,
        *mixer_buffers,
        square,
        pltpu.VMEM((length, 3 * width), BF16),
        pltpu.VMEM((length, BLOCK), BF16),
    )
    for reduce, result in ((reduce_gate, d_gate), (reduce_up, d_up), (reduce_down, d_down)):
        result[...] = reduce.finish()
    output[...] = (y1[...] + reduce_y.finish()).astype(BF16)
    for k in range(2, reduce_heads[-1].outer):
        reduce_heads[-1].join(k)
    dh = reduce_h.finish()
    x = tokens[...].astype(F32)
    s = lax.rsqrt(jnp.mean(x * x, axis=-1, keepdims=True) + 1e-06)
    small[first_row : first_row + 1] = jnp.sum(dh * x * s, axis=0, keepdims=True)
    for d in range(dp):
        small_part[d, 0:gain_row] = small[0:gain_row, d * lanes : (d + 1) * lanes]
        small_part[d, gain_row + 1 :] = jnp.zeros((small_part.shape[1] - gain_row - 1, lanes), F32)
    reduce_small.start()
    scaled = first[...] * dh
    input_grad[...] += s * scaled - x * (
        s * s * s * jnp.mean(x * scaled, axis=-1, keepdims=True)
    )
    reduce_small.join_all()
    def share(slot, reduce):
        size = reduce.near.shape[2]
        low_at = shared.at[:, slot * 3 * BLOCK : slot * 3 * BLOCK + size]
        low_at[...] = reduce.finish().astype(BF16)
        gather = Gather(
            "mp",
            mp,
            low_at,
            lambda i: shared_all.at[i, :, slot * 3 * BLOCK : slot * 3 * BLOCK + size],
            share_sems,
            slot,
        )
        gather.start()
        return gather

    gathers = [share(heads, reduce_out)]
    for head in range(heads - 1):
        gathers.append(share(head, reduce_heads[head]))
    small_low[...] = reduce_small.finish()
    narrow = Gather("mp", mp, small_low, leading(small_sums), share_sems, heads + 1)
    narrow.start()
    gathers.append(share(heads - 1, reduce_heads[-1]))
    for g in gathers[:-1]:
        g.forward_all()
    narrow.forward_all()
    gathers[-1].forward_all()
    narrow.finish()
    small_total = small_sums[0]
    for i in range(1, mp):
        small_total = small_total + small_sums[i]
    d_small[...] = small_total
    for g in gathers:
        g.finish()
    ab_gather_done = (reduce_y, reduce_h, *over_dp)
    for reduce in ab_gather_done:
        reduce.sent()


def finish_kernel(mp, heads, *refs):
    take = Taker(refs)
    small, shared_in, *passed_in = take(7)
    passed, models, smalls = take(5), take(4), take(7)
    held = take(5)
    shared, wide, sems = take(3)
    width = heads * BLOCK
    loads = [
        pltpu.make_async_copy(src, dst, sems.at[i])
        for i, (src, dst) in enumerate(zip(passed_in, held))
    ]
    copies = [
        pltpu.make_async_copy(src, dst, sems.at[10 + i])
        for i, (src, dst) in enumerate(zip(held, passed))
    ]
    load = pltpu.make_async_copy(shared_in, shared, sems.at[5])
    load.start()
    for copy in loads:
        copy.start()
    line = 0
    for ref in smalls:
        ref[...] = small[line : line + ref.shape[0], 0 : ref.shape[1]]
        line += ref.shape[0]
    for first, second in zip(loads, copies):
        first.wait()
        second.start()
    load.wait()
    for index, result in enumerate(models):
        for i in range(mp):
            for head in range(heads):
                at = head * 3 * BLOCK + index * BLOCK if index < 3 else 3 * width + head * BLOCK
                to = i * width + head * BLOCK
                wide[index, :, to : to + BLOCK] = shared[i, :, at : at + BLOCK].astype(F32)
        copies.append(pltpu.make_async_copy(wide.at[index], result, sems.at[6 + index]))
        copies[-1].start()
    for copy in copies:
        copy.wait()


def call(kernel, ins, outs, scratch, collective, name, limit):
    return pl.pallas_call(
        kernel,
        out_shape=[jax.ShapeDtypeStruct(shape, kind) for _, shape, kind in outs],
        in_specs=[spec for spec, _ in ins],
        out_specs=[spec for spec, _, _ in outs],
        scratch_shapes=list(scratch),
        compiler_params=pltpu.CompilerParams(
            collective_id=collective,
            has_side_effects=collective is not None,
            vmem_limit_bytes=limit * MIB,
        ),
        name=name,
    )(*[array for _, array in ins])


def shards(
    dp,
    mp,
    tokens,
    cotangent,
    domain,
    domain_weight,
    query_weight,
    key_weight,
    value_weight,
    beta_weight,
    conv_query,
    conv_key,
    conv_value,
    out_gain,
    out_weight,
    norm_first,
    norm_second,
    gate_weight,
    up_weight,
    down_weight,
):
    own, model = tokens.shape
    length = own * mp
    shard = query_weight.shape[0]
    taps = conv_query.shape[0]
    all_heads = beta_weight.shape[1]
    heads = all_heads // mp
    width = model // mp
    feed = gate_weight.shape[1]
    lanes = norm_first.shape[0]
    gains = out_gain.shape[0]
    conv_row, gain_row = all_heads, all_heads + 3 * taps + 2
    first_row, second_row = gain_row - 2, gain_row - 1
    small_rows = -(-(gain_row + 1) // 8) * 8
    rows_of = (conv_row, first_row, second_row, gain_row)
    flip = lanes % 128 == 0

    square = ((heads * (length // BLOCK), BLOCK, BLOCK), F32)
    stored = [
        ((length, model), BF16),
        ((length + 16, 3 * width), F32),
        *[square] * 6,
        ((length, width), F32),
        ((length, width), BF16),
    ]
    feed_shape = (feed, model) if flip else (dp, shard, feed)
    feed_block = (feed, shard) if flip else (shard, feed)
    feed_grad = (VM, feed_block, F32)
    feed_own = (
        (gate_weight.T, up_weight.T, down_weight) if flip else (gate_weight, up_weight, down_weight.T)
    )
    token_rows = ((mp, own, model), BF16)
    sizes = (feed_block,) * 3 + ((shard, width),) + ((shard, 3 * BLOCK),) * heads
    results = call(
        partial(block_kernel, dp, mp, taps, heads, gains, flip, rows_of),
        [
            (SM, domain), (SM, domain_weight),
            (VM, tokens), (VM, cotangent), (ANY, query_weight), (ANY, key_weight), (ANY, value_weight),
            (ANY, out_weight),
            (VM, beta_weight.T), (VM, conv_query), (VM, conv_key), (VM, conv_value),
            (VM, norm_first[None]), (VM, norm_second[None]), (VM, out_gain[None]),
            *[(ANY, a) for a in feed_own],
        ],
        [
            (VM, (own, model), BF16),
            (VM, (own, model), F32),
            (VM, (mp, shard, 4 * width), BF16),
            (VM, (small_rows, lanes), F32),
            *[feed_grad] * 3,
            (ANY, *token_rows), *[(ANY, feed_shape, BF16)] * 3,
            *[(ANY, *kind) for kind in stored],
        ],
        [pltpu.VMEM(*token_rows)] * 4
        + [
            pltpu.VMEM((own, model), BF16),
            pltpu.VMEM((dp, shard, 3 * width), BF16),
            pltpu.VMEM((dp // mp, shard, model), BF16),
            pltpu.VMEM((dp, shard, width), BF16),
            pltpu.VMEM((own, model), F32),
            pltpu.VMEM((BLOCK, model), BF16),
            pltpu.VMEM((taps, 3 * width), F32),
            pltpu.VMEM((1, model), F32),
            pltpu.VMEM((1, model), F32),
            pltpu.VMEM((1, BLOCK), F32),
            pltpu.VMEM((length, BLOCK), F32),
        ]
        + [pltpu.VMEM(feed_shape, BF16)] * 3
        + [
            pltpu.VMEM((mp, dp // mp, shard, width), BF16),
            *[pltpu.VMEM((dp, shard, 3 * BLOCK), BF16)] * heads,
        ]
        + ReduceScatter.buffers(mp, own, model) * 2
        + [b for size in sizes for b in ReduceScatter.buffers(dp, *size)]
        + ReduceScatter.buffers(dp, small_rows, lanes, F32)
        + [
            pltpu.VMEM((small_rows, lanes), F32),
            pltpu.VMEM((dp, small_rows, lanes), F32),
            pltpu.VMEM((small_rows, model), F32),
            pltpu.VMEM((dp, small_rows, lanes), F32),
            pltpu.VMEM((small_rows, lanes), F32),
            pltpu.VMEM((mp, small_rows, lanes), F32),
            pltpu.VMEM((shard, 4 * width), BF16),
        ]
        + Gather.scratch(mp, 4)
        + Gather.scratch(dp, 9)
        + ReduceScatter.scratch(mp, 4)
        + ReduceScatter.scratch(dp, 5 + heads)
        + Gather.scratch(mp, 2 + heads)
        + [pltpu.SemaphoreType.DMA((mp,))] * 4
        + [
            pltpu.SemaphoreType.DMA((10,)),
            pltpu.SemaphoreType.DMA((10,)),
            pltpu.SemaphoreType.DMA((4,)),
        ],
        0,
        "block",
        63,
    )
    output, input_grad, shared, small, d_gate, d_up, d_down = results[:7]
    small_shapes = [(all_heads, lanes)] + [(taps, lanes)] * 3 + [(1, lanes)] * 2 + [(1, gains)]
    results = call(
        partial(finish_kernel, mp, heads),
        [(VM, small)] + [(ANY, a) for a in (shared, output, input_grad, d_gate, d_up, d_down)],
        [
            (ANY, (own, model), BF16),
            (ANY, (own, model), F32),
            *[(ANY, feed_block, F32)] * 3,
            *[(ANY, (shard, model), F32)] * 4,
            *[(VM, shape, F32) for shape in small_shapes],
        ],
        [
            pltpu.VMEM((own, model), BF16),
            pltpu.VMEM((own, model), F32),
            *[pltpu.VMEM(feed_block, F32)] * 3,
            pltpu.VMEM((mp, shard, 4 * width), BF16),
            pltpu.VMEM((4, shard, model), F32),
            pltpu.SemaphoreType.DMA((15,)),
        ],
        None,
        "finish",
        60,
    )
    output, input_grad, d_gate, d_up, d_down = results[:5]
    d_query, d_key, d_value, d_outw = results[5:9]
    d_beta, d_conv_q, d_conv_k, d_conv_v, d_first, d_second, d_gain = results[9:]
    if flip:
        d_gate, d_up = d_gate.T, d_up.T
    else:
        d_down = d_down.T
    return (
        output,
        input_grad,
        d_query,
        d_key,
        d_value,
        d_beta.T,
        d_conv_q,
        d_conv_k,
        d_conv_v,
        d_gain[0],
        d_outw,
        d_first[0],
        d_second[0],
        d_gate,
        d_up,
        d_down,
    )


def solution(mesh):
    dp, mp = mesh.shape["dp"], mesh.shape["mp"]
    weight = P("dp", None)
    split = P(None, "dp")
    rows = P(("dp", "mp"), None)
    return jax.shard_map(
        partial(shards, dp, mp),
        mesh=mesh,
        in_specs=(
            rows, rows, P("dp"), P(), weight, weight, weight, weight, split, split, split,
            P("dp"), weight, P("dp"), P("dp"), P("dp", "mp"), P("dp", "mp"), P("mp", "dp"),
        ),
        out_specs=(
            rows, rows, weight, weight, weight, weight, split, split, split,
            P("dp"), weight, P("dp"), P("dp"), P("dp", "mp"), P("dp", "mp"), P("mp", "dp"),
        ),
        check_vma=False,
    )
```
